32 devices in a mesh: grp: 4 (over z), mod: 8 (over y, x, core).
Axes of the slice: x: 2, y: 2, z: 4, core: 2. Of those that a mesh axis runs over, the one named last changes fastest.
Arguments:
- tokens: bfloat16 [64, 64, 8, 128], P(('grp', 'mod')), may hold values from -3 to 3
- lengths: int32 [64], P(('grp', 'mod')), may hold values from 1 to 64, 2048 in all
- module_order: int32 [8], replicated, may hold values from 0 to 7, each once
Outputs:
- preconditioned: float32 [8, 64, 4096], P('mod', 'grp')
The draws below stay inside these ranges and needn't reach their ends.
Inputs may be any that keep to these rules, and one draw needn't show every extreme that they name: `lengths`: each example's live tokens are its first slots; some example has exactly 64. `module_order`: each module appears exactly once.
All inputs are finite; a program needn't handle non-finite values. No bound on the sum of `lengths` on one device may be relied on, other than what follows from the above.
Results may differ from the reference program's by a relative error of at most 0.0068.
Values may be sent and summed in bfloat16 or wider, within the bound.
No kernel may reach another device: no remote copies, remote signals or barrier semaphores. Data moves between devices by JAX's collectives and lax.ppermute only.
A program may use at most 64 MiB of HBM per device.

```python
import math
import jax
import jax.numpy as jnp
import numpy as np
from jax import lax

PROJ = 64
LEN = 64
ITERS = 3
MODULES = 8
EX_GRP = 16
EXAMPLES = 64
N_GRP = 4


def steps_of(key, shape, cuts, low, largest):
    gain = 1.0
    for position, shards_of in cuts:
        steps = jax.random.uniform(jax.random.fold_in(jax.random.fold_in(key, 6), position), (shards_of,), jnp.float32, low / len(cuts), largest / len(cuts))
        gain = gain * jnp.repeat(jnp.exp(steps), shape[position] // shards_of).reshape((-1,) + (1,) * (len(shape) - 1 - position))
    return gain


def profile(amount, total, limit, skew):
    portions = [(1 << 20) // math.isqrt(grade ** skew) + 1 for grade in range(2, amount + 1)]
    surplus, counts = total - limit - (amount - 1), [1] * (amount - 1)
    while surplus > 0:
        movable = [i for i in range(amount - 1) if counts[i] < limit]
        whole, budget = sum([portions[i] for i in movable]), surplus
        for i in movable:
            addition = min(limit - counts[i], max(1, budget * portions[i] // whole), surplus)
            counts[i] = counts[i] + addition
            surplus = surplus - addition
    return np.array([limit] + counts)


def uneven_parts(stream_key, count, total, most, slope):
    if count == 2:
        one = jax.random.randint(stream_key, (), max(1, total - most), min(most, total - 1) + 1)
        return jnp.stack([one, total - one])
    tallies = jnp.asarray(profile(count, total, most, slope), jnp.int32)
    twos = (count - 1) // 2
    donor, sink = tallies[1:1 + 2 * twos:2], tallies[2:2 + 2 * twos:2]
    room = jnp.minimum(donor - 1, most - sink)
    shifted = jax.random.randint(jax.random.fold_in(stream_key, 1), (twos,), 0, 1 << 20) % (room + 1)
    tallies = tallies.at[1:1 + 2 * twos:2].set(donor - shifted).at[2:2 + 2 * twos:2].set(sink + shifted)
    return tallies[jax.random.permutation(jax.random.fold_in(stream_key, 2), count)]


def centred(rng, shape, spread, bound, cuts=(), held_as=jnp.bfloat16):
    result = jax.random.normal(rng, shape, jnp.float32) * spread
    if len(cuts) > 0:
        result = steps_of(rng, shape, cuts, -0.22, 0.18) * result
    return jnp.clip(result, min=-bound, max=bound).astype(held_as)


def setup_inputs(seed: int = 0) -> dict:
    streams_of = jax.random.split(jax.random.key(seed), 4)
    return {
        "tokens": centred(streams_of[0], (EXAMPLES, LEN, MODULES, 2 * PROJ), 0.5, 3.0, ((0, 32),)),
        "lengths": uneven_parts(streams_of[1], EXAMPLES, EXAMPLES * LEN // 2, LEN, 1).astype(jnp.int32),
        "module_order": jax.random.permutation(streams_of[2], MODULES).astype(jnp.int32),
    }


def start_basis(row_count, col_count):
    row_index = jnp.arange(row_count, dtype=jnp.float32)[:, None] + 0.5
    col_index = jnp.arange(col_count, dtype=jnp.float32)[None, :] + 0.5
    return jnp.cos(jnp.pi * row_index * col_index / row_count)

def orthonormal(matrix):
    for repeat in range(2):
        cross_gram = jnp.dot(matrix.T, matrix, precision=lax.Precision.HIGHEST)
        factor = jnp.linalg.cholesky(cross_gram)
        matrix = jax.scipy.linalg.solve_triangular(factor, matrix.T, lower=True).T
    return matrix

def merge_pair(lower_sketch, upper_sketch):
    stacked = jnp.concatenate([lower_sketch, upper_sketch], axis=0)
    kernel = jnp.dot(stacked, stacked.T, precision=lax.Precision.HIGHEST)
    current = start_basis(stacked.shape[0], lower_sketch.shape[0])
    for repeat in range(ITERS):
        current = orthonormal(jnp.dot(kernel, current, precision=lax.Precision.HIGHEST))
    return jnp.dot(current.T, stacked, precision=lax.Precision.HIGHEST)

def precondition(group_rows, sketch):
    sketch_rows = sketch.shape[0]
    damping = 0.1 * jnp.sum(sketch * sketch) / sketch_rows + 1e-06
    capacitance = jnp.dot(sketch, sketch.T, precision=lax.Precision.HIGHEST) + damping * jnp.eye(sketch_rows, dtype=jnp.float32)
    projected = jnp.dot(group_rows, sketch.T, precision=lax.Precision.HIGHEST)
    factor = jnp.linalg.cholesky(capacitance)
    middle = jax.scipy.linalg.solve_triangular(factor, projected.T, lower=True)
    weights = jax.scipy.linalg.solve_triangular(factor, middle, lower=True, trans=1).T
    return group_rows - jnp.dot(weights, sketch, precision=lax.Precision.HIGHEST)

def module_features(picked, lengths):
    half_width = picked.shape[-1] // 2
    live_mask = jnp.arange(picked.shape[1], dtype=jnp.int32)[None, :] < lengths[:, None]
    grad_side = jnp.where(live_mask[:, :, None], picked[:, :, half_width:], jnp.zeros((), picked.dtype))
    input_side = picked[:, :, :half_width]
    outer = jnp.einsum('eto,eti->eoi', grad_side.astype(jnp.float32), input_side.astype(jnp.float32))
    return outer.reshape(picked.shape[0], half_width * half_width).astype(jnp.bfloat16)

def reference(tokens, lengths, module_order):
    levels = N_GRP.bit_length() - 1

    def one_module(slot):
        picked = lax.dynamic_index_in_dim(tokens, module_order[slot], axis=2, keepdims=False)
        leaves = module_features(picked, lengths).astype(jnp.float32)
        sketches = leaves.reshape(N_GRP, EX_GRP, leaves.shape[-1])
        for height in range(levels):
            sketches = jax.vmap(merge_pair)(sketches[0::2], sketches[1::2])
        return precondition(leaves, sketches[0])
    return lax.map(one_module, jnp.arange(MODULES, dtype=jnp.int32))
```

```python
import functools

import jax
import jax.numpy as jnp
import numpy as np
from jax import lax
from jax.experimental import pallas as pl
from jax.experimental.pallas import tpu as pltpu
from jax.sharding import PartitionSpec as P

ITERS = 3
HI = lax.Precision.HIGHEST


def partner(value, axis, bit):
    mask = 2**bit
    return xor_send(value, axis, mask)


def xor_send(value, axis, mask):
    pairs = [(source, source ^ mask) for source in range(lax.axis_size(axis))]
    return lax.ppermute(value, axis, pairs)


def start_basis(row_count, col_count):
    row_index = np.arange(row_count, dtype=np.float64)[:, None] + 0.5
    col_index = np.arange(col_count, dtype=np.float64)[None, :] + 0.5
    return np.cos(np.pi * row_index * col_index / row_count).astype(np.float32)


def orthonormal(matrix):
    for repeat in range(2):
        cross_gram = jnp.dot(matrix.T, matrix, precision=HI)
        factor = jnp.linalg.cholesky(cross_gram)
        matrix = jax.scipy.linalg.solve_triangular(factor, matrix.T, lower=True).T
    return matrix


def merge_pair(lower_sketch, upper_sketch):
    stacked = jnp.concatenate([lower_sketch, upper_sketch], axis=0)
    kernel = jnp.dot(stacked, stacked.T, precision=HI)
    current = start_basis(stacked.shape[0], lower_sketch.shape[0])
    for repeat in range(ITERS):
        current = orthonormal(jnp.dot(kernel, current, precision=HI))
    return jnp.dot(current.T, stacked, precision=HI)


def precondition(group_rows, sketch):
    sketch_rows = sketch.shape[0]
    damping = 0.1 * jnp.sum(sketch * sketch) / sketch_rows + 1e-06
    capacitance = jnp.dot(sketch, sketch.T, precision=HI) + damping * jnp.eye(sketch_rows, dtype=jnp.float32)
    projected = jnp.dot(group_rows, sketch.T, precision=HI)
    factor = jnp.linalg.cholesky(capacitance)
    middle = jax.scipy.linalg.solve_triangular(factor, projected.T, lower=True)
    weights = jax.scipy.linalg.solve_triangular(factor, middle, lower=True, trans=1).T
    return group_rows - jnp.dot(weights, sketch, precision=HI)


def sketch_tree(features, module_order):
    ordered = jnp.take(features, module_order, axis=0)
    group_rows = lax.all_to_all(ordered, "mod", split_axis=0, concat_axis=1, tiled=True)
    leaves = group_rows.astype(jnp.float32)
    merge_all = jax.vmap(merge_pair)
    levels = lax.axis_size("grp").bit_length() - 1
    position = lax.axis_index("grp")
    sketch = leaves
    for height in range(levels):
        sister = partner(sketch, "grp", height)
        upper_side = position // 2**height % 2 == 1
        lower_part = jnp.where(upper_side, sister, sketch)
        upper_part = jnp.where(upper_side, sketch, sister)
        sketch = merge_all(lower_part, upper_part)
    return jax.vmap(precondition)(leaves, sketch)


def dot_nt(a, b):
    return lax.dot_general(a, b, (((1,), (1,)), ((), ())), precision=HI, preferred_element_type=jnp.float32)


def dot_nn(a, b):
    return jnp.dot(a, b, precision=HI, preferred_element_type=jnp.float32)


def spread_columns(gram, first, count, width):
    columns = []
    for j in range(count):
        column = gram[first : first + count, first + j : first + j + 1]
        blocks = {b: jnp.broadcast_to(column[8 * b : 8 * b + 8], (8, width)) for b in range(j // 8, count // 8)}
        columns.append(blocks)
    return columns


def eliminate(columns, rhs):
    count = len(columns)
    width = rhs.shape[1]
    parts = [rhs[8 * b : 8 * b + 8] for b in range(count // 8)]
    row = lax.broadcasted_iota(jnp.int32, (8, width), 0)
    diag = [jnp.ones((8, width), jnp.float32) for _ in parts]
    for p in range(count):
        home, at = divmod(p, 8)
        pivot_column = columns[p]
        pivot = pivot_column[home][at : at + 1]
        diag[home] = jnp.where(row == at, pivot, diag[home])
        if p == count - 1:
            break
        inverse = 1.0 / pivot
        factor = {}
        for b in pivot_column:
            scaled = pivot_column[b] * inverse
            factor[b] = jnp.where(row > at, scaled, 0.0) if b == home else scaled
        for j in range(p + 1, count):
            along = pivot_column[j // 8][j % 8 : j % 8 + 1]
            columns[j] = {b: block - factor[b] * along for b, block in columns[j].items()}
        pivot_row = parts[home][at : at + 1]
        for b in factor:
            parts[b] = parts[b] - factor[b] * pivot_row
    return jnp.concatenate([part * lax.rsqrt(d) for part, d in zip(parts, diag)], axis=0)


def orthogonal_iteration(start, kernel, problems):
    rows = start.shape[0] // problems
    moved = dot_nn(start, kernel)
    for step in range(ITERS + 1):
        gram = dot_nt(moved, moved)
        onward = dot_nn(moved, kernel) if step < ITERS - 1 else moved
        done = []
        for k in range(problems):
            columns = spread_columns(gram, k * rows, rows, onward.shape[1])
            done.append(eliminate(columns, onward[k * rows : (k + 1) * rows]))
        moved = jnp.concatenate(done, axis=0)
    return moved


def combine_kernel(rows, near_ref, a_ref, b_ref, c_ref, start_ref, pair_ref, leaf_ref, out_ref):
    gram = (near_ref[...] + a_ref[...]) + (b_ref[...] + c_ref[...])
    count = gram.shape[0]
    half = count // 2
    r = lax.broadcasted_iota(jnp.int32, gram.shape, 0)
    c = lax.broadcasted_iota(jnp.int32, gram.shape, 1)
    own_pair = jnp.where((r < half) == (c < half), gram, 0.0)
    first = orthogonal_iteration(pair_ref[...], own_pair, 2)
    reached = dot_nn(first, gram)
    kernel = dot_nt(reached, first)
    second = orthogonal_iteration(start_ref[...], kernel, 1)
    weights = dot_nn(second, first)
    projected = dot_nn(second, reached)
    capacitance = dot_nt(projected, weights)
    columns = spread_columns(capacitance, 0, rows, 2 * count)
    total = sum(columns[j][j // 8][j % 8 : j % 8 + 1] for j in range(rows))
    damping = 0.1 * total / rows + 1e-06
    row = lax.broadcasted_iota(jnp.int32, (8, 2 * count), 0)
    for j in range(rows):
        columns[j][j // 8] = columns[j][j // 8] + jnp.where(row == j % 8, damping, 0.0)
    solved = eliminate(columns, jnp.concatenate([projected, weights], axis=1))
    change = lax.dot_general(
        solved[:, :count], solved[:, count:], (((0,), (0,)), ((), ())), precision=HI, preferred_element_type=jnp.float32
    )
    top = change.astype(jnp.bfloat16)
    rest = (change - top.astype(jnp.float32)).astype(jnp.bfloat16)
    leaf = leaf_ref[...]
    moved = jnp.dot(top, leaf, preferred_element_type=jnp.float32) + jnp.dot(rest, leaf, preferred_element_type=jnp.float32)
    out_ref[...] = (leaf.astype(jnp.float32) - moved).astype(out_ref.dtype)


def gram_route(features, module_order):
    groups, owners = lax.axis_size("grp"), lax.axis_size("mod")
    modules, own, width = features.shape
    rows = owners * own
    count = groups * rows
    ordered = jnp.take(features, module_order, axis=0)
    pieces = ordered.reshape(modules, own, groups, width // groups).transpose(2, 0, 1, 3)
    pieces = pieces.reshape(groups * modules, own, width // groups)
    leaf = lax.all_to_all(pieces, ("grp", "mod"), split_axis=0, concat_axis=0, tiled=True)
    leaf = leaf.reshape(count, width // groups)
    gram = lax.dot_general(leaf, leaf, (((1,), (1,)), ((), ())), preferred_element_type=jnp.float32)
    others = [xor_send(gram, "grp", mask) for mask in range(1, groups)]
    start = start_basis(2 * rows, rows).T
    pair = np.zeros((2 * rows, 4 * rows), np.float32)
    pair[:rows, : 2 * rows] = start
    pair[rows:, 2 * rows :] = start
    out = pl.pallas_call(
        functools.partial(combine_kernel, rows),
        out_shape=jax.ShapeDtypeStruct(leaf.shape, jnp.bfloat16),
        compiler_params=pltpu.CompilerParams(vmem_limit_bytes=32 * 1024 * 1024),
    )(gram, *others, jnp.asarray(start), jnp.asarray(pair), leaf)
    blocks = out.reshape(groups, rows, width // groups)
    me = lax.axis_index("grp")
    received = [lax.dynamic_index_in_dim(blocks, me, 0, keepdims=False)]
    for mask in range(1, groups):
        mine = lax.dynamic_index_in_dim(blocks, me ^ mask, 0, keepdims=False)
        received.append(xor_send(mine, "grp", mask))
    received = jnp.stack(received)
    chunks = [lax.dynamic_index_in_dim(received, me ^ g, 0, keepdims=False) for g in range(groups)]
    return jnp.concatenate(chunks, axis=1).astype(jnp.float32)[None]


def local_features(token_block, live_counts):
    example_count, token_slots, module_count, full_width = token_block.shape
    half_width = full_width // 2
    live_mask = jnp.arange(token_slots, dtype=jnp.int32)[None, :] < live_counts[:, None]
    grad_side = jnp.where(
        live_mask[:, :, None, None],
        token_block[:, :, :, half_width:],
        jnp.zeros((), token_block.dtype),
    )
    input_side = token_block[:, :, :, :half_width]
    outer = jnp.einsum("etmo,etmi->meoi", grad_side, input_side, preferred_element_type=jnp.float32)
    return outer.reshape(module_count, example_count, half_width * half_width).astype(jnp.bfloat16)


def per_device(tokens, lengths, module_order):
    features = local_features(tokens, lengths)
    groups, owners = lax.axis_size("grp"), lax.axis_size("mod")
    rows = owners * features.shape[1]
    if groups == 4 and rows == 16 and owners == features.shape[0]:
        return gram_route(features, module_order)
    return sketch_tree(features, module_order)


def solution(mesh):
    return jax.shard_map(
        per_device,
        mesh=mesh,
        in_specs=(P(("grp", "mod"), None, None, None), P(("grp", "mod")), P()),
        out_specs=P("mod", "grp", None),
        check_vma=False,
    )
```

```python
import functools

import jax
import jax.numpy as jnp
import numpy as np
from jax import lax
from jax.experimental import pallas as pl
from jax.experimental.pallas import tpu as pltpu
from jax.sharding import PartitionSpec as P

ITERS = 3
HI = lax.Precision.HIGHEST


def partner(value, axis, bit):
    mask = 2**bit
    return xor_send(value, axis, mask)


def xor_send(value, axis, mask):
    pairs = [(source, source ^ mask) for source in range(lax.axis_size(axis))]
    return lax.ppermute(value, axis, pairs)


def start_basis(row_count, col_count):
    row_index = np.arange(row_count, dtype=np.float64)[:, None] + 0.5
    col_index = np.arange(col_count, dtype=np.float64)[None, :] + 0.5
    return np.cos(np.pi * row_index * col_index / row_count).astype(np.float32)


def orthonormal(matrix):
    for repeat in range(2):
        cross_gram = jnp.dot(matrix.T, matrix, precision=HI)
        factor = jnp.linalg.cholesky(cross_gram)
        matrix = jax.scipy.linalg.solve_triangular(factor, matrix.T, lower=True).T
    return matrix


def merge_pair(lower_sketch, upper_sketch):
    stacked = jnp.concatenate([lower_sketch, upper_sketch], axis=0)
    kernel = jnp.dot(stacked, stacked.T, precision=HI)
    current = start_basis(stacked.shape[0], lower_sketch.shape[0])
    for repeat in range(ITERS):
        current = orthonormal(jnp.dot(kernel, current, precision=HI))
    return jnp.dot(current.T, stacked, precision=HI)


def precondition(group_rows, sketch):
    sketch_rows = sketch.shape[0]
    damping = 0.1 * jnp.sum(sketch * sketch) / sketch_rows + 1e-06
    capacitance = jnp.dot(sketch, sketch.T, precision=HI) + damping * jnp.eye(sketch_rows, dtype=jnp.float32)
    projected = jnp.dot(group_rows, sketch.T, precision=HI)
    factor = jnp.linalg.cholesky(capacitance)
    middle = jax.scipy.linalg.solve_triangular(factor, projected.T, lower=True)
    weights = jax.scipy.linalg.solve_triangular(factor, middle, lower=True, trans=1).T
    return group_rows - jnp.dot(weights, sketch, precision=HI)


def sketch_tree(features, module_order):
    ordered = jnp.take(features, module_order, axis=0)
    group_rows = lax.all_to_all(ordered, "mod", split_axis=0, concat_axis=1, tiled=True)
    leaves = group_rows.astype(jnp.float32)
    merge_all = jax.vmap(merge_pair)
    levels = lax.axis_size("grp").bit_length() - 1
    position = lax.axis_index("grp")
    sketch = leaves
    for height in range(levels):
        sister = partner(sketch, "grp", height)
        upper_side = position // 2**height % 2 == 1
        lower_part = jnp.where(upper_side, sister, sketch)
        upper_part = jnp.where(upper_side, sketch, sister)
        sketch = merge_all(lower_part, upper_part)
    return jax.vmap(precondition)(leaves, sketch)


def dot_nt(a, b):
    return lax.dot_general(a, b, (((1,), (1,)), ((), ())), precision=HI, preferred_element_type=jnp.float32)


def dot_nn(a, b):
    return jnp.dot(a, b, precision=HI, preferred_element_type=jnp.float32)


def spread_columns(gram, first, count, width):
    columns = []
    for j in range(count):
        column = gram[first : first + count, first + j : first + j + 1]
        blocks = {b: jnp.broadcast_to(column[8 * b : 8 * b + 8], (8, width)) for b in range(j // 8, count // 8)}
        columns.append(blocks)
    return columns


def eliminate(columns, rhs):
    count = len(columns)
    width = rhs.shape[1]
    parts = [rhs[8 * b : 8 * b + 8] for b in range(count // 8)]
    row = lax.broadcasted_iota(jnp.int32, (8, width), 0)
    diag = [jnp.ones((8, width), jnp.float32) for _ in parts]
    for p in range(count):
        home, at = divmod(p, 8)
        pivot_column = columns[p]
        pivot = pivot_column[home][at : at + 1]
        diag[home] = jnp.where(row == at, pivot, diag[home])
        if p == count - 1:
            break
        inverse = 1.0 / pivot
        factor = {}
        for b in pivot_column:
            scaled = pivot_column[b] * inverse
            factor[b] = jnp.where(row > at, scaled, 0.0) if b == home else scaled
        for j in range(p + 1, count):
            along = pivot_column[j // 8][j % 8 : j % 8 + 1]
            columns[j] = {b: block - factor[b] * along for b, block in columns[j].items()}
        pivot_row = parts[home][at : at + 1]
        for b in factor:
            parts[b] = parts[b] - factor[b] * pivot_row
    return jnp.concatenate([part * lax.rsqrt(d) for part, d in zip(parts, diag)], axis=0)


def orthogonal_iteration(start, kernel, problems):
    rows = start.shape[0] // problems
    moved = dot_nn(start, kernel)
    for step in range(ITERS + 1):
        gram = dot_nt(moved, moved)
        onward = dot_nn(moved, kernel) if step < ITERS - 1 else moved
        done = []
        for k in range(problems):
            columns = spread_columns(gram, k * rows, rows, onward.shape[1])
            done.append(eliminate(columns, onward[k * rows : (k + 1) * rows]))
        moved = jnp.concatenate(done, axis=0)
    return moved


def combine_kernel(rows, gram_ref, start_ref, pair_ref, leaf_ref, out_ref):
    gram = gram_ref[...]
    count = gram.shape[0]
    half = count // 2
    r = lax.broadcasted_iota(jnp.int32, gram.shape, 0)
    c = lax.broadcasted_iota(jnp.int32, gram.shape, 1)
    own_pair = jnp.where((r < half) == (c < half), gram, 0.0)
    first = orthogonal_iteration(pair_ref[...], own_pair, 2)
    reached = dot_nn(first, gram)
    kernel = dot_nt(reached, first)
    second = orthogonal_iteration(start_ref[...], kernel, 1)
    weights = dot_nn(second, first)
    projected = dot_nn(second, reached)
    capacitance = dot_nt(projected, weights)
    columns = spread_columns(capacitance, 0, rows, 2 * count)
    total = sum(columns[j][j // 8][j % 8 : j % 8 + 1] for j in range(rows))
    damping = 0.1 * total / rows + 1e-06
    row = lax.broadcasted_iota(jnp.int32, (8, 2 * count), 0)
    for j in range(rows):
        columns[j][j // 8] = columns[j][j // 8] + jnp.where(row == j % 8, damping, 0.0)
    solved = eliminate(columns, jnp.concatenate([projected, weights], axis=1))
    change = lax.dot_general(
        solved[:, :count], solved[:, count:], (((0,), (0,)), ((), ())), precision=HI, preferred_element_type=jnp.float32
    )
    top = change.astype(jnp.bfloat16)
    rest = (change - top.astype(jnp.float32)).astype(jnp.bfloat16)
    leaf = leaf_ref[...]
    moved = jnp.dot(top, leaf, preferred_element_type=jnp.float32) + jnp.dot(rest, leaf, preferred_element_type=jnp.float32)
    out_ref[...] = (leaf.astype(jnp.float32) - moved).astype(out_ref.dtype)


def gram_route(features, module_order):
    groups, owners = lax.axis_size("grp"), lax.axis_size("mod")
    modules, own, width = features.shape
    rows = owners * own
    count = groups * rows
    ordered = jnp.take(features, module_order, axis=0)
    pieces = ordered.reshape(modules, own, groups, width // groups).transpose(2, 0, 1, 3)
    pieces = pieces.reshape(groups * modules, own, width // groups)
    leaf = lax.all_to_all(pieces, ("grp", "mod"), split_axis=0, concat_axis=0, tiled=True)
    leaf = leaf.reshape(count, width // groups)
    gram = lax.dot_general(leaf, leaf, (((1,), (1,)), ((), ())), preferred_element_type=jnp.float32)
    gram = lax.psum(gram, "grp")
    start = start_basis(2 * rows, rows).T
    pair = np.zeros((2 * rows, 4 * rows), np.float32)
    pair[:rows, : 2 * rows] = start
    pair[rows:, 2 * rows :] = start
    out = pl.pallas_call(
        functools.partial(combine_kernel, rows),
        out_shape=jax.ShapeDtypeStruct(leaf.shape, jnp.bfloat16),
        compiler_params=pltpu.CompilerParams(vmem_limit_bytes=32 * 1024 * 1024),
    )(gram, jnp.asarray(start), jnp.asarray(pair), leaf)
    blocks = out.reshape(groups, rows, width // groups)
    received = lax.all_to_all(blocks, "grp", split_axis=0, concat_axis=0, tiled=True)
    return received.transpose(1, 0, 2).reshape(1, rows, width).astype(jnp.float32)


def local_features(token_block, live_counts):
    example_count, token_slots, module_count, full_width = token_block.shape
    half_width = full_width // 2
    live_mask = jnp.arange(token_slots, dtype=jnp.int32)[None, :] < live_counts[:, None]
    grad_side = jnp.where(
        live_mask[:, :, None, None],
        token_block[:, :, :, half_width:],
        jnp.zeros((), token_block.dtype),
    )
    input_side = token_block[:, :, :, :half_width]
    outer = jnp.einsum("etmo,etmi->meoi", grad_side, input_side, preferred_element_type=jnp.float32)
    return outer.reshape(module_count, example_count, half_width * half_width).astype(jnp.bfloat16)


def per_device(tokens, lengths, module_order):
    features = local_features(tokens, lengths)
    groups, owners = lax.axis_size("grp"), lax.axis_size("mod")
    rows = owners * features.shape[1]
    if groups == 4 and rows == 16 and owners == features.shape[0]:
        return gram_route(features, module_order)
    return sketch_tree(features, module_order)


def solution(mesh):
    return jax.shard_map(
        per_device,
        mesh=mesh,
        in_specs=(P(("grp", "mod"), None, None, None), P(("grp", "mod")), P()),
        out_specs=P("mod", "grp", None),
        check_vma=False,
    )
```

```python
import functools

import jax
import jax.numpy as jnp
import numpy as np
from jax import lax
from jax.experimental import pallas as pl
from jax.experimental.pallas import tpu as pltpu
from jax.sharding import PartitionSpec as P

ITERS = 3
HI = lax.Precision.HIGHEST


def partner(value, axis, bit):
    mask = 2**bit
    return xor_send(value, axis, mask)


def xor_send(value, axis, mask):
    pairs = [(source, source ^ mask) for source in range(lax.axis_size(axis))]
    return lax.ppermute(value, axis, pairs)


def start_basis(row_count, col_count):
    row_index = np.arange(row_count, dtype=np.float64)[:, None] + 0.5
    col_index = np.arange(col_count, dtype=np.float64)[None, :] + 0.5
    return np.cos(np.pi * row_index * col_index / row_count).astype(np.float32)


def orthonormal(matrix):
    for repeat in range(2):
        cross_gram = jnp.dot(matrix.T, matrix, precision=HI)
        factor = jnp.linalg.cholesky(cross_gram)
        matrix = jax.scipy.linalg.solve_triangular(factor, matrix.T, lower=True).T
    return matrix


def merge_pair(lower_sketch, upper_sketch):
    stacked = jnp.concatenate([lower_sketch, upper_sketch], axis=0)
    kernel = jnp.dot(stacked, stacked.T, precision=HI)
    current = start_basis(stacked.shape[0], lower_sketch.shape[0])
    for repeat in range(ITERS):
        current = orthonormal(jnp.dot(kernel, current, precision=HI))
    return jnp.dot(current.T, stacked, precision=HI)


def precondition(group_rows, sketch):
    sketch_rows = sketch.shape[0]
    damping = 0.1 * jnp.sum(sketch * sketch) / sketch_rows + 1e-06
    capacitance = jnp.dot(sketch, sketch.T, precision=HI) + damping * jnp.eye(sketch_rows, dtype=jnp.float32)
    projected = jnp.dot(group_rows, sketch.T, precision=HI)
    factor = jnp.linalg.cholesky(capacitance)
    middle = jax.scipy.linalg.solve_triangular(factor, projected.T, lower=True)
    weights = jax.scipy.linalg.solve_triangular(factor, middle, lower=True, trans=1).T
    return group_rows - jnp.dot(weights, sketch, precision=HI)


def sketch_tree(features, module_order):
    ordered = jnp.take(features, module_order, axis=0)
    group_rows = lax.all_to_all(ordered, "mod", split_axis=0, concat_axis=1, tiled=True)
    leaves = group_rows.astype(jnp.float32)
    merge_all = jax.vmap(merge_pair)
    levels = lax.axis_size("grp").bit_length() - 1
    position = lax.axis_index("grp")
    sketch = leaves
    for height in range(levels):
        sister = partner(sketch, "grp", height)
        upper_side = position // 2**height % 2 == 1
        lower_part = jnp.where(upper_side, sister, sketch)
        upper_part = jnp.where(upper_side, sketch, sister)
        sketch = merge_all(lower_part, upper_part)
    return jax.vmap(precondition)(leaves, sketch)


def dot_nt(a, b):
    return lax.dot_general(a, b, (((1,), (1,)), ((), ())), precision=HI, preferred_element_type=jnp.float32)


def dot_nn(a, b):
    return jnp.dot(a, b, precision=HI, preferred_element_type=jnp.float32)


def spread_columns(gram, first, count, width):
    columns = []
    for j in range(count):
        column = gram[first : first + count, first + j : first + j + 1]
        blocks = {b: jnp.broadcast_to(column[8 * b : 8 * b + 8], (8, width)) for b in range(j // 8, count // 8)}
        columns.append(blocks)
    return columns


def eliminate(columns, rhs):
    count = len(columns)
    width = rhs.shape[1]
    parts = [rhs[8 * b : 8 * b + 8] for b in range(count // 8)]
    row = lax.broadcasted_iota(jnp.int32, (8, width), 0)
    diag = [jnp.ones((8, width), jnp.float32) for _ in parts]
    for p in range(count):
        home, at = divmod(p, 8)
        pivot_column = columns[p]
        pivot = pivot_column[home][at : at + 1]
        diag[home] = jnp.where(row == at, pivot, diag[home])
        if p == count - 1:
            break
        inverse = 1.0 / pivot
        factor = {}
        for b in pivot_column:
            scaled = pivot_column[b] * inverse
            factor[b] = jnp.where(row > at, scaled, 0.0) if b == home else scaled
        for j in range(p + 1, count):
            along = pivot_column[j // 8][j % 8 : j % 8 + 1]
            columns[j] = {b: block - factor[b] * along for b, block in columns[j].items()}
        pivot_row = parts[home][at : at + 1]
        for b in factor:
            parts[b] = parts[b] - factor[b] * pivot_row
    return jnp.concatenate([part * lax.rsqrt(d) for part, d in zip(parts, diag)], axis=0)


def orthogonal_iteration(start, kernel, problems):
    rows = start.shape[0] // problems
    moved = dot_nn(start, kernel)
    for step in range(ITERS + 1):
        gram = dot_nt(moved, moved)
        onward = dot_nn(moved, kernel) if step < ITERS - 1 else moved
        done = []
        for k in range(problems):
            columns = spread_columns(gram, k * rows, rows, onward.shape[1])
            done.append(eliminate(columns, onward[k * rows : (k + 1) * rows]))
        moved = jnp.concatenate(done, axis=0)
    return moved


def combine_kernel(rows, start_ref, pair_ref, leaf_ref, out_ref, change_ref):
    count, width = leaf_ref.shape
    leaf = leaf_ref[...]
    gram = lax.dot_general(leaf, leaf, (((1,), (1,)), ((), ())), preferred_element_type=jnp.float32)
    half = count // 2
    r = lax.broadcasted_iota(jnp.int32, gram.shape, 0)
    c = lax.broadcasted_iota(jnp.int32, gram.shape, 1)
    own_pair = jnp.where((r < half) == (c < half), gram, 0.0)
    first = orthogonal_iteration(pair_ref[...], own_pair, 2)
    reached = dot_nn(first, gram)
    kernel = dot_nt(reached, first)
    second = orthogonal_iteration(start_ref[...], kernel, 1)
    weights = dot_nn(second, first)
    projected = dot_nn(second, reached)
    capacitance = dot_nt(projected, weights)
    columns = spread_columns(capacitance, 0, rows, 2 * count)
    total = sum(columns[j][j // 8][j % 8 : j % 8 + 1] for j in range(rows))
    damping = 0.1 * total / rows + 1e-06
    row = lax.broadcasted_iota(jnp.int32, (8, 2 * count), 0)
    for j in range(rows):
        columns[j][j // 8] = columns[j][j // 8] + jnp.where(row == j % 8, damping, 0.0)
    solved = eliminate(columns, jnp.concatenate([projected, weights], axis=1))
    change_ref[...] = lax.dot_general(
        solved[:, :count], solved[:, count:], (((0,), (0,)), ((), ())), precision=HI, preferred_element_type=jnp.float32
    )
    own = pl.ds(pl.multiple_of(lax.axis_index("grp") * rows, rows), rows)
    change = change_ref[own, :]
    top = change.astype(jnp.bfloat16)
    rest = (change - top.astype(jnp.float32)).astype(jnp.bfloat16)
    moved = jnp.dot(top, leaf, preferred_element_type=jnp.float32) + jnp.dot(rest, leaf, preferred_element_type=jnp.float32)
    out_ref[0] = leaf_ref[own, :].astype(jnp.float32) - moved


def gram_route(features, module_order):
    groups, owners = lax.axis_size("grp"), lax.axis_size("mod")
    modules, own, width = features.shape
    rows = owners * own
    count = groups * rows
    ordered = jnp.take(features, module_order, axis=0)
    pieces = jnp.broadcast_to(ordered[None], (groups, modules, own, width)).reshape(groups * modules, own, width)
    leaf = lax.all_to_all(pieces, ("grp", "mod"), split_axis=0, concat_axis=0, tiled=True)
    leaf = leaf.reshape(count, width)
    start = start_basis(2 * rows, rows).T
    pair = np.zeros((2 * rows, 4 * rows), np.float32)
    pair[:rows, : 2 * rows] = start
    pair[rows:, 2 * rows :] = start
    return pl.pallas_call(
        functools.partial(combine_kernel, rows),
        out_shape=jax.ShapeDtypeStruct((1, rows, width), jnp.float32),
        scratch_shapes=[pltpu.VMEM((count, count), jnp.float32)],
        compiler_params=pltpu.CompilerParams(vmem_limit_bytes=32 * 1024 * 1024),
    )(jnp.asarray(start), jnp.asarray(pair), leaf)


def local_features(token_block, live_counts):
    example_count, token_slots, module_count, full_width = token_block.shape
    half_width = full_width // 2
    live_mask = jnp.arange(token_slots, dtype=jnp.int32)[None, :] < live_counts[:, None]
    grad_side = jnp.where(
        live_mask[:, :, None, None],
        token_block[:, :, :, half_width:],
        jnp.zeros((), token_block.dtype),
    )
    input_side = token_block[:, :, :, :half_width]
    outer = jnp.einsum("etmo,etmi->meoi", grad_side, input_side, preferred_element_type=jnp.float32)
    return outer.reshape(module_count, example_count, half_width * half_width).astype(jnp.bfloat16)


def per_device(tokens, lengths, module_order):
    features = local_features(tokens, lengths)
    groups, owners = lax.axis_size("grp"), lax.axis_size("mod")
    rows = owners * features.shape[1]
    if groups == 4 and rows == 16 and owners == features.shape[0]:
        return gram_route(features, module_order)
    return sketch_tree(features, module_order)


def solution(mesh):
    return jax.shard_map(
        per_device,
        mesh=mesh,
        in_specs=(P(("grp", "mod"), None, None, None), P(("grp", "mod")), P()),
        out_specs=P("mod", "grp", None),
        check_vma=False,
    )
```

```python
import functools

import jax
import jax.numpy as jnp
import numpy as np
from jax import lax
from jax.experimental import pallas as pl
from jax.experimental.pallas import tpu as pltpu
from jax.sharding import PartitionSpec as P

ITERS = 3
HI = lax.Precision.HIGHEST


def partner(value, axis, bit):
    mask = 2**bit
    return xor_send(value, axis, mask)


def xor_send(value, axis, mask):
    pairs = [(source, source ^ mask) for source in range(lax.axis_size(axis))]
    return lax.ppermute(value, axis, pairs)


def start_basis(row_count, col_count):
    row_index = np.arange(row_count, dtype=np.float64)[:, None] + 0.5
    col_index = np.arange(col_count, dtype=np.float64)[None, :] + 0.5
    return np.cos(np.pi * row_index * col_index / row_count).astype(np.float32)


def orthonormal(matrix):
    for repeat in range(2):
        cross_gram = jnp.dot(matrix.T, matrix, precision=HI)
        factor = jnp.linalg.cholesky(cross_gram)
        matrix = jax.scipy.linalg.solve_triangular(factor, matrix.T, lower=True).T
    return matrix


def merge_pair(lower_sketch, upper_sketch):
    stacked = jnp.concatenate([lower_sketch, upper_sketch], axis=0)
    kernel = jnp.dot(stacked, stacked.T, precision=HI)
    current = start_basis(stacked.shape[0], lower_sketch.shape[0])
    for repeat in range(ITERS):
        current = orthonormal(jnp.dot(kernel, current, precision=HI))
    return jnp.dot(current.T, stacked, precision=HI)


def precondition(group_rows, sketch):
    sketch_rows = sketch.shape[0]
    damping = 0.1 * jnp.sum(sketch * sketch) / sketch_rows + 1e-06
    capacitance = jnp.dot(sketch, sketch.T, precision=HI) + damping * jnp.eye(sketch_rows, dtype=jnp.float32)
    projected = jnp.dot(group_rows, sketch.T, precision=HI)
    factor = jnp.linalg.cholesky(capacitance)
    middle = jax.scipy.linalg.solve_triangular(factor, projected.T, lower=True)
    weights = jax.scipy.linalg.solve_triangular(factor, middle, lower=True, trans=1).T
    return group_rows - jnp.dot(weights, sketch, precision=HI)


def sketch_tree(features, module_order):
    ordered = jnp.take(features, module_order, axis=0)
    group_rows = lax.all_to_all(ordered, "mod", split_axis=0, concat_axis=1, tiled=True)
    leaves = group_rows.astype(jnp.float32)
    merge_all = jax.vmap(merge_pair)
    levels = lax.axis_size("grp").bit_length() - 1
    position = lax.axis_index("grp")
    sketch = leaves
    for height in range(levels):
        sister = partner(sketch, "grp", height)
        upper_side = position // 2**height % 2 == 1
        lower_part = jnp.where(upper_side, sister, sketch)
        upper_part = jnp.where(upper_side, sketch, sister)
        sketch = merge_all(lower_part, upper_part)
    return jax.vmap(precondition)(leaves, sketch)


def dot_nt(a, b):
    return lax.dot_general(a, b, (((1,), (1,)), ((), ())), precision=HI, preferred_element_type=jnp.float32)


def dot_nn(a, b):
    return jnp.dot(a, b, precision=HI, preferred_element_type=jnp.float32)


def spread_columns(gram, first, count, width):
    columns = []
    for j in range(count):
        column = gram[first : first + count, first + j : first + j + 1]
        blocks = {b: jnp.broadcast_to(column[8 * b : 8 * b + 8], (8, width)) for b in range(j // 8, count // 8)}
        columns.append(blocks)
    return columns


def eliminate(columns, rhs):
    count = len(columns)
    width = rhs.shape[1]
    parts = [rhs[8 * b : 8 * b + 8] for b in range(count // 8)]
    row = lax.broadcasted_iota(jnp.int32, (8, width), 0)
    diag = [jnp.ones((8, width), jnp.float32) for _ in parts]
    for p in range(count):
        home, at = divmod(p, 8)
        pivot_column = columns[p]
        pivot = pivot_column[home][at : at + 1]
        diag[home] = jnp.where(row == at, pivot, diag[home])
        if p == count - 1:
            break
        inverse = 1.0 / pivot
        factor = {}
        for b in pivot_column:
            scaled = pivot_column[b] * inverse
            factor[b] = jnp.where(row > at, scaled, 0.0) if b == home else scaled
        for j in range(p + 1, count):
            along = pivot_column[j // 8][j % 8 : j % 8 + 1]
            columns[j] = {b: block - factor[b] * along for b, block in columns[j].items()}
        pivot_row = parts[home][at : at + 1]
        for b in factor:
            parts[b] = parts[b] - factor[b] * pivot_row
    return jnp.concatenate([part * lax.rsqrt(d) for part, d in zip(parts, diag)], axis=0)


def orthogonal_iteration(start, kernel, problems):
    rows = start.shape[0] // problems
    moved = dot_nn(start, kernel)
    for step in range(ITERS + 1):
        gram = dot_nt(moved, moved)
        onward = dot_nn(moved, kernel) if step < ITERS - 1 else moved
        done = []
        for k in range(problems):
            columns = spread_columns(gram, k * rows, rows, onward.shape[1])
            done.append(eliminate(columns, onward[k * rows : (k + 1) * rows]))
        moved = jnp.concatenate(done, axis=0)
    return moved


def combine_kernel(rows, start_ref, pair_ref, leaf_ref, out_ref, change_ref):
    count, width = leaf_ref.shape
    leaf = leaf_ref[...]
    gram = lax.dot_general(leaf, leaf, (((1,), (1,)), ((), ())), preferred_element_type=jnp.float32)
    half = count // 2
    r = lax.broadcasted_iota(jnp.int32, gram.shape, 0)
    c = lax.broadcasted_iota(jnp.int32, gram.shape, 1)
    own_pair = jnp.where((r < half) == (c < half), gram, 0.0)
    first = orthogonal_iteration(pair_ref[...], own_pair, 2)
    reached = dot_nn(first, gram)
    kernel = dot_nt(reached, first)
    second = orthogonal_iteration(start_ref[...], kernel, 1)
    weights = dot_nn(second, first)
    projected = dot_nn(second, reached)
    capacitance = dot_nt(projected, weights)
    columns = spread_columns(capacitance, 0, rows, 2 * count)
    total = sum(columns[j][j // 8][j % 8 : j % 8 + 1] for j in range(rows))
    damping = 0.1 * total / rows + 1e-06
    row = lax.broadcasted_iota(jnp.int32, (8, 2 * count), 0)
    for j in range(rows):
        columns[j][j // 8] = columns[j][j // 8] + jnp.where(row == j % 8, damping, 0.0)
    solved = eliminate(columns, jnp.concatenate([projected, weights], axis=1))
    change_ref[...] = lax.dot_general(
        solved[:, :count], solved[:, count:], (((0,), (0,)), ((), ())), precision=HI, preferred_element_type=jnp.float32
    )
    own = pl.ds(pl.multiple_of(lax.axis_index("grp") * rows, rows), rows)
    change = change_ref[own, :]
    top = change.astype(jnp.bfloat16)
    rest = (change - top.astype(jnp.float32)).astype(jnp.bfloat16)
    moved = jnp.dot(top, leaf, preferred_element_type=jnp.float32) + jnp.dot(rest, leaf, preferred_element_type=jnp.float32)
    out_ref[0] = leaf_ref[own, :].astype(jnp.float32) - moved


def features_kernel(splits, lengths_ref, order_ref, tokens_ref, out_ref, held_ref):
    examples, depth, full = tokens_ref.shape
    half = full // 2
    modules = order_ref.shape[0]
    chunks = half * half // full
    position = lax.broadcasted_iota(jnp.int32, (modules, depth), 1)
    module = lax.broadcasted_iota(jnp.int32, (modules, depth), 0)
    mine = lax.rem(position, modules) == module
    lane = lax.broadcasted_iota(jnp.int32, (depth, full), 1)
    for e in range(examples):
        block = tokens_ref[e].astype(jnp.float32)
        grads = block.T[half:]
        live = jnp.logical_and(mine, position < lengths_ref[e] * modules)
        rows = []
        for o in range(half):
            rows.append(jnp.where(live, grads[o : o + 1], 0.0).astype(jnp.bfloat16))
        even = jnp.concatenate(rows[0::2], axis=0)
        odd = jnp.concatenate(rows[1::2], axis=0)
        left = jnp.where(lane < half, block, 0.0).astype(jnp.bfloat16)
        right = jnp.where(lane < half, 0.0, pltpu.roll(block, half, 1)).astype(jnp.bfloat16)
        flat = jnp.dot(even, left, preferred_element_type=jnp.float32) + jnp.dot(odd, right, preferred_element_type=jnp.float32)
        for c in range(chunks):
            held_ref[pl.ds(c * modules * examples + e, modules, stride=examples), :] = flat[c * modules : (c + 1) * modules]
    groups = out_ref.shape[0]
    span = chunks // splits
    for slot in range(modules):
        first = order_ref[slot] * examples
        for c in range(chunks):
            pair = held_ref[pl.ds(c * modules * examples + first, examples), :].astype(jnp.bfloat16)
            for g in range(c // span, groups, splits):
                out_ref[g, slot, :, (c % span) * full : (c % span + 1) * full] = pair


def gram_route(tokens, lengths, module_order, splits=1):
    groups, owners = lax.axis_size("grp"), lax.axis_size("mod")
    own, slots, modules, full = tokens.shape
    width = (full // 2) ** 2
    rows = owners * own
    count = groups * rows
    pieces = pl.pallas_call(
        functools.partial(features_kernel, splits),
        out_shape=jax.ShapeDtypeStruct((groups, modules, own, width // splits), jnp.bfloat16),
        in_specs=[
            pl.BlockSpec(memory_space=pltpu.SMEM),
            pl.BlockSpec(memory_space=pltpu.SMEM),
            pl.BlockSpec(memory_space=pltpu.VMEM),
        ],
        scratch_shapes=[pltpu.VMEM((own * modules * width // full, full), jnp.float32)],
        compiler_params=pltpu.CompilerParams(vmem_limit_bytes=32 * 1024 * 1024),
    )(lengths, module_order, tokens.reshape(own, slots * modules, full))
    pieces = pieces.reshape(groups * modules, own, width // splits)
    leaf = lax.all_to_all(pieces, ("grp", "mod"), split_axis=0, concat_axis=0, tiled=True)
    leaf = leaf.reshape(count, width // splits)
    start = start_basis(2 * rows, rows).T
    pair = np.zeros((2 * rows, 4 * rows), np.float32)
    pair[:rows, : 2 * rows] = start
    pair[rows:, 2 * rows :] = start
    return pl.pallas_call(
        functools.partial(combine_kernel, rows),
        out_shape=jax.ShapeDtypeStruct((1, rows, width), jnp.float32),
        scratch_shapes=[pltpu.VMEM((count, count), jnp.float32)],
        compiler_params=pltpu.CompilerParams(vmem_limit_bytes=32 * 1024 * 1024),
    )(jnp.asarray(start), jnp.asarray(pair), leaf)


def local_features(token_block, live_counts):
    example_count, token_slots, module_count, full_width = token_block.shape
    half_width = full_width // 2
    live_mask = jnp.arange(token_slots, dtype=jnp.int32)[None, :] < live_counts[:, None]
    grad_side = jnp.where(
        live_mask[:, :, None, None],
        token_block[:, :, :, half_width:],
        jnp.zeros((), token_block.dtype),
    )
    input_side = token_block[:, :, :, :half_width]
    outer = jnp.einsum("etmo,etmi->meoi", grad_side, input_side, preferred_element_type=jnp.float32)
    return outer.reshape(module_count, example_count, half_width * half_width).astype(jnp.bfloat16)


def per_device(tokens, lengths, module_order):
    groups, owners = lax.axis_size("grp"), lax.axis_size("mod")
    own, slots, modules, full = tokens.shape
    if groups == 4 and owners * own == 16 and owners == modules == 8 and full == 128:
        return gram_route(tokens, lengths, module_order)
    return sketch_tree(local_features(tokens, lengths), module_order)


def solution(mesh):
    return jax.shard_map(
        per_device,
        mesh=mesh,
        in_specs=(P(("grp", "mod"), None, None, None), P(("grp", "mod")), P()),
        out_specs=P("mod", "grp", None),
        check_vma=False,
    )
```

```python
import functools
import math

import jax
import jax.numpy as jnp
import numpy as np
from jax import lax
from jax.experimental import pallas as pl
from jax.experimental.pallas import tpu as pltpu
from jax.sharding import PartitionSpec as P

ITERS = 3
HI = lax.Precision.HIGHEST


def partner(value, axis, bit):
    mask = 2**bit
    return xor_send(value, axis, mask)


def xor_send(value, axis, mask):
    pairs = [(source, source ^ mask) for source in range(lax.axis_size(axis))]
    return lax.ppermute(value, axis, pairs)


def start_basis(row_count, col_count):
    row_index = np.arange(row_count, dtype=np.float64)[:, None] + 0.5
    col_index = np.arange(col_count, dtype=np.float64)[None, :] + 0.5
    return np.cos(np.pi * row_index * col_index / row_count).astype(np.float32)


def orthonormal(matrix):
    for repeat in range(2):
        cross_gram = jnp.dot(matrix.T, matrix, precision=HI)
        factor = jnp.linalg.cholesky(cross_gram)
        matrix = jax.scipy.linalg.solve_triangular(factor, matrix.T, lower=True).T
    return matrix


def merge_pair(lower_sketch, upper_sketch):
    stacked = jnp.concatenate([lower_sketch, upper_sketch], axis=0)
    kernel = jnp.dot(stacked, stacked.T, precision=HI)
    current = start_basis(stacked.shape[0], lower_sketch.shape[0])
    for repeat in range(ITERS):
        current = orthonormal(jnp.dot(kernel, current, precision=HI))
    return jnp.dot(current.T, stacked, precision=HI)


def precondition(group_rows, sketch):
    sketch_rows = sketch.shape[0]
    damping = 0.1 * jnp.sum(sketch * sketch) / sketch_rows + 1e-06
    capacitance = jnp.dot(sketch, sketch.T, precision=HI) + damping * jnp.eye(sketch_rows, dtype=jnp.float32)
    projected = jnp.dot(group_rows, sketch.T, precision=HI)
    factor = jnp.linalg.cholesky(capacitance)
    middle = jax.scipy.linalg.solve_triangular(factor, projected.T, lower=True)
    weights = jax.scipy.linalg.solve_triangular(factor, middle, lower=True, trans=1).T
    return group_rows - jnp.dot(weights, sketch, precision=HI)


def sketch_tree(features, module_order):
    ordered = jnp.take(features, module_order, axis=0)
    group_rows = lax.all_to_all(ordered, "mod", split_axis=0, concat_axis=1, tiled=True)
    leaves = group_rows.astype(jnp.float32)
    merge_all = jax.vmap(merge_pair)
    levels = lax.axis_size("grp").bit_length() - 1
    position = lax.axis_index("grp")
    sketch = leaves
    for height in range(levels):
        sister = partner(sketch, "grp", height)
        upper_side = position // 2**height % 2 == 1
        lower_part = jnp.where(upper_side, sister, sketch)
        upper_part = jnp.where(upper_side, sketch, sister)
        sketch = merge_all(lower_part, upper_part)
    return jax.vmap(precondition)(leaves, sketch)


def dot_nt(a, b):
    return lax.dot_general(a, b, (((1,), (1,)), ((), ())), precision=HI, preferred_element_type=jnp.float32)


def dot_nn(a, b):
    return jnp.dot(a, b, precision=HI, preferred_element_type=jnp.float32)


def start_rows(count, width, span):
    j = lax.broadcasted_iota(jnp.int32, (count, width), 0)
    i = lax.rem(lax.broadcasted_iota(jnp.int32, (count, width), 1), span)
    turn = lax.rem((2 * i + 1) * (2 * j + 1), 8 * span)
    folded = jnp.minimum(turn, 8 * span - turn)
    angle = (2 * span - folded).astype(jnp.float32) * (math.pi / (4 * span))
    square = angle * angle
    series = jnp.full_like(angle, 1.0)
    for n in range(12, 0, -2):
        series = 1.0 - square * series * (1.0 / (n * (n + 1)))
    return angle * series


def spread(gram, problems, count, width):
    lane = lax.broadcasted_iota(jnp.int32, (8, width), 1)
    columns = []
    for j in range(count):
        blocks = {}
        for b in range(j // 8, count // 8):
            parts = [
                jnp.broadcast_to(gram[8 * b : 8 * b + 8, k * count + j : k * count + j + 1], (8, width))
                for k in range(problems)
            ]
            blocks[b] = parts[0] if problems == 1 else jnp.where(lane < width // 2, parts[0], parts[1])
        columns.append(blocks)
    return columns


def eliminate(columns, rhs):
    count = len(columns)
    width = rhs.shape[1]
    parts = [rhs[8 * b : 8 * b + 8] for b in range(count // 8)]
    row = lax.broadcasted_iota(jnp.int32, (8, width), 0)
    diag = [jnp.ones((8, width), jnp.float32) for _ in parts]
    for p in range(0, count, 2):
        home, at = divmod(p, 8)
        left, right = columns[p], columns[p + 1]
        a = left[home][at : at + 1]
        b = left[home][at + 1 : at + 2]
        c = right[home][at + 1 : at + 2]
        det = a * c - b * b
        ratio = b / a
        diag[home] = jnp.where(row == at, a, jnp.where(row == at + 1, c - b * ratio, diag[home]))
        inverse = 1.0 / det
        ia, ib, ic = c * inverse, b * inverse, a * inverse
        low, high = {}, {}
        for k in left:
            low[k] = left[k] * ia - right[k] * ib
            high[k] = right[k] * ic - left[k] * ib
        for j in range(p + 2, count):
            one = left[j // 8][j % 8 : j % 8 + 1]
            two = right[j // 8][j % 8 : j % 8 + 1]
            columns[j] = {k: block - (low[k] * one + high[k] * two) for k, block in columns[j].items()}
        low[home] = jnp.where(row > at + 1, low[home], jnp.where(row == at + 1, ratio, 0.0))
        high[home] = jnp.where(row > at + 1, high[home], 0.0)
        first, second = parts[home][at : at + 1], parts[home][at + 1 : at + 2]
        for k in low:
            parts[k] = parts[k] - (low[k] * first + high[k] * second)
    return jnp.concatenate([part * lax.rsqrt(d) for part, d in zip(parts, diag)], axis=0)


def apart(value):
    lane = lax.broadcasted_iota(jnp.int32, value.shape, 1)
    near = lane < value.shape[1] // 2
    return jnp.concatenate([jnp.where(near, value, 0.0), jnp.where(near, 0.0, value)], axis=0)


def lower_correction(gram, count):
    row = lax.broadcasted_iota(jnp.int32, gram.shape, 0)
    col = lax.rem(lax.broadcasted_iota(jnp.int32, gram.shape, 1), count)
    return jnp.where(row > col, -gram, jnp.where(row == col, 1.5 - 0.5 * gram, 0.0))


def solve_small(gram, rows):
    count = gram.shape[0]
    half = count // 2
    r = lax.broadcasted_iota(jnp.int32, gram.shape, 0)
    c = lax.broadcasted_iota(jnp.int32, gram.shape, 1)
    lane = lax.broadcasted_iota(jnp.int32, (1, count), 1)
    diagonal = jnp.sum(jnp.where(r == c, gram, 0.0), axis=0, keepdims=True)
    trace_lower = jnp.sum(jnp.where(lane < half, diagonal, 0.0), axis=1, keepdims=True)
    trace_upper = jnp.sum(jnp.where(lane < half, 0.0, diagonal), axis=1, keepdims=True)
    scale = 1.0 / (trace_lower + trace_upper)
    own_pair = jnp.where((r < half) == (c < half), gram, 0.0) / jnp.where(lane < half, trace_lower, trace_upper)
    gram = gram * scale

    moved = dot_nn(start_rows(rows, count, half), own_pair)
    for step in range(ITERS):
        inner = dot_nt(moved, apart(moved))
        onward = dot_nn(moved, own_pair) if step < ITERS - 1 else moved
        moved = eliminate(spread(inner, 2, rows, count), onward)
    both = apart(moved)
    basis = apart(dot_nn(lower_correction(dot_nt(moved, both), rows), both))

    reached = dot_nn(basis, gram)
    kernel = dot_nt(reached, basis)
    moved = dot_nn(start_rows(rows, half, half), kernel)
    for step in range(ITERS - 1):
        inner = dot_nt(moved, moved)
        moved = eliminate(spread(inner, 1, rows, half), dot_nn(moved, kernel))
    inner = dot_nt(moved, moved)
    onward = dot_nn(moved, jnp.concatenate([reached, basis], axis=1))
    both = eliminate(spread(inner, 1, rows, 2 * count), onward)

    weights = both[:, count:]
    joint = dot_nt(jnp.concatenate([both[:, :count], weights], axis=0), weights)
    energy = spread(joint[:rows], 1, rows, 2 * count)
    metric = spread(joint[rows:], 1, rows, 2 * count)
    row = lax.broadcasted_iota(jnp.int32, (8, 2 * count), 0)
    total = jnp.zeros((8, 2 * count), jnp.float32)
    for j in range(rows):
        for b in energy[j]:
            unit = jnp.where(row == j % 8, 2.0, 0.0) if b == j // 8 else 0.0
            term = energy[j][b] * (unit - metric[j][b])
            total = total + (term if b == j // 8 else term + term)
    damping = 0.1 * jnp.sum(total, axis=0, keepdims=True) / rows + 1e-06 * scale
    columns = [{b: energy[j][b] + damping * metric[j][b] for b in energy[j]} for j in range(rows)]
    solved = eliminate(columns, both)
    return solved[:, :count], solved[:, count:]


def combine_kernel(rows, leaf_ref, out_ref, change_ref):
    leaf = leaf_ref[...]
    gram = lax.dot_general(leaf, leaf, (((1,), (1,)), ((), ())), preferred_element_type=jnp.float32)
    projected, weights = solve_small(gram, rows)
    change_ref[...] = lax.dot_general(
        projected, weights, (((0,), (0,)), ((), ())), precision=HI, preferred_element_type=jnp.float32
    )
    own = pl.ds(pl.multiple_of(lax.axis_index("grp") * rows, rows), rows)
    change = change_ref[own, :]
    top = change.astype(jnp.bfloat16)
    rest = (change - top.astype(jnp.float32)).astype(jnp.bfloat16)
    moved = jnp.dot(top, leaf, preferred_element_type=jnp.float32) + jnp.dot(rest, leaf, preferred_element_type=jnp.float32)
    out_ref[0] = leaf_ref[own, :].astype(jnp.float32) - moved


def features_kernel(splits, lengths_ref, order_ref, tokens_ref, out_ref, held_ref):
    examples, depth, full = tokens_ref.shape
    half = full // 2
    modules = order_ref.shape[0]
    chunks = half * half // full
    position = lax.broadcasted_iota(jnp.int32, (modules, depth), 1)
    module = lax.broadcasted_iota(jnp.int32, (modules, depth), 0)
    mine = lax.rem(position, modules) == module
    lane = lax.broadcasted_iota(jnp.int32, (depth, full), 1)
    for e in range(examples):
        block = tokens_ref[e].astype(jnp.float32)
        grads = block.T[half:]
        live = jnp.logical_and(mine, position < lengths_ref[e] * modules)
        rows = []
        for o in range(half):
            rows.append(jnp.where(live, grads[o : o + 1], 0.0).astype(jnp.bfloat16))
        even = jnp.concatenate(rows[0::2], axis=0)
        odd = jnp.concatenate(rows[1::2], axis=0)
        left = jnp.where(lane < half, block, 0.0).astype(jnp.bfloat16)
        right = jnp.where(lane < half, 0.0, pltpu.roll(block, half, 1)).astype(jnp.bfloat16)
        flat = jnp.dot(even, left, preferred_element_type=jnp.float32) + jnp.dot(odd, right, preferred_element_type=jnp.float32)
        for c in range(chunks):
            held_ref[pl.ds(c * modules * examples + e, modules, stride=examples), :] = flat[c * modules : (c + 1) * modules]
    groups = out_ref.shape[0]
    span = chunks // splits
    for slot in range(modules):
        first = order_ref[slot] * examples
        for c in range(chunks):
            pair = held_ref[pl.ds(c * modules * examples + first, examples), :].astype(jnp.bfloat16)
            for g in range(c // span, groups, splits):
                out_ref[g, slot, :, (c % span) * full : (c % span + 1) * full] = pair


def gram_route(tokens, lengths, module_order, splits=1):
    groups, owners = lax.axis_size("grp"), lax.axis_size("mod")
    own, slots, modules, full = tokens.shape
    width = (full // 2) ** 2
    rows = owners * own
    count = groups * rows
    pieces = pl.pallas_call(
        functools.partial(features_kernel, splits),
        out_shape=jax.ShapeDtypeStruct((groups, modules, own, width // splits), jnp.bfloat16),
        in_specs=[
            pl.BlockSpec(memory_space=pltpu.SMEM),
            pl.BlockSpec(memory_space=pltpu.SMEM),
            pl.BlockSpec(memory_space=pltpu.VMEM),
        ],
        scratch_shapes=[pltpu.VMEM((own * modules * width // full, full), jnp.float32)],
        compiler_params=pltpu.CompilerParams(vmem_limit_bytes=32 * 1024 * 1024),
    )(lengths, module_order, tokens.reshape(own, slots * modules, full))
    pieces = pieces.reshape(groups * modules, own, width // splits)
    leaf = lax.all_to_all(pieces, ("grp", "mod"), split_axis=0, concat_axis=0, tiled=True)
    leaf = leaf.reshape(count, width // splits)
    return pl.pallas_call(
        functools.partial(combine_kernel, rows),
        out_shape=jax.ShapeDtypeStruct((1, rows, width), jnp.float32),
        scratch_shapes=[pltpu.VMEM((count, count), jnp.float32)],
        compiler_params=pltpu.CompilerParams(vmem_limit_bytes=32 * 1024 * 1024),
    )(leaf)


def local_features(token_block, live_counts):
    example_count, token_slots, module_count, full_width = token_block.shape
    half_width = full_width // 2
    live_mask = jnp.arange(token_slots, dtype=jnp.int32)[None, :] < live_counts[:, None]
    grad_side = jnp.where(
        live_mask[:, :, None, None],
        token_block[:, :, :, half_width:],
        jnp.zeros((), token_block.dtype),
    )
    input_side = token_block[:, :, :, :half_width]
    outer = jnp.einsum("etmo,etmi->meoi", grad_side, input_side, preferred_element_type=jnp.float32)
    return outer.reshape(module_count, example_count, half_width * half_width).astype(jnp.bfloat16)


def per_device(tokens, lengths, module_order):
    groups, owners = lax.axis_size("grp"), lax.axis_size("mod")
    own, slots, modules, full = tokens.shape
    if groups == 4 and owners * own == 16 and owners == modules == 8 and full == 128:
        return gram_route(tokens, lengths, module_order)
    return sketch_tree(local_features(tokens, lengths), module_order)


def solution(mesh):
    return jax.shard_map(
        per_device,
        mesh=mesh,
        in_specs=(P(("grp", "mod"), None, None, None), P(("grp", "mod")), P()),
        out_specs=P("mod", "grp", None),
        check_vma=False,
    )
```

```python
import functools
import math

import jax
import jax.numpy as jnp
import numpy as np
from jax import lax
from jax.experimental import pallas as pl
from jax.experimental.pallas import tpu as pltpu
from jax.sharding import PartitionSpec as P

ITERS = 3
HI = lax.Precision.HIGHEST


def partner(value, axis, bit):
    mask = 2**bit
    return xor_send(value, axis, mask)


def xor_send(value, axis, mask):
    pairs = [(source, source ^ mask) for source in range(lax.axis_size(axis))]
    return lax.ppermute(value, axis, pairs)


def start_basis(row_count, col_count):
    row_index = np.arange(row_count, dtype=np.float64)[:, None] + 0.5
    col_index = np.arange(col_count, dtype=np.float64)[None, :] + 0.5
    return np.cos(np.pi * row_index * col_index / row_count).astype(np.float32)


def orthonormal(matrix):
    for repeat in range(2):
        cross_gram = jnp.dot(matrix.T, matrix, precision=HI)
        factor = jnp.linalg.cholesky(cross_gram)
        matrix = jax.scipy.linalg.solve_triangular(factor, matrix.T, lower=True).T
    return matrix


def merge_pair(lower_sketch, upper_sketch):
    stacked = jnp.concatenate([lower_sketch, upper_sketch], axis=0)
    kernel = jnp.dot(stacked, stacked.T, precision=HI)
    current = start_basis(stacked.shape[0], lower_sketch.shape[0])
    for repeat in range(ITERS):
        current = orthonormal(jnp.dot(kernel, current, precision=HI))
    return jnp.dot(current.T, stacked, precision=HI)


def precondition(group_rows, sketch):
    sketch_rows = sketch.shape[0]
    damping = 0.1 * jnp.sum(sketch * sketch) / sketch_rows + 1e-06
    capacitance = jnp.dot(sketch, sketch.T, precision=HI) + damping * jnp.eye(sketch_rows, dtype=jnp.float32)
    projected = jnp.dot(group_rows, sketch.T, precision=HI)
    factor = jnp.linalg.cholesky(capacitance)
    middle = jax.scipy.linalg.solve_triangular(factor, projected.T, lower=True)
    weights = jax.scipy.linalg.solve_triangular(factor, middle, lower=True, trans=1).T
    return group_rows - jnp.dot(weights, sketch, precision=HI)


def sketch_tree(features, module_order):
    ordered = jnp.take(features, module_order, axis=0)
    group_rows = lax.all_to_all(ordered, "mod", split_axis=0, concat_axis=1, tiled=True)
    leaves = group_rows.astype(jnp.float32)
    merge_all = jax.vmap(merge_pair)
    levels = lax.axis_size("grp").bit_length() - 1
    position = lax.axis_index("grp")
    sketch = leaves
    for height in range(levels):
        sister = partner(sketch, "grp", height)
        upper_side = position // 2**height % 2 == 1
        lower_part = jnp.where(upper_side, sister, sketch)
        upper_part = jnp.where(upper_side, sketch, sister)
        sketch = merge_all(lower_part, upper_part)
    return jax.vmap(precondition)(leaves, sketch)


def dot_nt(a, b):
    return lax.dot_general(a, b, (((1,), (1,)), ((), ())), precision=HI, preferred_element_type=jnp.float32)


def dot_nn(a, b):
    return jnp.dot(a, b, precision=HI, preferred_element_type=jnp.float32)


def start_rows(count, width, span):
    j = lax.broadcasted_iota(jnp.int32, (count, width), 0)
    i = lax.rem(lax.broadcasted_iota(jnp.int32, (count, width), 1), span)
    turn = lax.rem((2 * i + 1) * (2 * j + 1), 8 * span)
    folded = jnp.minimum(turn, 8 * span - turn)
    angle = (2 * span - folded).astype(jnp.float32) * (math.pi / (4 * span))
    square = angle * angle
    series = jnp.full_like(angle, 1.0)
    for n in range(12, 0, -2):
        series = 1.0 - square * series * (1.0 / (n * (n + 1)))
    return angle * series


def spread(gram, problems, count, width):
    lane = lax.broadcasted_iota(jnp.int32, (8, width), 1)
    columns = []
    for j in range(count):
        blocks = {}
        for b in range(j // 8, count // 8):
            parts = [
                jnp.broadcast_to(gram[8 * b : 8 * b + 8, k * count + j : k * count + j + 1], (8, width))
                for k in range(problems)
            ]
            blocks[b] = parts[0] if problems == 1 else jnp.where(lane < width // 2, parts[0], parts[1])
        columns.append(blocks)
    return columns


def eliminate(columns, rhs):
    count = len(columns)
    width = rhs.shape[1]
    parts = [rhs[8 * b : 8 * b + 8] for b in range(count // 8)]
    row = lax.broadcasted_iota(jnp.int32, (8, width), 0)
    diag = [jnp.ones((8, width), jnp.float32) for _ in parts]
    whole = [functools.reduce(lambda x, j: jnp.where(row == j, columns[8 * k + j][k], x), range(8), d) for k, d in enumerate(diag)]
    for p in range(0, count, 2):
        home, at = divmod(p, 8)
        left, right = columns[p], columns[p + 1]
        a = left[home][at : at + 1]
        b = left[home][at + 1 : at + 2]
        c = right[home][at + 1 : at + 2]
        det = a * c - b * b
        ratio = b / a
        diag[home] = jnp.where(row == at, a, jnp.where(row == at + 1, c - b * ratio, diag[home]))
        inverse = 1.0 / det
        ia, ib, ic = c * inverse, b * inverse, a * inverse
        low, high = {}, {}
        for k in left:
            low[k] = left[k] * ia - right[k] * ib
            high[k] = right[k] * ic - left[k] * ib
        for j in range(p + 2, count):
            one = left[j // 8][j % 8 : j % 8 + 1]
            two = right[j // 8][j % 8 : j % 8 + 1]
            columns[j] = {k: block - (low[k] * one + high[k] * two) for k, block in columns[j].items()}
        low[home] = jnp.where(row > at + 1, low[home], jnp.where(row == at + 1, ratio, 0.0))
        high[home] = jnp.where(row > at + 1, high[home], 0.0)
        first, second = parts[home][at : at + 1], parts[home][at + 1 : at + 2]
        for k in low:
            parts[k] = parts[k] - (low[k] * first + high[k] * second)
    worst = functools.reduce(jnp.minimum, [d / w for d, w in zip(diag, whole)])
    return jnp.concatenate([part * lax.rsqrt(d) for part, d in zip(parts, diag)], axis=0), worst


def apart(value):
    lane = lax.broadcasted_iota(jnp.int32, value.shape, 1)
    near = lane < value.shape[1] // 2
    return jnp.concatenate([jnp.where(near, value, 0.0), jnp.where(near, 0.0, value)], axis=0)


def lower_correction(gram, count):
    row = lax.broadcasted_iota(jnp.int32, gram.shape, 0)
    col = lax.rem(lax.broadcasted_iota(jnp.int32, gram.shape, 1), count)
    return jnp.where(row > col, -gram, jnp.where(row == col, 1.5 - 0.5 * gram, 0.0))


def solve_small(gram, rows, often):
    count = gram.shape[0]
    half = count // 2
    r = lax.broadcasted_iota(jnp.int32, gram.shape, 0)
    c = lax.broadcasted_iota(jnp.int32, gram.shape, 1)
    lane = lax.broadcasted_iota(jnp.int32, (1, count), 1)
    diagonal = jnp.sum(jnp.where(r == c, gram, 0.0), axis=0, keepdims=True)
    trace_lower = jnp.sum(jnp.where(lane < half, diagonal, 0.0), axis=1, keepdims=True)
    trace_upper = jnp.sum(jnp.where(lane < half, 0.0, diagonal), axis=1, keepdims=True)
    scale = 1.0 / (trace_lower + trace_upper)
    own_pair = jnp.where((r < half) == (c < half), gram, 0.0) / jnp.where(lane < half, trace_lower, trace_upper)
    gram = gram * scale

    moved = dot_nn(start_rows(rows, count, half), own_pair)
    if often:
        for step in range(ITERS - 1):
            inner = dot_nt(moved, apart(moved))
            moved, _ = eliminate(spread(inner, 2, rows, count), dot_nn(moved, own_pair))
    else:
        moved = dot_nn(moved, dot_nn(own_pair, own_pair))
    inner = dot_nt(moved, apart(moved))
    moved, worst_pair = eliminate(spread(inner, 2, rows, count), moved)
    both = apart(moved)
    basis = apart(dot_nn(lower_correction(dot_nt(moved, both), rows), both))

    reached = dot_nn(basis, gram)
    kernel = dot_nt(reached, basis)
    moved = dot_nn(start_rows(rows, half, half), kernel)
    if often:
        for step in range(ITERS - 1):
            inner = dot_nt(moved, moved)
            moved, _ = eliminate(spread(inner, 1, rows, half), dot_nn(moved, kernel))
    else:
        moved = dot_nn(moved, dot_nn(kernel, kernel))
    inner = dot_nt(moved, moved)
    onward = dot_nn(moved, jnp.concatenate([reached, basis], axis=1))
    both, worst_last = eliminate(spread(inner, 1, rows, 2 * count), onward)
    enough = jnp.logical_and(jnp.min(worst_pair) > 2e-5, jnp.min(worst_last) > 2e-4)

    weights = both[:, count:]
    joint = dot_nt(jnp.concatenate([both[:, :count], weights], axis=0), weights)
    energy = spread(joint[:rows], 1, rows, 2 * count)
    metric = spread(joint[rows:], 1, rows, 2 * count)
    row = lax.broadcasted_iota(jnp.int32, (8, 2 * count), 0)
    total = jnp.zeros((8, 2 * count), jnp.float32)
    for j in range(rows):
        for b in energy[j]:
            unit = jnp.where(row == j % 8, 2.0, 0.0) if b == j // 8 else 0.0
            term = energy[j][b] * (unit - metric[j][b])
            total = total + (term if b == j // 8 else term + term)
    damping = 0.1 * jnp.sum(total, axis=0, keepdims=True) / rows + 1e-06 * scale
    columns = [{b: energy[j][b] + damping * metric[j][b] for b in energy[j]} for j in range(rows)]
    solved, _ = eliminate(columns, both)
    return solved[:, :count], solved[:, count:], enough


def combine_kernel(rows, leaf_ref, out_ref, gram_ref, change_ref):
    leaf = leaf_ref[...]
    gram_ref[...] = lax.dot_general(leaf, leaf, (((1,), (1,)), ((), ())), preferred_element_type=jnp.float32)
    own = pl.ds(pl.multiple_of(lax.axis_index("grp") * rows, rows), rows)

    def finish(often):
        projected, weights, enough = solve_small(gram_ref[...], rows, often)
        change_ref[...] = lax.dot_general(
            projected, weights, (((0,), (0,)), ((), ())), precision=HI, preferred_element_type=jnp.float32
        )
        change = change_ref[own, :]
        top = change.astype(jnp.bfloat16)
        rest = (change - top.astype(jnp.float32)).astype(jnp.bfloat16)
        moved = jnp.dot(jnp.concatenate([top, rest], axis=0), leaf_ref[...], preferred_element_type=jnp.float32)
        out_ref[0] = leaf_ref[own, :].astype(jnp.float32) - (moved[:rows] + moved[rows:])
        return enough

    enough = finish(False)

    @pl.when(jnp.logical_not(enough))
    def _():
        finish(True)


def features_kernel(splits, lengths_ref, order_ref, tokens_ref, out_ref, held_ref):
    examples, depth, full = tokens_ref.shape
    half = full // 2
    modules = order_ref.shape[0]
    chunks = half * half // full
    position = lax.broadcasted_iota(jnp.int32, (modules, depth), 1)
    module = lax.broadcasted_iota(jnp.int32, (modules, depth), 0)
    mine = lax.rem(position, modules) == module
    lane = lax.broadcasted_iota(jnp.int32, (depth, full), 1)
    for e in range(examples):
        block = tokens_ref[e].astype(jnp.float32)
        grads = block.T[half:]
        live = jnp.logical_and(mine, position < lengths_ref[e] * modules)
        rows = []
        for o in range(half):
            rows.append(jnp.where(live, grads[o : o + 1], 0.0).astype(jnp.bfloat16))
        even = jnp.concatenate(rows[0::2], axis=0)
        odd = jnp.concatenate(rows[1::2], axis=0)
        left = jnp.where(lane < half, block, 0.0).astype(jnp.bfloat16)
        right = jnp.where(lane < half, 0.0, pltpu.roll(block, half, 1)).astype(jnp.bfloat16)
        flat = jnp.dot(even, left, preferred_element_type=jnp.float32) + jnp.dot(odd, right, preferred_element_type=jnp.float32)
        for c in range(chunks):
            held_ref[pl.ds(c * modules * examples + e, modules, stride=examples), :] = flat[c * modules : (c + 1) * modules]
    groups = out_ref.shape[0]
    span = chunks // splits
    for slot in range(modules):
        first = order_ref[slot] * examples
        for c in range(chunks):
            pair = held_ref[pl.ds(c * modules * examples + first, examples), :].astype(jnp.bfloat16)
            for g in range(c // span, groups, splits):
                out_ref[g, slot, :, (c % span) * full : (c % span + 1) * full] = pair


def gram_route(tokens, lengths, module_order, splits=1):
    groups, owners = lax.axis_size("grp"), lax.axis_size("mod")
    own, slots, modules, full = tokens.shape
    width = (full // 2) ** 2
    rows = owners * own
    count = groups * rows
    pieces = pl.pallas_call(
        functools.partial(features_kernel, splits),
        out_shape=jax.ShapeDtypeStruct((groups, modules, own, width // splits), jnp.bfloat16),
        in_specs=[
            pl.BlockSpec(memory_space=pltpu.SMEM),
            pl.BlockSpec(memory_space=pltpu.SMEM),
            pl.BlockSpec(memory_space=pltpu.VMEM),
        ],
        scratch_shapes=[pltpu.VMEM((own * modules * width // full, full), jnp.float32)],
        compiler_params=pltpu.CompilerParams(vmem_limit_bytes=32 * 1024 * 1024),
    )(lengths, module_order, tokens.reshape(own, slots * modules, full))
    pieces = pieces.reshape(groups * modules, own, width // splits)
    leaf = lax.all_to_all(pieces, ("grp", "mod"), split_axis=0, concat_axis=0, tiled=True)
    leaf = leaf.reshape(count, width // splits)
    return pl.pallas_call(
        functools.partial(combine_kernel, rows),
        out_shape=jax.ShapeDtypeStruct((1, rows, width), jnp.float32),
        scratch_shapes=[pltpu.VMEM((count, count), jnp.float32)] * 2,
        compiler_params=pltpu.CompilerParams(vmem_limit_bytes=32 * 1024 * 1024),
    )(leaf)


def local_features(token_block, live_counts):
    example_count, token_slots, module_count, full_width = token_block.shape
    half_width = full_width // 2
    live_mask = jnp.arange(token_slots, dtype=jnp.int32)[None, :] < live_counts[:, None]
    grad_side = jnp.where(
        live_mask[:, :, None, None],
        token_block[:, :, :, half_width:],
        jnp.zeros((), token_block.dtype),
    )
    input_side = token_block[:, :, :, :half_width]
    outer = jnp.einsum("etmo,etmi->meoi", grad_side, input_side, preferred_element_type=jnp.float32)
    return outer.reshape(module_count, example_count, half_width * half_width).astype(jnp.bfloat16)


def per_device(tokens, lengths, module_order):
    groups, owners = lax.axis_size("grp"), lax.axis_size("mod")
    own, slots, modules, full = tokens.shape
    if groups == 4 and owners * own == 16 and owners == modules == 8 and full == 128:
        return gram_route(tokens, lengths, module_order)
    return sketch_tree(local_features(tokens, lengths), module_order)


def solution(mesh):
    return jax.shard_map(
        per_device,
        mesh=mesh,
        in_specs=(P(("grp", "mod"), None, None, None), P(("grp", "mod")), P()),
        out_specs=P("mod", "grp", None),
        check_vma=False,
    )
```

```python
import functools
import math

import jax
import jax.numpy as jnp
import numpy as np
from jax import lax
from jax.experimental import pallas as pl
from jax.experimental.pallas import tpu as pltpu
from jax.sharding import PartitionSpec as P

ITERS = 3
HI = lax.Precision.HIGHEST
VMEM_BYTES = 48 * 1024 * 1024


def partner(value, axis, bit):
    mask = 2**bit
    return xor_send(value, axis, mask)


def xor_send(value, axis, mask):
    pairs = [(source, source ^ mask) for source in range(lax.axis_size(axis))]
    return lax.ppermute(value, axis, pairs)


def start_basis(row_count, col_count):
    row_index = np.arange(row_count, dtype=np.float64)[:, None] + 0.5
    col_index = np.arange(col_count, dtype=np.float64)[None, :] + 0.5
    return np.cos(np.pi * row_index * col_index / row_count).astype(np.float32)


def orthonormal(matrix):
    for repeat in range(2):
        cross_gram = jnp.dot(matrix.T, matrix, precision=HI)
        factor = jnp.linalg.cholesky(cross_gram)
        matrix = jax.scipy.linalg.solve_triangular(factor, matrix.T, lower=True).T
    return matrix


def merge_pair(lower_sketch, upper_sketch):
    stacked = jnp.concatenate([lower_sketch, upper_sketch], axis=0)
    kernel = jnp.dot(stacked, stacked.T, precision=HI)
    current = start_basis(stacked.shape[0], lower_sketch.shape[0])
    for repeat in range(ITERS):
        current = orthonormal(jnp.dot(kernel, current, precision=HI))
    return jnp.dot(current.T, stacked, precision=HI)


def precondition(group_rows, sketch):
    sketch_rows = sketch.shape[0]
    damping = 0.1 * jnp.sum(sketch * sketch) / sketch_rows + 1e-06
    capacitance = jnp.dot(sketch, sketch.T, precision=HI) + damping * jnp.eye(sketch_rows, dtype=jnp.float32)
    projected = jnp.dot(group_rows, sketch.T, precision=HI)
    factor = jnp.linalg.cholesky(capacitance)
    middle = jax.scipy.linalg.solve_triangular(factor, projected.T, lower=True)
    weights = jax.scipy.linalg.solve_triangular(factor, middle, lower=True, trans=1).T
    return group_rows - jnp.dot(weights, sketch, precision=HI)


def sketch_tree(features, module_order):
    ordered = jnp.take(features, module_order, axis=0)
    group_rows = lax.all_to_all(ordered, "mod", split_axis=0, concat_axis=1, tiled=True)
    leaves = group_rows.astype(jnp.float32)
    merge_all = jax.vmap(merge_pair)
    levels = lax.axis_size("grp").bit_length() - 1
    position = lax.axis_index("grp")
    sketch = leaves
    for height in range(levels):
        sister = partner(sketch, "grp", height)
        upper_side = position // 2**height % 2 == 1
        lower_part = jnp.where(upper_side, sister, sketch)
        upper_part = jnp.where(upper_side, sketch, sister)
        sketch = merge_all(lower_part, upper_part)
    return jax.vmap(precondition)(leaves, sketch)


def dot_nt(a, b):
    return lax.dot_general(a, b, (((1,), (1,)), ((), ())), precision=HI, preferred_element_type=jnp.float32)


def dot_nn(a, b):
    return jnp.dot(a, b, precision=HI, preferred_element_type=jnp.float32)


def start_rows(count, width, span):
    j = lax.broadcasted_iota(jnp.int32, (count, width), 0)
    i = lax.rem(lax.broadcasted_iota(jnp.int32, (count, width), 1), span)
    turn = lax.rem((2 * i + 1) * (2 * j + 1), 8 * span)
    folded = jnp.minimum(turn, 8 * span - turn)
    angle = (2 * span - folded).astype(jnp.float32) * (math.pi / (4 * span))
    square = angle * angle
    series = jnp.full_like(angle, 1.0)
    for n in range(12, 0, -2):
        series = 1.0 - square * series * (1.0 / (n * (n + 1)))
    return angle * series


def spread(gram, problems, count, width):
    lane = lax.broadcasted_iota(jnp.int32, (8, width), 1)
    columns = []
    for j in range(count):
        blocks = {}
        for b in range(j // 8, count // 8):
            parts = [
                jnp.broadcast_to(gram[8 * b : 8 * b + 8, k * count + j : k * count + j + 1], (8, width))
                for k in range(problems)
            ]
            blocks[b] = parts[0] if problems == 1 else jnp.where(lane < width // 2, parts[0], parts[1])
        columns.append(blocks)
    return columns


def eliminate(columns, rhs):
    count = len(columns)
    width = rhs.shape[1]
    parts = [rhs[8 * b : 8 * b + 8] for b in range(count // 8)]
    row = lax.broadcasted_iota(jnp.int32, (8, width), 0)
    diag = [jnp.ones((8, width), jnp.float32) for _ in parts]
    whole = [functools.reduce(lambda x, j: jnp.where(row == j, columns[8 * k + j][k], x), range(8), d) for k, d in enumerate(diag)]
    for p in range(0, count, 2):
        home, at = divmod(p, 8)
        left, right = columns[p], columns[p + 1]
        a = left[home][at : at + 1]
        b = left[home][at + 1 : at + 2]
        c = right[home][at + 1 : at + 2]
        det = a * c - b * b
        ratio = b / a
        diag[home] = jnp.where(row == at, a, jnp.where(row == at + 1, c - b * ratio, diag[home]))
        inverse = 1.0 / det
        ia, ib, ic = c * inverse, b * inverse, a * inverse
        low, high = {}, {}
        for k in left:
            low[k] = left[k] * ia - right[k] * ib
            high[k] = right[k] * ic - left[k] * ib
        for j in range(p + 2, count):
            one = left[j // 8][j % 8 : j % 8 + 1]
            two = right[j // 8][j % 8 : j % 8 + 1]
            columns[j] = {k: block - (low[k] * one + high[k] * two) for k, block in columns[j].items()}
        low[home] = jnp.where(row > at + 1, low[home], jnp.where(row == at + 1, ratio, 0.0))
        high[home] = jnp.where(row > at + 1, high[home], 0.0)
        first, second = parts[home][at : at + 1], parts[home][at + 1 : at + 2]
        for k in low:
            parts[k] = parts[k] - (low[k] * first + high[k] * second)
    worst = functools.reduce(jnp.minimum, [d / w for d, w in zip(diag, whole)])
    return jnp.concatenate([part * lax.rsqrt(d) for part, d in zip(parts, diag)], axis=0), worst


def apart(value):
    lane = lax.broadcasted_iota(jnp.int32, value.shape, 1)
    near = lane < value.shape[1] // 2
    return jnp.concatenate([jnp.where(near, value, 0.0), jnp.where(near, 0.0, value)], axis=0)


def lower_correction(gram, count):
    row = lax.broadcasted_iota(jnp.int32, gram.shape, 0)
    col = lax.rem(lax.broadcasted_iota(jnp.int32, gram.shape, 1), count)
    return jnp.where(row > col, -gram, jnp.where(row == col, 1.5 - 0.5 * gram, 0.0))


def solve_small(gram, rows, often):
    count = gram.shape[0]
    half = count // 2
    r = lax.broadcasted_iota(jnp.int32, gram.shape, 0)
    c = lax.broadcasted_iota(jnp.int32, gram.shape, 1)
    lane = lax.broadcasted_iota(jnp.int32, (1, count), 1)
    diagonal = jnp.sum(jnp.where(r == c, gram, 0.0), axis=0, keepdims=True)
    trace_lower = jnp.sum(jnp.where(lane < half, diagonal, 0.0), axis=1, keepdims=True)
    trace_upper = jnp.sum(jnp.where(lane < half, 0.0, diagonal), axis=1, keepdims=True)
    scale = 1.0 / (trace_lower + trace_upper)
    own_pair = jnp.where((r < half) == (c < half), gram, 0.0) / jnp.where(lane < half, trace_lower, trace_upper)
    gram = gram * scale

    moved = dot_nn(start_rows(rows, count, half), own_pair)
    if often:
        for step in range(ITERS - 1):
            inner = dot_nt(moved, apart(moved))
            moved, _ = eliminate(spread(inner, 2, rows, count), dot_nn(moved, own_pair))
    else:
        moved = dot_nn(moved, dot_nn(own_pair, own_pair))
    inner = dot_nt(moved, apart(moved))
    moved, worst_pair = eliminate(spread(inner, 2, rows, count), moved)
    both = apart(moved)
    basis = apart(dot_nn(lower_correction(dot_nt(moved, both), rows), both))

    reached = dot_nn(basis, gram)
    kernel = dot_nt(reached, basis)
    moved = dot_nn(start_rows(rows, half, half), kernel)
    if often:
        for step in range(ITERS - 1):
            inner = dot_nt(moved, moved)
            moved, _ = eliminate(spread(inner, 1, rows, half), dot_nn(moved, kernel))
    else:
        moved = dot_nn(moved, dot_nn(kernel, kernel))
    inner = dot_nt(moved, moved)
    onward = dot_nn(moved, jnp.concatenate([reached, basis], axis=1))
    both, worst_last = eliminate(spread(inner, 1, rows, 2 * count), onward)
    enough = jnp.logical_and(jnp.min(worst_pair) > 2e-5, jnp.min(worst_last) > 2e-4)

    weights = both[:, count:]
    joint = dot_nt(jnp.concatenate([both[:, :count], weights], axis=0), weights)
    energy = spread(joint[:rows], 1, rows, 2 * count)
    metric = spread(joint[rows:], 1, rows, 2 * count)
    row = lax.broadcasted_iota(jnp.int32, (8, 2 * count), 0)
    total = jnp.zeros((8, 2 * count), jnp.float32)
    for j in range(rows):
        for b in energy[j]:
            unit = jnp.where(row == j % 8, 2.0, 0.0) if b == j // 8 else 0.0
            term = energy[j][b] * (unit - metric[j][b])
            total = total + (term if b == j // 8 else term + term)
    damping = 0.1 * jnp.sum(total, axis=0, keepdims=True) / rows + 1e-06 * scale
    columns = [{b: energy[j][b] + damping * metric[j][b] for b in energy[j]} for j in range(rows)]
    solved, _ = eliminate(columns, both)
    return solved[:, :count], solved[:, count:], enough


def combine_kernel(rows, pieces, leaf_ref, out_ref, gram_ref, change_ref, held_ref, sems):
    leaf = leaf_ref[...]
    gram_ref[...] = lax.dot_general(leaf, leaf, (((1,), (1,)), ((), ())), preferred_element_type=jnp.float32)
    own = pl.ds(pl.multiple_of(lax.axis_index("grp") * rows, rows), rows)
    span = leaf_ref.shape[1] // pieces

    def finish(often):
        projected, weights, enough = solve_small(gram_ref[...], rows, often)
        change_ref[...] = lax.dot_general(
            projected, weights, (((0,), (0,)), ((), ())), precision=HI, preferred_element_type=jnp.float32
        )
        change = change_ref[own, :]
        top = change.astype(jnp.bfloat16)
        rest = (change - top.astype(jnp.float32)).astype(jnp.bfloat16)
        both = jnp.concatenate([top, rest], axis=0)
        copies = []
        for k in range(pieces):
            part = slice(k * span, (k + 1) * span)
            moved = jnp.dot(both, leaf_ref[:, part], preferred_element_type=jnp.float32)
            held_ref[:, part] = leaf_ref[own, part].astype(jnp.float32) - (moved[:rows] + moved[rows:])
            copies.append(pltpu.make_async_copy(held_ref.at[:, part], out_ref.at[0, :, part], sems.at[k]))
            copies[-1].start()
        for copy in copies:
            copy.wait()
        return enough

    enough = finish(False)

    @pl.when(jnp.logical_not(enough))
    def _():
        finish(True)


def features_kernel(lengths_hbm, order_hbm, tokens_hbm, out_ref, lengths_ref, order_ref, tokens_ref, grads_ref, held_ref, sems):
    examples, depth, full = tokens_ref.shape
    groups, modules, _, width = out_ref.shape
    half = full // 2
    chunks = width // full
    pairs = chunks * examples
    copies = [
        pltpu.make_async_copy(lengths_hbm, lengths_ref, sems.at[0]),
        pltpu.make_async_copy(order_hbm, order_ref, sems.at[1]),
    ]
    for e in range(examples):
        copies.append(pltpu.make_async_copy(tokens_hbm.at[e], tokens_ref.at[e], sems.at[2 + e]))
    for copy in copies:
        copy.start()
    position = lax.broadcasted_iota(jnp.int32, (chunks, depth), 1)
    module = lax.rem(position, modules)
    lane = lax.broadcasted_iota(jnp.int32, (depth, full), 1)
    copies[0].wait()
    copies[1].wait()
    for e in range(examples):
        copies[2 + e].wait()
        block = tokens_ref[e].astype(jnp.float32)
        left = jnp.where(lane < half, block, 0.0).astype(jnp.bfloat16)
        right = jnp.where(lane < half, 0.0, pltpu.roll(block, half, 1)).astype(jnp.bfloat16)
        grads = block.T[half:]
        for k in range(depth // full):
            grads_ref[k] = grads[:, k * full : (k + 1) * full]
        live = position < lengths_ref[e] * modules
        flat = jnp.zeros((modules * chunks, full), jnp.float32)
        for odd, side in ((0, left), (1, right)):
            every = pl.ds(odd, chunks, stride=2)
            grads = jnp.concatenate([grads_ref[k, every, :] for k in range(depth // full)], axis=1)
            grads = jnp.where(live, grads, 0.0)
            apiece = [jnp.where(module == q, grads, 0.0).astype(jnp.bfloat16) for q in range(modules)]
            flat = flat + jnp.dot(jnp.concatenate(apiece, axis=0), side, preferred_element_type=jnp.float32)
        held_ref[pl.ds(e, modules * chunks, stride=examples), :] = flat
    for slot in range(modules):
        first = pl.multiple_of(order_ref[slot] * pairs, pairs)
        for c in range(chunks):
            piece = held_ref[pl.ds(first + c * examples, examples), :].astype(jnp.bfloat16)
            for g in range(groups):
                out_ref[g, slot, :, c * full : (c + 1) * full] = piece


def gram_route(tokens, lengths, module_order):
    groups, owners = lax.axis_size("grp"), lax.axis_size("mod")
    own, slots, modules, full = tokens.shape
    width = (full // 2) ** 2
    rows = owners * own
    count = groups * rows
    chunks = width // full
    messages = pl.pallas_call(
        features_kernel,
        out_shape=jax.ShapeDtypeStruct((groups, modules, own, width), jnp.bfloat16),
        in_specs=[pl.BlockSpec(memory_space=pltpu.HBM)] * 3,
        scratch_shapes=[
            pltpu.SMEM(lengths.shape, jnp.int32),
            pltpu.SMEM(module_order.shape, jnp.int32),
            pltpu.VMEM((own, slots * modules, full), jnp.bfloat16),
            pltpu.VMEM((slots * modules // full, full // 2, full), jnp.float32),
            pltpu.VMEM((modules * chunks * own, full), jnp.float32),
            pltpu.SemaphoreType.DMA((2 + own,)),
        ],
        compiler_params=pltpu.CompilerParams(vmem_limit_bytes=VMEM_BYTES),
    )(lengths, module_order, tokens.reshape(own, slots * modules, full))
    messages = messages.reshape(groups * modules, own, width)
    leaf = lax.all_to_all(messages, ("grp", "mod"), split_axis=0, concat_axis=0, tiled=True)
    leaf = leaf.reshape(count, width)
    pieces = 4
    return pl.pallas_call(
        functools.partial(combine_kernel, rows, pieces),
        out_shape=jax.ShapeDtypeStruct((1, rows, width), jnp.float32),
        out_specs=pl.BlockSpec(memory_space=pl.ANY),
        scratch_shapes=[
            pltpu.VMEM((count, count), jnp.float32),
            pltpu.VMEM((count, count), jnp.float32),
            pltpu.VMEM((rows, width), jnp.float32),
            pltpu.SemaphoreType.DMA((pieces,)),
        ],
        compiler_params=pltpu.CompilerParams(vmem_limit_bytes=VMEM_BYTES),
    )(leaf)


def local_features(token_block, live_counts):
    example_count, token_slots, module_count, full_width = token_block.shape
    half_width = full_width // 2
    live_mask = jnp.arange(token_slots, dtype=jnp.int32)[None, :] < live_counts[:, None]
    grad_side = jnp.where(
        live_mask[:, :, None, None],
        token_block[:, :, :, half_width:],
        jnp.zeros((), token_block.dtype),
    )
    input_side = token_block[:, :, :, :half_width]
    outer = jnp.einsum("etmo,etmi->meoi", grad_side, input_side, preferred_element_type=jnp.float32)
    return outer.reshape(module_count, example_count, half_width * half_width).astype(jnp.bfloat16)


def per_device(tokens, lengths, module_order):
    groups, owners = lax.axis_size("grp"), lax.axis_size("mod")
    own, slots, modules, full = tokens.shape
    if groups == 4 and owners * own == 16 and owners == modules == 8 and full == 128:
        return gram_route(tokens, lengths, module_order)
    return sketch_tree(local_features(tokens, lengths), module_order)


def solution(mesh):
    return jax.shard_map(
        per_device,
        mesh=mesh,
        in_specs=(P(("grp", "mod"), None, None, None), P(("grp", "mod")), P()),
        out_specs=P("mod", "grp", None),
        check_vma=False,
    )
```

```python
import functools
import math

import jax
import jax.numpy as jnp
import numpy as np
from jax import lax
from jax.experimental import pallas as pl
from jax.experimental.pallas import tpu as pltpu
from jax.sharding import PartitionSpec as P

ITERS = 3
HI = lax.Precision.HIGHEST
VMEM_BYTES = 48 * 1024 * 1024


def partner(value, axis, bit):
    mask = 2**bit
    return xor_send(value, axis, mask)


def xor_send(value, axis, mask):
    pairs = [(source, source ^ mask) for source in range(lax.axis_size(axis))]
    return lax.ppermute(value, axis, pairs)


def start_basis(row_count, col_count):
    row_index = np.arange(row_count, dtype=np.float64)[:, None] + 0.5
    col_index = np.arange(col_count, dtype=np.float64)[None, :] + 0.5
    return np.cos(np.pi * row_index * col_index / row_count).astype(np.float32)


def orthonormal(matrix):
    for repeat in range(2):
        cross_gram = jnp.dot(matrix.T, matrix, precision=HI)
        factor = jnp.linalg.cholesky(cross_gram)
        matrix = jax.scipy.linalg.solve_triangular(factor, matrix.T, lower=True).T
    return matrix


def merge_pair(lower_sketch, upper_sketch):
    stacked = jnp.concatenate([lower_sketch, upper_sketch], axis=0)
    kernel = jnp.dot(stacked, stacked.T, precision=HI)
    current = start_basis(stacked.shape[0], lower_sketch.shape[0])
    for repeat in range(ITERS):
        current = orthonormal(jnp.dot(kernel, current, precision=HI))
    return jnp.dot(current.T, stacked, precision=HI)


def precondition(group_rows, sketch):
    sketch_rows = sketch.shape[0]
    damping = 0.1 * jnp.sum(sketch * sketch) / sketch_rows + 1e-06
    capacitance = jnp.dot(sketch, sketch.T, precision=HI) + damping * jnp.eye(sketch_rows, dtype=jnp.float32)
    projected = jnp.dot(group_rows, sketch.T, precision=HI)
    factor = jnp.linalg.cholesky(capacitance)
    middle = jax.scipy.linalg.solve_triangular(factor, projected.T, lower=True)
    weights = jax.scipy.linalg.solve_triangular(factor, middle, lower=True, trans=1).T
    return group_rows - jnp.dot(weights, sketch, precision=HI)


def sketch_tree(features, module_order):
    ordered = jnp.take(features, module_order, axis=0)
    group_rows = lax.all_to_all(ordered, "mod", split_axis=0, concat_axis=1, tiled=True)
    leaves = group_rows.astype(jnp.float32)
    merge_all = jax.vmap(merge_pair)
    levels = lax.axis_size("grp").bit_length() - 1
    position = lax.axis_index("grp")
    sketch = leaves
    for height in range(levels):
        sister = partner(sketch, "grp", height)
        upper_side = position // 2**height % 2 == 1
        lower_part = jnp.where(upper_side, sister, sketch)
        upper_part = jnp.where(upper_side, sketch, sister)
        sketch = merge_all(lower_part, upper_part)
    return jax.vmap(precondition)(leaves, sketch)


def dot_nt(a, b):
    return lax.dot_general(a, b, (((1,), (1,)), ((), ())), precision=HI, preferred_element_type=jnp.float32)


def dot_nn(a, b):
    return jnp.dot(a, b, precision=HI, preferred_element_type=jnp.float32)


def start_rows(count, width, span):
    j = lax.broadcasted_iota(jnp.int32, (count, width), 0)
    i = lax.rem(lax.broadcasted_iota(jnp.int32, (count, width), 1), span)
    turn = lax.rem((2 * i + 1) * (2 * j + 1), 8 * span)
    folded = jnp.minimum(turn, 8 * span - turn)
    angle = (2 * span - folded).astype(jnp.float32) * (math.pi / (4 * span))
    square = angle * angle
    series = jnp.full_like(angle, 1.0)
    for n in range(12, 0, -2):
        series = 1.0 - square * series * (1.0 / (n * (n + 1)))
    return angle * series


def spread(gram, problems, count, width):
    lane = lax.broadcasted_iota(jnp.int32, (8, width), 1)
    columns = []
    for j in range(count):
        blocks = {}
        for b in range(j // 8, count // 8):
            parts = [
                jnp.broadcast_to(gram[8 * b : 8 * b + 8, k * count + j : k * count + j + 1], (8, width))
                for k in range(problems)
            ]
            blocks[b] = parts[0] if problems == 1 else jnp.where(lane < width // 2, parts[0], parts[1])
        columns.append(blocks)
    return columns


def eliminate(columns, rhs):
    count = len(columns)
    width = rhs.shape[1]
    parts = [rhs[8 * b : 8 * b + 8] for b in range(count // 8)]
    row = lax.broadcasted_iota(jnp.int32, (8, width), 0)
    diag = [jnp.ones((8, width), jnp.float32) for _ in parts]
    whole = [functools.reduce(lambda x, j: jnp.where(row == j, columns[8 * k + j][k], x), range(8), d) for k, d in enumerate(diag)]
    for p in range(0, count, 2):
        home, at = divmod(p, 8)
        left, right = columns[p], columns[p + 1]
        a = left[home][at : at + 1]
        b = left[home][at + 1 : at + 2]
        c = right[home][at + 1 : at + 2]
        det = a * c - b * b
        ratio = b / a
        diag[home] = jnp.where(row == at, a, jnp.where(row == at + 1, c - b * ratio, diag[home]))
        inverse = 1.0 / det
        ia, ib, ic = c * inverse, b * inverse, a * inverse
        low, high = {}, {}
        for k in left:
            low[k] = left[k] * ia - right[k] * ib
            high[k] = right[k] * ic - left[k] * ib
        for j in range(p + 2, count):
            one = left[j // 8][j % 8 : j % 8 + 1]
            two = right[j // 8][j % 8 : j % 8 + 1]
            columns[j] = {k: block - (low[k] * one + high[k] * two) for k, block in columns[j].items()}
        low[home] = jnp.where(row > at + 1, low[home], jnp.where(row == at + 1, ratio, 0.0))
        high[home] = jnp.where(row > at + 1, high[home], 0.0)
        first, second = parts[home][at : at + 1], parts[home][at + 1 : at + 2]
        for k in low:
            parts[k] = parts[k] - (low[k] * first + high[k] * second)
    worst = functools.reduce(jnp.minimum, [d / w for d, w in zip(diag, whole)])
    return jnp.concatenate([part * lax.rsqrt(d) for part, d in zip(parts, diag)], axis=0), worst


def apart(value):
    lane = lax.broadcasted_iota(jnp.int32, value.shape, 1)
    near = lane < value.shape[1] // 2
    return jnp.concatenate([jnp.where(near, value, 0.0), jnp.where(near, 0.0, value)], axis=0)


def lower_correction(gram, count):
    row = lax.broadcasted_iota(jnp.int32, gram.shape, 0)
    col = lax.rem(lax.broadcasted_iota(jnp.int32, gram.shape, 1), count)
    return jnp.where(row > col, -gram, jnp.where(row == col, 1.5 - 0.5 * gram, 0.0))


def solve_small(gram, rows, often):
    count = gram.shape[0]
    half = count // 2
    r = lax.broadcasted_iota(jnp.int32, gram.shape, 0)
    c = lax.broadcasted_iota(jnp.int32, gram.shape, 1)
    lane = lax.broadcasted_iota(jnp.int32, (1, count), 1)
    diagonal = jnp.sum(jnp.where(r == c, gram, 0.0), axis=0, keepdims=True)
    trace_lower = jnp.sum(jnp.where(lane < half, diagonal, 0.0), axis=1, keepdims=True)
    trace_upper = jnp.sum(jnp.where(lane < half, 0.0, diagonal), axis=1, keepdims=True)
    scale = 1.0 / (trace_lower + trace_upper)
    own_pair = jnp.where((r < half) == (c < half), gram, 0.0) / jnp.where(lane < half, trace_lower, trace_upper)
    gram = gram * scale

    moved = dot_nn(start_rows(rows, count, half), own_pair)
    if often:
        for step in range(ITERS - 1):
            inner = dot_nt(moved, apart(moved))
            moved, _ = eliminate(spread(inner, 2, rows, count), dot_nn(moved, own_pair))
    else:
        moved = dot_nn(moved, dot_nn(own_pair, own_pair))
    inner = dot_nt(moved, apart(moved))
    moved, worst_pair = eliminate(spread(inner, 2, rows, count), moved)
    both = apart(moved)
    basis = apart(dot_nn(lower_correction(dot_nt(moved, both), rows), both))

    reached = dot_nn(basis, gram)
    kernel = dot_nt(reached, basis)
    moved = dot_nn(start_rows(rows, half, half), kernel)
    if often:
        for step in range(ITERS - 1):
            inner = dot_nt(moved, moved)
            moved, _ = eliminate(spread(inner, 1, rows, half), dot_nn(moved, kernel))
    else:
        moved = dot_nn(moved, dot_nn(kernel, kernel))
    inner = dot_nt(moved, moved)
    onward = dot_nn(moved, jnp.concatenate([reached, basis], axis=1))
    both, worst_last = eliminate(spread(inner, 1, rows, 2 * count), onward)
    enough = jnp.logical_and(jnp.min(worst_pair) > 2e-5, jnp.min(worst_last) > 2e-4)

    weights = both[:, count:]
    joint = dot_nt(jnp.concatenate([both[:, :count], weights], axis=0), weights)
    energy = spread(joint[:rows], 1, rows, 2 * count)
    metric = spread(joint[rows:], 1, rows, 2 * count)
    row = lax.broadcasted_iota(jnp.int32, (8, 2 * count), 0)
    total = jnp.zeros((8, 2 * count), jnp.float32)
    for j in range(rows):
        for b in energy[j]:
            unit = jnp.where(row == j % 8, 2.0, 0.0) if b == j // 8 else 0.0
            term = energy[j][b] * (unit - metric[j][b])
            total = total + (term if b == j // 8 else term + term)
    damping = 0.1 * jnp.sum(total, axis=0, keepdims=True) / rows + 1e-06 * scale
    columns = [{b: energy[j][b] + damping * metric[j][b] for b in energy[j]} for j in range(rows)]
    solved, _ = eliminate(columns, both)
    return solved[:, :count], solved[:, count:], enough


def combine_kernel(rows, leaf_ref, out_ref, gram_ref, change_ref):
    leaf = leaf_ref[...]
    gram_ref[...] = lax.dot_general(leaf, leaf, (((1,), (1,)), ((), ())), preferred_element_type=jnp.float32)
    own = pl.ds(pl.multiple_of(lax.axis_index("grp") * rows, rows), rows)

    def finish(often):
        projected, weights, enough = solve_small(gram_ref[...], rows, often)
        change_ref[...] = lax.dot_general(
            projected, weights, (((0,), (0,)), ((), ())), precision=HI, preferred_element_type=jnp.float32
        )
        change = change_ref[own, :]
        top = change.astype(jnp.bfloat16)
        rest = (change - top.astype(jnp.float32)).astype(jnp.bfloat16)
        moved = jnp.dot(jnp.concatenate([top, rest], axis=0), leaf_ref[...], preferred_element_type=jnp.float32)
        out_ref[0] = leaf_ref[own, :].astype(jnp.float32) - (moved[:rows] + moved[rows:])
        return enough

    enough = finish(False)

    @pl.when(jnp.logical_not(enough))
    def _():
        finish(True)


def features_kernel(lengths_ref, order_ref, tokens_ref, out_ref, grads_ref, held_ref):
    examples, depth, full = tokens_ref.shape
    groups, modules, pairs, _ = out_ref.shape
    half = full // 2
    chunks = pairs // examples
    position = lax.broadcasted_iota(jnp.int32, (chunks, depth), 1)
    module = lax.rem(position, modules)
    lane = lax.broadcasted_iota(jnp.int32, (depth, full), 1)
    for e in range(examples):
        block = tokens_ref[e].astype(jnp.float32)
        left = jnp.where(lane < half, block, 0.0).astype(jnp.bfloat16)
        right = jnp.where(lane < half, 0.0, pltpu.roll(block, half, 1)).astype(jnp.bfloat16)
        grads = block.T[half:]
        for k in range(depth // full):
            grads_ref[k] = grads[:, k * full : (k + 1) * full]
        live = position < lengths_ref[e] * modules
        flat = jnp.zeros((modules * chunks, full), jnp.float32)
        for odd, side in ((0, left), (1, right)):
            every = pl.ds(odd, chunks, stride=2)
            grads = jnp.concatenate([grads_ref[k, every, :] for k in range(depth // full)], axis=1)
            grads = jnp.where(live, grads, 0.0)
            apiece = [jnp.where(module == q, grads, 0.0).astype(jnp.bfloat16) for q in range(modules)]
            flat = flat + jnp.dot(jnp.concatenate(apiece, axis=0), side, preferred_element_type=jnp.float32)
        held_ref[pl.ds(e, modules * chunks, stride=examples), :] = flat
    for slot in range(modules):
        first = pl.multiple_of(order_ref[slot] * pairs, pairs)
        message = held_ref[pl.ds(first, pairs), :].astype(jnp.bfloat16)
        for g in range(groups):
            out_ref[g, slot] = message


def gram_route(tokens, lengths, module_order):
    groups, owners = lax.axis_size("grp"), lax.axis_size("mod")
    own, slots, modules, full = tokens.shape
    width = (full // 2) ** 2
    rows = owners * own
    count = groups * rows
    chunks = width // full
    messages = pl.pallas_call(
        features_kernel,
        out_shape=jax.ShapeDtypeStruct((groups, modules, chunks * own, full), jnp.bfloat16),
        in_specs=[pl.BlockSpec(memory_space=space) for space in (pltpu.SMEM, pltpu.SMEM, pltpu.VMEM)],
        scratch_shapes=[
            pltpu.VMEM((slots * modules // full, full // 2, full), jnp.float32),
            pltpu.VMEM((modules * chunks * own, full), jnp.float32),
        ],
        compiler_params=pltpu.CompilerParams(vmem_limit_bytes=VMEM_BYTES),
    )(lengths, module_order, tokens.reshape(own, slots * modules, full))
    messages = messages.reshape(groups * modules, chunks, own, full).transpose(0, 2, 1, 3).reshape(groups * modules, own, width)
    leaf = lax.all_to_all(messages, ("grp", "mod"), split_axis=0, concat_axis=0, tiled=True)
    leaf = leaf.reshape(count, width)
    return pl.pallas_call(
        functools.partial(combine_kernel, rows),
        out_shape=jax.ShapeDtypeStruct((1, rows, width), jnp.float32),
        scratch_shapes=[pltpu.VMEM((count, count), jnp.float32)] * 2,
        compiler_params=pltpu.CompilerParams(vmem_limit_bytes=VMEM_BYTES),
    )(leaf)


def local_features(token_block, live_counts):
    example_count, token_slots, module_count, full_width = token_block.shape
    half_width = full_width // 2
    live_mask = jnp.arange(token_slots, dtype=jnp.int32)[None, :] < live_counts[:, None]
    grad_side = jnp.where(
        live_mask[:, :, None, None],
        token_block[:, :, :, half_width:],
        jnp.zeros((), token_block.dtype),
    )
    input_side = token_block[:, :, :, :half_width]
    outer = jnp.einsum("etmo,etmi->meoi", grad_side, input_side, preferred_element_type=jnp.float32)
    return outer.reshape(module_count, example_count, half_width * half_width).astype(jnp.bfloat16)


def per_device(tokens, lengths, module_order):
    groups, owners = lax.axis_size("grp"), lax.axis_size("mod")
    own, slots, modules, full = tokens.shape
    if groups == 4 and owners * own == 16 and owners == modules == 8 and full == 128:
        return gram_route(tokens, lengths, module_order)
    return sketch_tree(local_features(tokens, lengths), module_order)


def solution(mesh):
    return jax.shard_map(
        per_device,
        mesh=mesh,
        in_specs=(P(("grp", "mod"), None, None, None), P(("grp", "mod")), P()),
        out_specs=P("mod", "grp", None),
        check_vma=False,
    )
```

```python
import functools
import math

import jax
import jax.numpy as jnp
import numpy as np
from jax import lax
from jax.experimental import pallas as pl
from jax.experimental.pallas import tpu as pltpu
from jax.sharding import PartitionSpec as P

ITERS = 3
HI = lax.Precision.HIGHEST
VMEM_BYTES = 48 * 1024 * 1024


def partner(value, axis, bit):
    mask = 2**bit
    return xor_send(value, axis, mask)


def xor_send(value, axis, mask):
    pairs = [(source, source ^ mask) for source in range(lax.axis_size(axis))]
    return lax.ppermute(value, axis, pairs)


def start_basis(row_count, col_count):
    row_index = np.arange(row_count, dtype=np.float64)[:, None] + 0.5
    col_index = np.arange(col_count, dtype=np.float64)[None, :] + 0.5
    return np.cos(np.pi * row_index * col_index / row_count).astype(np.float32)


def orthonormal(matrix):
    for repeat in range(2):
        cross_gram = jnp.dot(matrix.T, matrix, precision=HI)
        factor = jnp.linalg.cholesky(cross_gram)
        matrix = jax.scipy.linalg.solve_triangular(factor, matrix.T, lower=True).T
    return matrix


def merge_pair(lower_sketch, upper_sketch):
    stacked = jnp.concatenate([lower_sketch, upper_sketch], axis=0)
    kernel = jnp.dot(stacked, stacked.T, precision=HI)
    current = start_basis(stacked.shape[0], lower_sketch.shape[0])
    for repeat in range(ITERS):
        current = orthonormal(jnp.dot(kernel, current, precision=HI))
    return jnp.dot(current.T, stacked, precision=HI)


def precondition(group_rows, sketch):
    sketch_rows = sketch.shape[0]
    damping = 0.1 * jnp.sum(sketch * sketch) / sketch_rows + 1e-06
    capacitance = jnp.dot(sketch, sketch.T, precision=HI) + damping * jnp.eye(sketch_rows, dtype=jnp.float32)
    projected = jnp.dot(group_rows, sketch.T, precision=HI)
    factor = jnp.linalg.cholesky(capacitance)
    middle = jax.scipy.linalg.solve_triangular(factor, projected.T, lower=True)
    weights = jax.scipy.linalg.solve_triangular(factor, middle, lower=True, trans=1).T
    return group_rows - jnp.dot(weights, sketch, precision=HI)


def sketch_tree(features, module_order):
    ordered = jnp.take(features, module_order, axis=0)
    group_rows = lax.all_to_all(ordered, "mod", split_axis=0, concat_axis=1, tiled=True)
    leaves = group_rows.astype(jnp.float32)
    merge_all = jax.vmap(merge_pair)
    levels = lax.axis_size("grp").bit_length() - 1
    position = lax.axis_index("grp")
    sketch = leaves
    for height in range(levels):
        sister = partner(sketch, "grp", height)
        upper_side = position // 2**height % 2 == 1
        lower_part = jnp.where(upper_side, sister, sketch)
        upper_part = jnp.where(upper_side, sketch, sister)
        sketch = merge_all(lower_part, upper_part)
    return jax.vmap(precondition)(leaves, sketch)


def dot_nt(a, b):
    return lax.dot_general(a, b, (((1,), (1,)), ((), ())), precision=HI, preferred_element_type=jnp.float32)


def dot_nn(a, b):
    return jnp.dot(a, b, precision=HI, preferred_element_type=jnp.float32)


def start_rows(count, width, span):
    j = lax.broadcasted_iota(jnp.int32, (count, width), 0)
    i = lax.rem(lax.broadcasted_iota(jnp.int32, (count, width), 1), span)
    turn = lax.rem((2 * i + 1) * (2 * j + 1), 8 * span)
    folded = jnp.minimum(turn, 8 * span - turn)
    angle = (2 * span - folded).astype(jnp.float32) * (math.pi / (4 * span))
    square = angle * angle
    series = jnp.full_like(angle, 1.0)
    for n in range(12, 0, -2):
        series = 1.0 - square * series * (1.0 / (n * (n + 1)))
    return angle * series


def spread(gram, problems, count, width):
    lane = lax.broadcasted_iota(jnp.int32, (8, width), 1)
    columns = []
    for j in range(count):
        blocks = {}
        for b in range(j // 8, count // 8):
            parts = [
                jnp.broadcast_to(gram[8 * b : 8 * b + 8, k * count + j : k * count + j + 1], (8, width))
                for k in range(problems)
            ]
            blocks[b] = parts[0] if problems == 1 else jnp.where(lane < width // 2, parts[0], parts[1])
        columns.append(blocks)
    return columns


def eliminate(columns, rhs):
    count = len(columns)
    width = rhs.shape[1]
    parts = [rhs[8 * b : 8 * b + 8] for b in range(count // 8)]
    row = lax.broadcasted_iota(jnp.int32, (8, width), 0)
    diag = [jnp.ones((8, width), jnp.float32) for _ in parts]
    whole = [functools.reduce(lambda x, j: jnp.where(row == j, columns[8 * k + j][k], x), range(8), d) for k, d in enumerate(diag)]
    for p in range(0, count, 2):
        home, at = divmod(p, 8)
        left, right = columns[p], columns[p + 1]
        a = left[home][at : at + 1]
        b = left[home][at + 1 : at + 2]
        c = right[home][at + 1 : at + 2]
        det = a * c - b * b
        ratio = b / a
        diag[home] = jnp.where(row == at, a, jnp.where(row == at + 1, c - b * ratio, diag[home]))
        inverse = 1.0 / det
        ia, ib, ic = c * inverse, b * inverse, a * inverse
        low, high = {}, {}
        for k in left:
            low[k] = left[k] * ia - right[k] * ib
            high[k] = right[k] * ic - left[k] * ib
        for j in range(p + 2, count):
            one = left[j // 8][j % 8 : j % 8 + 1]
            two = right[j // 8][j % 8 : j % 8 + 1]
            columns[j] = {k: block - (low[k] * one + high[k] * two) for k, block in columns[j].items()}
        low[home] = jnp.where(row > at + 1, low[home], jnp.where(row == at + 1, ratio, 0.0))
        high[home] = jnp.where(row > at + 1, high[home], 0.0)
        first, second = parts[home][at : at + 1], parts[home][at + 1 : at + 2]
        for k in low:
            parts[k] = parts[k] - (low[k] * first + high[k] * second)
    worst = functools.reduce(jnp.minimum, [d / w for d, w in zip(diag, whole)])
    return jnp.concatenate([part * lax.rsqrt(d) for part, d in zip(parts, diag)], axis=0), worst


def apart(value):
    lane = lax.broadcasted_iota(jnp.int32, value.shape, 1)
    near = lane < value.shape[1] // 2
    return jnp.concatenate([jnp.where(near, value, 0.0), jnp.where(near, 0.0, value)], axis=0)


def solve_small(gram, rows, often):
    count = gram.shape[0]
    half = count // 2
    r = lax.broadcasted_iota(jnp.int32, gram.shape, 0)
    c = lax.broadcasted_iota(jnp.int32, gram.shape, 1)
    lane = lax.broadcasted_iota(jnp.int32, (1, count), 1)
    diagonal = jnp.sum(jnp.where(r == c, gram, 0.0), axis=0, keepdims=True)
    trace_lower = jnp.sum(jnp.where(lane < half, diagonal, 0.0), axis=1, keepdims=True)
    trace_upper = jnp.sum(jnp.where(lane < half, 0.0, diagonal), axis=1, keepdims=True)
    scale = 1.0 / (trace_lower + trace_upper)
    pair_scale = 1.0 / jnp.where(lane < half, trace_lower, trace_upper)
    own_pair = jnp.where((r < half) == (c < half), gram, 0.0)

    moved = dot_nn(start_rows(rows, count, half), own_pair) * pair_scale
    own_pair = own_pair * pair_scale
    smallest = []
    if not often:
        moved = dot_nn(moved, own_pair)
    for onward_too in (True, True, False, False) if often else (True, False):
        inner = dot_nt(moved, apart(moved))
        onward = dot_nn(moved, own_pair) if onward_too else moved
        moved, worst = eliminate(spread(inner, 2, rows, count), onward)
        smallest.append(jnp.min(worst))
    basis = apart(moved)

    gram = gram * scale
    reached = dot_nn(basis, gram)
    kernel = dot_nt(reached, basis)
    moved = dot_nn(start_rows(rows, half, half), kernel)
    if often:
        for onward_too in (True, True, False):
            inner = dot_nt(moved, moved)
            onward = dot_nn(moved, kernel) if onward_too else moved
            moved, _ = eliminate(spread(inner, 1, rows, half), onward)
    else:
        moved = dot_nn(moved, dot_nn(kernel, kernel))
    inner = dot_nt(moved, moved)
    onward = dot_nn(moved, jnp.concatenate([reached, basis], axis=1))
    both, worst = eliminate(spread(inner, 1, rows, 2 * count), onward)
    smallest.append(jnp.min(worst))
    enough = jnp.logical_and(jnp.logical_and(smallest[0] > 1e-4, smallest[1] > 1e-2), smallest[-1] > 3e-4)

    weights = both[:, count:]
    row = lax.broadcasted_iota(jnp.int32, (8, 2 * count), 0)
    joint = dot_nt(jnp.concatenate([both[:, :count], weights], axis=0), weights)
    energy = spread(joint[:rows], 1, rows, 2 * count)
    metric = spread(joint[rows:], 1, rows, 2 * count)
    total = jnp.zeros((8, 2 * count), jnp.float32)
    for j in range(rows):
        for b in energy[j]:
            unit = jnp.where(row == j % 8, 2.0, 0.0) if b == j // 8 else 0.0
            term = energy[j][b] * (unit - metric[j][b])
            total = total + (term if b == j // 8 else term + term)
    total = jnp.sum(total, axis=0, keepdims=True)
    damping = 0.1 * total / rows + 1e-06 * scale
    columns = [{b: energy[j][b] + damping * metric[j][b] for b in energy[j]} for j in range(rows)]
    solved, _ = eliminate(columns, both)
    return solved[:, :count], solved[:, count:], enough


def combine_kernel(rows, leaf_ref, out_ref, gram_ref, change_ref):
    leaf = leaf_ref[...]
    gram_ref[...] = lax.dot_general(leaf, leaf, (((1,), (1,)), ((), ())), preferred_element_type=jnp.float32)
    own = pl.ds(pl.multiple_of(lax.axis_index("grp") * rows, rows), rows)

    def finish(often):
        projected, weights, enough = solve_small(gram_ref[...], rows, often)
        change_ref[...] = lax.dot_general(
            projected, weights, (((0,), (0,)), ((), ())), precision=HI, preferred_element_type=jnp.float32
        )
        change = change_ref[own, :]
        top = change.astype(jnp.bfloat16)
        rest = (change - top.astype(jnp.float32)).astype(jnp.bfloat16)
        moved = jnp.dot(jnp.concatenate([top, rest], axis=0), leaf_ref[...], preferred_element_type=jnp.float32)
        out_ref[0] = leaf_ref[own, :].astype(jnp.float32) - (moved[:rows] + moved[rows:])
        return enough

    enough = finish(False)

    @pl.when(jnp.logical_not(enough))
    def _():
        finish(True)


def features_kernel(lengths_ref, order_ref, tokens_ref, out_ref, grads_ref, held_ref):
    examples, depth, full = tokens_ref.shape
    groups, modules, pairs, _ = out_ref.shape
    half = full // 2
    chunks = pairs // examples
    position = lax.broadcasted_iota(jnp.int32, (chunks, depth), 1)
    module = lax.rem(position, modules)
    lane = lax.broadcasted_iota(jnp.int32, (depth, full), 1)
    for e in range(examples):
        block = tokens_ref[e].astype(jnp.float32)
        left = jnp.where(lane < half, block, 0.0).astype(jnp.bfloat16)
        right = jnp.where(lane < half, 0.0, pltpu.roll(block, half, 1)).astype(jnp.bfloat16)
        grads = block.T[half:]
        for k in range(depth // full):
            grads_ref[k] = grads[:, k * full : (k + 1) * full]
        live = position < lengths_ref[e] * modules
        flat = jnp.zeros((modules * chunks, full), jnp.float32)
        for odd, side in ((0, left), (1, right)):
            every = pl.ds(odd, chunks, stride=2)
            grads = jnp.concatenate([grads_ref[k, every, :] for k in range(depth // full)], axis=1)
            grads = jnp.where(live, grads, 0.0)
            apiece = [jnp.where(module == q, grads, 0.0).astype(jnp.bfloat16) for q in range(modules)]
            flat = flat + jnp.dot(jnp.concatenate(apiece, axis=0), side, preferred_element_type=jnp.float32)
        held_ref[pl.ds(e, modules * chunks, stride=examples), :] = flat
    for slot in range(modules):
        first = pl.multiple_of(order_ref[slot] * pairs, pairs)
        message = held_ref[pl.ds(first, pairs), :].astype(jnp.bfloat16)
        for g in range(groups):
            out_ref[g, slot] = message


def gram_route(tokens, lengths, module_order):
    groups, owners = lax.axis_size("grp"), lax.axis_size("mod")
    own, slots, modules, full = tokens.shape
    width = (full // 2) ** 2
    rows = owners * own
    count = groups * rows
    chunks = width // full
    messages = pl.pallas_call(
        features_kernel,
        out_shape=jax.ShapeDtypeStruct((groups, modules, chunks * own, full), jnp.bfloat16),
        in_specs=[pl.BlockSpec(memory_space=space) for space in (pltpu.SMEM, pltpu.SMEM, pltpu.VMEM)],
        scratch_shapes=[
            pltpu.VMEM((slots * modules // full, full // 2, full), jnp.float32),
            pltpu.VMEM((modules * chunks * own, full), jnp.float32),
        ],
        compiler_params=pltpu.CompilerParams(vmem_limit_bytes=VMEM_BYTES),
    )(lengths, module_order, tokens.reshape(own, slots * modules, full))
    messages = messages.reshape(groups * modules, chunks, own, full).transpose(0, 2, 1, 3).reshape(groups * modules, own, width)
    leaf = lax.all_to_all(messages, ("grp", "mod"), split_axis=0, concat_axis=0, tiled=True)
    leaf = leaf.reshape(count, width)
    return pl.pallas_call(
        functools.partial(combine_kernel, rows),
        out_shape=jax.ShapeDtypeStruct((1, rows, width), jnp.float32),
        scratch_shapes=[pltpu.VMEM((count, count), jnp.float32)] * 2,
        compiler_params=pltpu.CompilerParams(vmem_limit_bytes=VMEM_BYTES),
    )(leaf)


def local_features(token_block, live_counts):
    example_count, token_slots, module_count, full_width = token_block.shape
    half_width = full_width // 2
    live_mask = jnp.arange(token_slots, dtype=jnp.int32)[None, :] < live_counts[:, None]
    grad_side = jnp.where(
        live_mask[:, :, None, None],
        token_block[:, :, :, half_width:],
        jnp.zeros((), token_block.dtype),
    )
    input_side = token_block[:, :, :, :half_width]
    outer = jnp.einsum("etmo,etmi->meoi", grad_side, input_side, preferred_element_type=jnp.float32)
    return outer.reshape(module_count, example_count, half_width * half_width).astype(jnp.bfloat16)


def per_device(tokens, lengths, module_order):
    groups, owners = lax.axis_size("grp"), lax.axis_size("mod")
    own, slots, modules, full = tokens.shape
    if groups == 4 and owners * own == 16 and owners == modules == 8 and full == 128:
        return gram_route(tokens, lengths, module_order)
    return sketch_tree(local_features(tokens, lengths), module_order)


def solution(mesh):
    return jax.shard_map(
        per_device,
        mesh=mesh,
        in_specs=(P(("grp", "mod"), None, None, None), P(("grp", "mod")), P()),
        out_specs=P("mod", "grp", None),
        check_vma=False,
    )
```

```python
import functools
import math

import jax
import jax.numpy as jnp
import numpy as np
from jax import lax
from jax.experimental import pallas as pl
from jax.experimental.pallas import tpu as pltpu
from jax.sharding import PartitionSpec as P

ITERS = 3
HI = lax.Precision.HIGHEST
VMEM_BYTES = 48 * 1024 * 1024


def partner(value, axis, bit):
    mask = 2**bit
    return xor_send(value, axis, mask)


def xor_send(value, axis, mask):
    pairs = [(source, source ^ mask) for source in range(lax.axis_size(axis))]
    return lax.ppermute(value, axis, pairs)


def start_basis(row_count, col_count):
    row_index = np.arange(row_count, dtype=np.float64)[:, None] + 0.5
    col_index = np.arange(col_count, dtype=np.float64)[None, :] + 0.5
    return np.cos(np.pi * row_index * col_index / row_count).astype(np.float32)


def orthonormal(matrix):
    for repeat in range(2):
        cross_gram = jnp.dot(matrix.T, matrix, precision=HI)
        factor = jnp.linalg.cholesky(cross_gram)
        matrix = jax.scipy.linalg.solve_triangular(factor, matrix.T, lower=True).T
    return matrix


def merge_pair(lower_sketch, upper_sketch):
    stacked = jnp.concatenate([lower_sketch, upper_sketch], axis=0)
    kernel = jnp.dot(stacked, stacked.T, precision=HI)
    current = start_basis(stacked.shape[0], lower_sketch.shape[0])
    for repeat in range(ITERS):
        current = orthonormal(jnp.dot(kernel, current, precision=HI))
    return jnp.dot(current.T, stacked, precision=HI)


def precondition(group_rows, sketch):
    sketch_rows = sketch.shape[0]
    damping = 0.1 * jnp.sum(sketch * sketch) / sketch_rows + 1e-06
    capacitance = jnp.dot(sketch, sketch.T, precision=HI) + damping * jnp.eye(sketch_rows, dtype=jnp.float32)
    projected = jnp.dot(group_rows, sketch.T, precision=HI)
    factor = jnp.linalg.cholesky(capacitance)
    middle = jax.scipy.linalg.solve_triangular(factor, projected.T, lower=True)
    weights = jax.scipy.linalg.solve_triangular(factor, middle, lower=True, trans=1).T
    return group_rows - jnp.dot(weights, sketch, precision=HI)


def sketch_tree(features, module_order):
    ordered = jnp.take(features, module_order, axis=0)
    group_rows = lax.all_to_all(ordered, "mod", split_axis=0, concat_axis=1, tiled=True)
    leaves = group_rows.astype(jnp.float32)
    merge_all = jax.vmap(merge_pair)
    levels = lax.axis_size("grp").bit_length() - 1
    position = lax.axis_index("grp")
    sketch = leaves
    for height in range(levels):
        sister = partner(sketch, "grp", height)
        upper_side = position // 2**height % 2 == 1
        lower_part = jnp.where(upper_side, sister, sketch)
        upper_part = jnp.where(upper_side, sketch, sister)
        sketch = merge_all(lower_part, upper_part)
    return jax.vmap(precondition)(leaves, sketch)


def terms(value):
    first = value.astype(jnp.bfloat16)
    left = value - first.astype(jnp.float32)
    second = left.astype(jnp.bfloat16)
    third = (left - second.astype(jnp.float32)).astype(jnp.bfloat16)
    return first, second, third


def small_dot(a, b, b_side):
    rows = a.shape[0]
    stacked = jnp.concatenate(terms(a), axis=0)
    products = []
    for k, term in enumerate(terms(b)):
        products.append(
            lax.dot_general(
                stacked[: (3 - k) * rows], term, (((1,), (b_side,)), ((), ())), preferred_element_type=jnp.float32
            )
        )
    large, middle, small = products
    least = large[2 * rows :] + middle[rows:] + small
    return large[:rows] + ((large[rows : 2 * rows] + middle[:rows]) + least)


def dot_nt(a, b):
    return small_dot(a, b, 1)


def dot_nn(a, b):
    return small_dot(a, b, 0)


def start_rows(count, width, span):
    j = lax.broadcasted_iota(jnp.int32, (count, width), 0)
    i = lax.rem(lax.broadcasted_iota(jnp.int32, (count, width), 1), span)
    turn = lax.rem((2 * i + 1) * (2 * j + 1), 8 * span)
    folded = jnp.minimum(turn, 8 * span - turn)
    angle = (2 * span - folded).astype(jnp.float32) * (math.pi / (4 * span))
    square = angle * angle
    series = jnp.full_like(angle, 1.0)
    for n in range(12, 0, -2):
        series = 1.0 - square * series * (1.0 / (n * (n + 1)))
    return angle * series


def spread(gram, problems, count, width):
    lane = lax.broadcasted_iota(jnp.int32, (8, width), 1)
    columns = []
    for j in range(count):
        blocks = {}
        for b in range(j // 8, count // 8):
            parts = [
                jnp.broadcast_to(gram[8 * b : 8 * b + 8, k * count + j : k * count + j + 1], (8, width))
                for k in range(problems)
            ]
            blocks[b] = parts[0] if problems == 1 else jnp.where(lane < width // 2, parts[0], parts[1])
        columns.append(blocks)
    return columns


def eliminate(columns, rhs):
    count = len(columns)
    width = rhs.shape[1]
    parts = [rhs[8 * b : 8 * b + 8] for b in range(count // 8)]
    row = lax.broadcasted_iota(jnp.int32, (8, width), 0)
    diag = [jnp.ones((8, width), jnp.float32) for _ in parts]
    whole = [functools.reduce(lambda x, j: jnp.where(row == j, columns[8 * k + j][k], x), range(8), d) for k, d in enumerate(diag)]
    for p in range(0, count, 2):
        home, at = divmod(p, 8)
        left, right = columns[p], columns[p + 1]
        a = left[home][at : at + 1]
        b = left[home][at + 1 : at + 2]
        c = right[home][at + 1 : at + 2]
        det = a * c - b * b
        ratio = b / a
        diag[home] = jnp.where(row == at, a, jnp.where(row == at + 1, c - b * ratio, diag[home]))
        inverse = 1.0 / det
        ia, ib, ic = c * inverse, b * inverse, a * inverse
        low, high = {}, {}
        for k in left:
            low[k] = left[k] * ia - right[k] * ib
            high[k] = right[k] * ic - left[k] * ib
        for j in range(p + 2, count):
            one = left[j // 8][j % 8 : j % 8 + 1]
            two = right[j // 8][j % 8 : j % 8 + 1]
            columns[j] = {k: block - (low[k] * one + high[k] * two) for k, block in columns[j].items()}
        low[home] = jnp.where(row > at + 1, low[home], jnp.where(row == at + 1, ratio, 0.0))
        high[home] = jnp.where(row > at + 1, high[home], 0.0)
        first, second = parts[home][at : at + 1], parts[home][at + 1 : at + 2]
        for k in low:
            parts[k] = parts[k] - (low[k] * first + high[k] * second)
    worst = functools.reduce(jnp.minimum, [d / w for d, w in zip(diag, whole)])
    return jnp.concatenate([part * lax.rsqrt(d) for part, d in zip(parts, diag)], axis=0), worst


def apart(value):
    lane = lax.broadcasted_iota(jnp.int32, value.shape, 1)
    near = lane < value.shape[1] // 2
    return jnp.concatenate([jnp.where(near, value, 0.0), jnp.where(near, 0.0, value)], axis=0)


def solve_small(gram, rows, often):
    count = gram.shape[0]
    half = count // 2
    r = lax.broadcasted_iota(jnp.int32, gram.shape, 0)
    c = lax.broadcasted_iota(jnp.int32, gram.shape, 1)
    lane = lax.broadcasted_iota(jnp.int32, (1, count), 1)
    diagonal = jnp.sum(jnp.where(r == c, gram, 0.0), axis=0, keepdims=True)
    trace_lower = jnp.sum(jnp.where(lane < half, diagonal, 0.0), axis=1, keepdims=True)
    trace_upper = jnp.sum(jnp.where(lane < half, 0.0, diagonal), axis=1, keepdims=True)
    scale = 1.0 / (trace_lower + trace_upper)
    pair_scale = 1.0 / jnp.where(lane < half, trace_lower, trace_upper)
    own_pair = jnp.where((r < half) == (c < half), gram, 0.0)

    moved = dot_nn(start_rows(rows, count, half), own_pair) * pair_scale
    own_pair = own_pair * pair_scale
    smallest = []
    if not often:
        moved = dot_nn(moved, own_pair)
    for onward_too in (True, True, False, False) if often else (True, False):
        inner = dot_nt(moved, apart(moved))
        onward = dot_nn(moved, own_pair) if onward_too else moved
        moved, worst = eliminate(spread(inner, 2, rows, count), onward)
        smallest.append(jnp.min(worst))
    basis = apart(moved)

    gram = gram * scale
    reached = dot_nn(basis, gram)
    kernel = dot_nt(reached, basis)
    moved = dot_nn(start_rows(rows, half, half), kernel)
    if often:
        for onward_too in (True, True, False):
            inner = dot_nt(moved, moved)
            onward = dot_nn(moved, kernel) if onward_too else moved
            moved, _ = eliminate(spread(inner, 1, rows, half), onward)
    else:
        moved = dot_nn(moved, dot_nn(kernel, kernel))
    inner = dot_nt(moved, moved)
    onward = dot_nn(moved, jnp.concatenate([reached, basis], axis=1))
    both, worst = eliminate(spread(inner, 1, rows, 2 * count), onward)
    smallest.append(jnp.min(worst))
    enough = jnp.logical_and(jnp.logical_and(smallest[0] > 1e-4, smallest[1] > 1e-2), smallest[-1] > 3e-4)

    weights = both[:, count:]
    row = lax.broadcasted_iota(jnp.int32, (8, 2 * count), 0)
    joint = dot_nt(jnp.concatenate([both[:, :count], weights], axis=0), weights)
    energy = spread(joint[:rows], 1, rows, 2 * count)
    metric = spread(joint[rows:], 1, rows, 2 * count)
    total = jnp.zeros((8, 2 * count), jnp.float32)
    for j in range(rows):
        for b in energy[j]:
            unit = jnp.where(row == j % 8, 2.0, 0.0) if b == j // 8 else 0.0
            term = energy[j][b] * (unit - metric[j][b])
            total = total + (term if b == j // 8 else term + term)
    total = jnp.sum(total, axis=0, keepdims=True)
    damping = 0.1 * total / rows + 1e-06 * scale
    columns = [{b: energy[j][b] + damping * metric[j][b] for b in energy[j]} for j in range(rows)]
    solved, _ = eliminate(columns, both)
    return solved[:, :count], solved[:, count:], enough


def combine_kernel(rows, leaf_ref, out_ref, gram_ref, change_ref):
    leaf = leaf_ref[...]
    gram_ref[...] = lax.dot_general(leaf, leaf, (((1,), (1,)), ((), ())), preferred_element_type=jnp.float32)
    own = pl.ds(pl.multiple_of(lax.axis_index("grp") * rows, rows), rows)

    def finish(often):
        projected, weights, enough = solve_small(gram_ref[...], rows, often)
        change_ref[...] = lax.dot_general(
            projected, weights, (((0,), (0,)), ((), ())), precision=HI, preferred_element_type=jnp.float32
        )
        change = change_ref[own, :]
        top = change.astype(jnp.bfloat16)
        rest = (change - top.astype(jnp.float32)).astype(jnp.bfloat16)
        moved = jnp.dot(jnp.concatenate([top, rest], axis=0), leaf_ref[...], preferred_element_type=jnp.float32)
        out_ref[0] = leaf_ref[own, :].astype(jnp.float32) - (moved[:rows] + moved[rows:])
        return enough

    enough = finish(False)

    @pl.when(jnp.logical_not(enough))
    def _():
        finish(True)


def features_kernel(lengths_ref, order_ref, tokens_ref, out_ref, grads_ref, held_ref):
    examples, depth, full = tokens_ref.shape
    groups, modules, pairs, _ = out_ref.shape
    half = full // 2
    chunks = pairs // examples
    position = lax.broadcasted_iota(jnp.int32, (chunks, depth), 1)
    module = lax.rem(position, modules)
    lane = lax.broadcasted_iota(jnp.int32, (depth, full), 1)
    for e in range(examples):
        block = tokens_ref[e].astype(jnp.float32)
        left = jnp.where(lane < half, block, 0.0).astype(jnp.bfloat16)
        right = jnp.where(lane < half, 0.0, pltpu.roll(block, half, 1)).astype(jnp.bfloat16)
        grads = block.T[half:]
        for k in range(depth // full):
            grads_ref[k] = grads[:, k * full : (k + 1) * full]
        live = position < lengths_ref[e] * modules
        flat = jnp.zeros((modules * chunks, full), jnp.float32)
        for odd, side in ((0, left), (1, right)):
            every = pl.ds(odd, chunks, stride=2)
            grads = jnp.concatenate([grads_ref[k, every, :] for k in range(depth // full)], axis=1)
            grads = jnp.where(live, grads, 0.0)
            apiece = [jnp.where(module == q, grads, 0.0).astype(jnp.bfloat16) for q in range(modules)]
            flat = flat + jnp.dot(jnp.concatenate(apiece, axis=0), side, preferred_element_type=jnp.float32)
        held_ref[pl.ds(e, modules * chunks, stride=examples), :] = flat
    for slot in range(modules):
        first = pl.multiple_of(order_ref[slot] * pairs, pairs)
        message = held_ref[pl.ds(first, pairs), :].astype(jnp.bfloat16)
        for g in range(groups):
            out_ref[g, slot] = message


def gram_route(tokens, lengths, module_order):
    groups, owners = lax.axis_size("grp"), lax.axis_size("mod")
    own, slots, modules, full = tokens.shape
    width = (full // 2) ** 2
    rows = owners * own
    count = groups * rows
    chunks = width // full
    messages = pl.pallas_call(
        features_kernel,
        out_shape=jax.ShapeDtypeStruct((groups, modules, chunks * own, full), jnp.bfloat16),
        in_specs=[pl.BlockSpec(memory_space=space) for space in (pltpu.SMEM, pltpu.SMEM, pltpu.VMEM)],
        scratch_shapes=[
            pltpu.VMEM((slots * modules // full, full // 2, full), jnp.float32),
            pltpu.VMEM((modules * chunks * own, full), jnp.float32),
        ],
        compiler_params=pltpu.CompilerParams(vmem_limit_bytes=VMEM_BYTES),
    )(lengths, module_order, tokens.reshape(own, slots * modules, full))
    messages = messages.reshape(groups * modules, chunks, own, full).transpose(0, 2, 1, 3).reshape(groups * modules, own, width)
    leaf = lax.all_to_all(messages, ("grp", "mod"), split_axis=0, concat_axis=0, tiled=True)
    leaf = leaf.reshape(count, width)
    return pl.pallas_call(
        functools.partial(combine_kernel, rows),
        out_shape=jax.ShapeDtypeStruct((1, rows, width), jnp.float32),
        scratch_shapes=[pltpu.VMEM((count, count), jnp.float32)] * 2,
        compiler_params=pltpu.CompilerParams(vmem_limit_bytes=VMEM_BYTES),
    )(leaf)


def local_features(token_block, live_counts):
    example_count, token_slots, module_count, full_width = token_block.shape
    half_width = full_width // 2
    live_mask = jnp.arange(token_slots, dtype=jnp.int32)[None, :] < live_counts[:, None]
    grad_side = jnp.where(
        live_mask[:, :, None, None],
        token_block[:, :, :, half_width:],
        jnp.zeros((), token_block.dtype),
    )
    input_side = token_block[:, :, :, :half_width]
    outer = jnp.einsum("etmo,etmi->meoi", grad_side, input_side, preferred_element_type=jnp.float32)
    return outer.reshape(module_count, example_count, half_width * half_width).astype(jnp.bfloat16)


def per_device(tokens, lengths, module_order):
    groups, owners = lax.axis_size("grp"), lax.axis_size("mod")
    own, slots, modules, full = tokens.shape
    if groups == 4 and owners * own == 16 and owners == modules == 8 and full == 128:
        return gram_route(tokens, lengths, module_order)
    return sketch_tree(local_features(tokens, lengths), module_order)


def solution(mesh):
    return jax.shard_map(
        per_device,
        mesh=mesh,
        in_specs=(P(("grp", "mod"), None, None, None), P(("grp", "mod")), P()),
        out_specs=P("mod", "grp", None),
        check_vma=False,
    )
```

```python
import functools
import math

import jax
import jax.numpy as jnp
import numpy as np
from jax import lax
from jax.experimental import pallas as pl
from jax.experimental.pallas import tpu as pltpu
from jax.sharding import PartitionSpec as P

ITERS = 3
HI = lax.Precision.HIGHEST
VMEM_BYTES = 48 * 1024 * 1024


def partner(value, axis, bit):
    mask = 2**bit
    return xor_send(value, axis, mask)


def xor_send(value, axis, mask):
    pairs = [(source, source ^ mask) for source in range(lax.axis_size(axis))]
    return lax.ppermute(value, axis, pairs)


def start_basis(row_count, col_count):
    row_index = np.arange(row_count, dtype=np.float64)[:, None] + 0.5
    col_index = np.arange(col_count, dtype=np.float64)[None, :] + 0.5
    return np.cos(np.pi * row_index * col_index / row_count).astype(np.float32)


def orthonormal(matrix):
    for repeat in range(2):
        cross_gram = jnp.dot(matrix.T, matrix, precision=HI)
        factor = jnp.linalg.cholesky(cross_gram)
        matrix = jax.scipy.linalg.solve_triangular(factor, matrix.T, lower=True).T
    return matrix


def merge_pair(lower_sketch, upper_sketch):
    stacked = jnp.concatenate([lower_sketch, upper_sketch], axis=0)
    kernel = jnp.dot(stacked, stacked.T, precision=HI)
    current = start_basis(stacked.shape[0], lower_sketch.shape[0])
    for repeat in range(ITERS):
        current = orthonormal(jnp.dot(kernel, current, precision=HI))
    return jnp.dot(current.T, stacked, precision=HI)


def precondition(group_rows, sketch):
    sketch_rows = sketch.shape[0]
    damping = 0.1 * jnp.sum(sketch * sketch) / sketch_rows + 1e-06
    capacitance = jnp.dot(sketch, sketch.T, precision=HI) + damping * jnp.eye(sketch_rows, dtype=jnp.float32)
    projected = jnp.dot(group_rows, sketch.T, precision=HI)
    factor = jnp.linalg.cholesky(capacitance)
    middle = jax.scipy.linalg.solve_triangular(factor, projected.T, lower=True)
    weights = jax.scipy.linalg.solve_triangular(factor, middle, lower=True, trans=1).T
    return group_rows - jnp.dot(weights, sketch, precision=HI)


def sketch_tree(features, module_order):
    ordered = jnp.take(features, module_order, axis=0)
    group_rows = lax.all_to_all(ordered, "mod", split_axis=0, concat_axis=1, tiled=True)
    leaves = group_rows.astype(jnp.float32)
    merge_all = jax.vmap(merge_pair)
    levels = lax.axis_size("grp").bit_length() - 1
    position = lax.axis_index("grp")
    sketch = leaves
    for height in range(levels):
        sister = partner(sketch, "grp", height)
        upper_side = position // 2**height % 2 == 1
        lower_part = jnp.where(upper_side, sister, sketch)
        upper_part = jnp.where(upper_side, sketch, sister)
        sketch = merge_all(lower_part, upper_part)
    return jax.vmap(precondition)(leaves, sketch)


def dot_nt(a, b):
    return lax.dot_general(a, b, (((1,), (1,)), ((), ())), precision=HI, preferred_element_type=jnp.float32)


def dot_nn(a, b):
    return jnp.dot(a, b, precision=HI, preferred_element_type=jnp.float32)


def start_rows(count, width, span):
    j = lax.broadcasted_iota(jnp.int32, (count, width), 0)
    i = lax.rem(lax.broadcasted_iota(jnp.int32, (count, width), 1), span)
    turn = lax.rem((2 * i + 1) * (2 * j + 1), 8 * span)
    folded = jnp.minimum(turn, 8 * span - turn)
    angle = (2 * span - folded).astype(jnp.float32) * (math.pi / (4 * span))
    square = angle * angle
    series = jnp.full_like(angle, 1.0)
    for n in range(12, 0, -2):
        series = 1.0 - square * series * (1.0 / (n * (n + 1)))
    return angle * series


def spread(gram, problems, count, width):
    lane = lax.broadcasted_iota(jnp.int32, (8, width), 1)
    columns = []
    for j in range(count):
        blocks = {}
        for b in range(j // 8, count // 8):
            parts = [
                jnp.broadcast_to(gram[8 * b : 8 * b + 8, k * count + j : k * count + j + 1], (8, width))
                for k in range(problems)
            ]
            blocks[b] = parts[0] if problems == 1 else jnp.where(lane < width // 2, parts[0], parts[1])
        columns.append(blocks)
    return columns


def reciprocal(value):
    guess = pl.reciprocal(value, approx=True)
    return guess * (2.0 - value * guess)


def eliminate(columns, rhs):
    count = len(columns)
    width = rhs.shape[1]
    parts = [rhs[8 * b : 8 * b + 8] for b in range(count // 8)]
    row = lax.broadcasted_iota(jnp.int32, (8, width), 0)
    diag = [jnp.ones((8, width), jnp.float32) for _ in parts]
    whole = [functools.reduce(lambda x, j: jnp.where(row == j, columns[8 * k + j][k], x), range(8), d) for k, d in enumerate(diag)]
    for p in range(0, count, 2):
        home, at = divmod(p, 8)
        left, right = columns[p], columns[p + 1]
        a = left[home][at : at + 1]
        b = left[home][at + 1 : at + 2]
        c = right[home][at + 1 : at + 2]
        det = a * c - b * b
        ratio = b * reciprocal(a)
        diag[home] = jnp.where(row == at, a, jnp.where(row == at + 1, c - b * ratio, diag[home]))
        inverse = reciprocal(det)
        ia, ib, ic = c * inverse, b * inverse, a * inverse
        low, high = {}, {}
        for k in left:
            low[k] = left[k] * ia - right[k] * ib
            high[k] = right[k] * ic - left[k] * ib
        for j in range(p + 2, count):
            one = left[j // 8][j % 8 : j % 8 + 1]
            two = right[j // 8][j % 8 : j % 8 + 1]
            columns[j] = {k: block - (low[k] * one + high[k] * two) for k, block in columns[j].items()}
        low[home] = jnp.where(row > at + 1, low[home], jnp.where(row == at + 1, ratio, 0.0))
        high[home] = jnp.where(row > at + 1, high[home], 0.0)
        first, second = parts[home][at : at + 1], parts[home][at + 1 : at + 2]
        for k in low:
            parts[k] = parts[k] - (low[k] * first + high[k] * second)
    worst = functools.reduce(jnp.minimum, [d / w for d, w in zip(diag, whole)])
    return jnp.concatenate([part * lax.rsqrt(d) for part, d in zip(parts, diag)], axis=0), worst


def apart(value):
    lane = lax.broadcasted_iota(jnp.int32, value.shape, 1)
    near = lane < value.shape[1] // 2
    return jnp.concatenate([jnp.where(near, value, 0.0), jnp.where(near, 0.0, value)], axis=0)


def solve_small(gram, rows, often):
    count = gram.shape[0]
    half = count // 2
    r = lax.broadcasted_iota(jnp.int32, gram.shape, 0)
    c = lax.broadcasted_iota(jnp.int32, gram.shape, 1)
    lane = lax.broadcasted_iota(jnp.int32, (1, count), 1)
    diagonal = jnp.sum(jnp.where(r == c, gram, 0.0), axis=0, keepdims=True)
    trace_lower = jnp.sum(jnp.where(lane < half, diagonal, 0.0), axis=1, keepdims=True)
    trace_upper = jnp.sum(jnp.where(lane < half, 0.0, diagonal), axis=1, keepdims=True)
    scale = 1.0 / (trace_lower + trace_upper)
    pair_scale = 1.0 / jnp.where(lane < half, trace_lower, trace_upper)
    own_pair = jnp.where((r < half) == (c < half), gram, 0.0)

    moved = dot_nn(start_rows(rows, count, half), own_pair) * pair_scale
    own_pair = own_pair * pair_scale
    smallest = []
    if not often:
        moved = dot_nn(moved, own_pair)
    for onward_too in (True, True, False, False) if often else (True, False):
        inner = dot_nt(moved, apart(moved))
        onward = dot_nn(moved, own_pair) if onward_too else moved
        moved, worst = eliminate(spread(inner, 2, rows, count), onward)
        smallest.append(jnp.min(worst))
    basis = apart(moved)

    gram = gram * scale
    reached = dot_nn(basis, gram)
    kernel = dot_nt(reached, basis)
    moved = dot_nn(start_rows(rows, half, half), kernel)
    if often:
        for onward_too in (True, True, False):
            inner = dot_nt(moved, moved)
            onward = dot_nn(moved, kernel) if onward_too else moved
            moved, _ = eliminate(spread(inner, 1, rows, half), onward)
    else:
        moved = dot_nn(moved, dot_nn(kernel, kernel))
    inner = dot_nt(moved, moved)
    onward = dot_nn(moved, jnp.concatenate([reached, basis], axis=1))
    both, worst = eliminate(spread(inner, 1, rows, 2 * count), onward)
    smallest.append(jnp.min(worst))
    enough = jnp.logical_and(jnp.logical_and(smallest[0] > 1e-4, smallest[1] > 1e-2), smallest[-1] > 3e-4)

    weights = both[:, count:]
    row = lax.broadcasted_iota(jnp.int32, (8, 2 * count), 0)
    joint = dot_nt(jnp.concatenate([both[:, :count], weights], axis=0), weights)
    energy = spread(joint[:rows], 1, rows, 2 * count)
    metric = spread(joint[rows:], 1, rows, 2 * count)
    total = jnp.zeros((8, 2 * count), jnp.float32)
    for j in range(rows):
        for b in energy[j]:
            unit = jnp.where(row == j % 8, 2.0, 0.0) if b == j // 8 else 0.0
            term = energy[j][b] * (unit - metric[j][b])
            total = total + (term if b == j // 8 else term + term)
    total = jnp.sum(total, axis=0, keepdims=True)
    damping = 0.1 * total / rows + 1e-06 * scale
    columns = [{b: energy[j][b] + damping * metric[j][b] for b in energy[j]} for j in range(rows)]
    solved, _ = eliminate(columns, both)
    return solved[:, :count], solved[:, count:], enough


def combine_kernel(rows, leaf_ref, out_ref, gram_ref, change_ref):
    leaf = leaf_ref[...]
    gram_ref[...] = lax.dot_general(leaf, leaf, (((1,), (1,)), ((), ())), preferred_element_type=jnp.float32)
    own = pl.ds(pl.multiple_of(lax.axis_index("grp") * rows, rows), rows)

    def finish(often):
        projected, weights, enough = solve_small(gram_ref[...], rows, often)
        change_ref[...] = lax.dot_general(
            projected, weights, (((0,), (0,)), ((), ())), precision=HI, preferred_element_type=jnp.float32
        )
        change = change_ref[own, :]
        top = change.astype(jnp.bfloat16)
        rest = (change - top.astype(jnp.float32)).astype(jnp.bfloat16)
        moved = jnp.dot(jnp.concatenate([top, rest], axis=0), leaf_ref[...], preferred_element_type=jnp.float32)
        out_ref[0] = leaf_ref[own, :].astype(jnp.float32) - (moved[:rows] + moved[rows:])
        return enough

    enough = finish(False)

    @pl.when(jnp.logical_not(enough))
    def _():
        finish(True)


def features_kernel(lengths_ref, order_ref, tokens_ref, out_ref, grads_ref, held_ref):
    examples, depth, full = tokens_ref.shape
    groups, modules, pairs, _ = out_ref.shape
    half = full // 2
    chunks = pairs // examples
    position = lax.broadcasted_iota(jnp.int32, (chunks, depth), 1)
    module = lax.rem(position, modules)
    lane = lax.broadcasted_iota(jnp.int32, (depth, full), 1)
    for e in range(examples):
        block = tokens_ref[e].astype(jnp.float32)
        inputs = jnp.where(lane < half, block, 0.0).astype(jnp.bfloat16)
        grads = block.T[half:]
        for k in range(depth // full):
            grads_ref[k] = grads[:, k * full : (k + 1) * full]
        live = position < lengths_ref[e] * modules
        apiece = []
        for odd in range(2):
            every = pl.ds(odd, chunks, stride=2)
            grads = jnp.concatenate([grads_ref[k, every, :] for k in range(depth // full)], axis=1)
            grads = jnp.where(live, grads, 0.0)
            apiece += [jnp.where(module == q, grads, 0.0).astype(jnp.bfloat16) for q in range(modules)]
        both = jnp.dot(jnp.concatenate(apiece, axis=0), inputs, preferred_element_type=jnp.float32)
        flat = both[: modules * chunks] + pltpu.roll(both[modules * chunks :], half, 1)
        held_ref[pl.ds(e, modules * chunks, stride=examples), :] = flat
    for slot in range(modules):
        first = pl.multiple_of(order_ref[slot] * pairs, pairs)
        message = held_ref[pl.ds(first, pairs), :].astype(jnp.bfloat16)
        for g in range(groups):
            out_ref[g, slot] = message


def gram_route(tokens, lengths, module_order):
    groups, owners = lax.axis_size("grp"), lax.axis_size("mod")
    own, slots, modules, full = tokens.shape
    width = (full // 2) ** 2
    rows = owners * own
    count = groups * rows
    chunks = width // full
    messages = pl.pallas_call(
        features_kernel,
        out_shape=jax.ShapeDtypeStruct((groups, modules, chunks * own, full), jnp.bfloat16),
        in_specs=[pl.BlockSpec(memory_space=space) for space in (pltpu.SMEM, pltpu.SMEM, pltpu.VMEM)],
        scratch_shapes=[
            pltpu.VMEM((slots * modules // full, full // 2, full), jnp.float32),
            pltpu.VMEM((modules * chunks * own, full), jnp.float32),
        ],
        compiler_params=pltpu.CompilerParams(vmem_limit_bytes=VMEM_BYTES),
    )(lengths, module_order, tokens.reshape(own, slots * modules, full))
    messages = messages.reshape(groups * modules, chunks, own, full).transpose(0, 2, 1, 3).reshape(groups * modules, own, width)
    leaf = lax.all_to_all(messages, ("grp", "mod"), split_axis=0, concat_axis=0, tiled=True)
    leaf = leaf.reshape(count, width)
    return pl.pallas_call(
        functools.partial(combine_kernel, rows),
        out_shape=jax.ShapeDtypeStruct((1, rows, width), jnp.float32),
        scratch_shapes=[pltpu.VMEM((count, count), jnp.float32)] * 2,
        compiler_params=pltpu.CompilerParams(vmem_limit_bytes=VMEM_BYTES),
    )(leaf)


def local_features(token_block, live_counts):
    example_count, token_slots, module_count, full_width = token_block.shape
    half_width = full_width // 2
    live_mask = jnp.arange(token_slots, dtype=jnp.int32)[None, :] < live_counts[:, None]
    grad_side = jnp.where(
        live_mask[:, :, None, None],
        token_block[:, :, :, half_width:],
        jnp.zeros((), token_block.dtype),
    )
    input_side = token_block[:, :, :, :half_width]
    outer = jnp.einsum("etmo,etmi->meoi", grad_side, input_side, preferred_element_type=jnp.float32)
    return outer.reshape(module_count, example_count, half_width * half_width).astype(jnp.bfloat16)


def per_device(tokens, lengths, module_order):
    groups, owners = lax.axis_size("grp"), lax.axis_size("mod")
    own, slots, modules, full = tokens.shape
    if groups == 4 and owners * own == 16 and owners == modules == 8 and full == 128:
        return gram_route(tokens, lengths, module_order)
    return sketch_tree(local_features(tokens, lengths), module_order)


def solution(mesh):
    return jax.shard_map(
        per_device,
        mesh=mesh,
        in_specs=(P(("grp", "mod"), None, None, None), P(("grp", "mod")), P()),
        out_specs=P("mod", "grp", None),
        check_vma=False,
    )
```

```python
import functools
import math

import jax
import jax.numpy as jnp
import numpy as np
from jax import lax
from jax.experimental import pallas as pl
from jax.experimental.pallas import tpu as pltpu
from jax.sharding import PartitionSpec as P

ITERS = 3
HI = lax.Precision.HIGHEST
VMEM_BYTES = 48 * 1024 * 1024


def partner(value, axis, bit):
    mask = 2**bit
    return xor_send(value, axis, mask)


def xor_send(value, axis, mask):
    pairs = [(source, source ^ mask) for source in range(lax.axis_size(axis))]
    return lax.ppermute(value, axis, pairs)


def start_basis(row_count, col_count):
    row_index = np.arange(row_count, dtype=np.float64)[:, None] + 0.5
    col_index = np.arange(col_count, dtype=np.float64)[None, :] + 0.5
    return np.cos(np.pi * row_index * col_index / row_count).astype(np.float32)


def orthonormal(matrix):
    for repeat in range(2):
        cross_gram = jnp.dot(matrix.T, matrix, precision=HI)
        factor = jnp.linalg.cholesky(cross_gram)
        matrix = jax.scipy.linalg.solve_triangular(factor, matrix.T, lower=True).T
    return matrix


def merge_pair(lower_sketch, upper_sketch):
    stacked = jnp.concatenate([lower_sketch, upper_sketch], axis=0)
    kernel = jnp.dot(stacked, stacked.T, precision=HI)
    current = start_basis(stacked.shape[0], lower_sketch.shape[0])
    for repeat in range(ITERS):
        current = orthonormal(jnp.dot(kernel, current, precision=HI))
    return jnp.dot(current.T, stacked, precision=HI)


def precondition(group_rows, sketch):
    sketch_rows = sketch.shape[0]
    damping = 0.1 * jnp.sum(sketch * sketch) / sketch_rows + 1e-06
    capacitance = jnp.dot(sketch, sketch.T, precision=HI) + damping * jnp.eye(sketch_rows, dtype=jnp.float32)
    projected = jnp.dot(group_rows, sketch.T, precision=HI)
    factor = jnp.linalg.cholesky(capacitance)
    middle = jax.scipy.linalg.solve_triangular(factor, projected.T, lower=True)
    weights = jax.scipy.linalg.solve_triangular(factor, middle, lower=True, trans=1).T
    return group_rows - jnp.dot(weights, sketch, precision=HI)


def sketch_tree(features, module_order):
    ordered = jnp.take(features, module_order, axis=0)
    group_rows = lax.all_to_all(ordered, "mod", split_axis=0, concat_axis=1, tiled=True)
    leaves = group_rows.astype(jnp.float32)
    merge_all = jax.vmap(merge_pair)
    levels = lax.axis_size("grp").bit_length() - 1
    position = lax.axis_index("grp")
    sketch = leaves
    for height in range(levels):
        sister = partner(sketch, "grp", height)
        upper_side = position // 2**height % 2 == 1
        lower_part = jnp.where(upper_side, sister, sketch)
        upper_part = jnp.where(upper_side, sketch, sister)
        sketch = merge_all(lower_part, upper_part)
    return jax.vmap(precondition)(leaves, sketch)


def dot_nt(a, b):
    return lax.dot_general(a, b, (((1,), (1,)), ((), ())), precision=HI, preferred_element_type=jnp.float32)


def dot_nn(a, b):
    return jnp.dot(a, b, precision=HI, preferred_element_type=jnp.float32)


def start_rows(count, width, span):
    j = lax.broadcasted_iota(jnp.int32, (count, width), 0)
    i = lax.rem(lax.broadcasted_iota(jnp.int32, (count, width), 1), span)
    turn = lax.rem((2 * i + 1) * (2 * j + 1), 8 * span)
    folded = jnp.minimum(turn, 8 * span - turn)
    angle = (2 * span - folded).astype(jnp.float32) * (math.pi / (4 * span))
    square = angle * angle
    series = jnp.full_like(angle, 1.0)
    for n in range(12, 0, -2):
        series = 1.0 - square * series * (1.0 / (n * (n + 1)))
    return angle * series


def spread(gram, problems, count, width):
    lane = lax.broadcasted_iota(jnp.int32, (8, width), 1)
    columns = []
    for j in range(count):
        blocks = {}
        for b in range(j // 8, count // 8):
            parts = [
                jnp.broadcast_to(gram[8 * b : 8 * b + 8, k * count + j : k * count + j + 1], (8, width))
                for k in range(problems)
            ]
            blocks[b] = parts[0] if problems == 1 else jnp.where(lane < width // 2, parts[0], parts[1])
        columns.append(blocks)
    return columns


def eliminate(columns, rhs):
    count = len(columns)
    width = rhs.shape[1]
    parts = [rhs[8 * b : 8 * b + 8] for b in range(count // 8)]
    row = lax.broadcasted_iota(jnp.int32, (8, width), 0)
    diag = [jnp.ones((8, width), jnp.float32) for _ in parts]
    whole = [functools.reduce(lambda x, j: jnp.where(row == j, columns[8 * k + j][k], x), range(8), d) for k, d in enumerate(diag)]
    for p in range(0, count, 2):
        home, at = divmod(p, 8)
        left, right = columns[p], columns[p + 1]
        a = left[home][at : at + 1]
        b = left[home][at + 1 : at + 2]
        c = right[home][at + 1 : at + 2]
        det = a * c - b * b
        ratio = b / a
        diag[home] = jnp.where(row == at, a, jnp.where(row == at + 1, c - b * ratio, diag[home]))
        inverse = 1.0 / det
        ia, ib, ic = c * inverse, b * inverse, a * inverse
        low, high = {}, {}
        for k in left:
            low[k] = left[k] * ia - right[k] * ib
            high[k] = right[k] * ic - left[k] * ib
        for j in range(p + 2, count):
            one = left[j // 8][j % 8 : j % 8 + 1]
            two = right[j // 8][j % 8 : j % 8 + 1]
            columns[j] = {k: block - (low[k] * one + high[k] * two) for k, block in columns[j].items()}
        low[home] = jnp.where(row > at + 1, low[home], jnp.where(row == at + 1, ratio, 0.0))
        high[home] = jnp.where(row > at + 1, high[home], 0.0)
        first, second = parts[home][at : at + 1], parts[home][at + 1 : at + 2]
        for k in low:
            parts[k] = parts[k] - (low[k] * first + high[k] * second)
    worst = functools.reduce(jnp.minimum, [d / w for d, w in zip(diag, whole)])
    return jnp.concatenate([part * lax.rsqrt(d) for part, d in zip(parts, diag)], axis=0), worst


def apart(value):
    lane = lax.broadcasted_iota(jnp.int32, value.shape, 1)
    near = lane < value.shape[1] // 2
    return jnp.concatenate([jnp.where(near, value, 0.0), jnp.where(near, 0.0, value)], axis=0)


def solve_small(gram, rows, often):
    count = gram.shape[0]
    half = count // 2
    r = lax.broadcasted_iota(jnp.int32, gram.shape, 0)
    c = lax.broadcasted_iota(jnp.int32, gram.shape, 1)
    lane = lax.broadcasted_iota(jnp.int32, (1, count), 1)
    diagonal = jnp.sum(jnp.where(r == c, gram, 0.0), axis=0, keepdims=True)
    trace_lower = jnp.sum(jnp.where(lane < half, diagonal, 0.0), axis=1, keepdims=True)
    trace_upper = jnp.sum(jnp.where(lane < half, 0.0, diagonal), axis=1, keepdims=True)
    scale = 1.0 / (trace_lower + trace_upper)
    pair_scale = 1.0 / jnp.where(lane < half, trace_lower, trace_upper)
    own_pair = jnp.where((r < half) == (c < half), gram, 0.0)

    moved = dot_nn(start_rows(rows, count, half), own_pair) * pair_scale
    own_pair = own_pair * pair_scale
    smallest = []
    if not often:
        moved = dot_nn(moved, own_pair)
    for onward_too in (True, True, False, False) if often else (True, False):
        inner = dot_nt(moved, apart(moved))
        onward = dot_nn(moved, own_pair) if onward_too else moved
        moved, worst = eliminate(spread(inner, 2, rows, count), onward)
        smallest.append(jnp.min(worst))
    basis = apart(moved)

    gram = gram * scale
    reached = dot_nn(basis, gram)
    kernel = dot_nt(reached, basis)
    moved = dot_nn(start_rows(rows, half, half), kernel)
    if often:
        for onward_too in (True, True, False):
            inner = dot_nt(moved, moved)
            onward = dot_nn(moved, kernel) if onward_too else moved
            moved, _ = eliminate(spread(inner, 1, rows, half), onward)
    else:
        moved = dot_nn(moved, dot_nn(kernel, kernel))
    inner = dot_nt(moved, moved)
    onward = dot_nn(moved, jnp.concatenate([reached, basis], axis=1))
    both, worst = eliminate(spread(inner, 1, rows, 2 * count), onward)
    smallest.append(jnp.min(worst))
    enough = jnp.logical_and(jnp.logical_and(smallest[0] > 1e-4, smallest[1] > 1e-2), smallest[-1] > 3e-4)

    weights = both[:, count:]
    row = lax.broadcasted_iota(jnp.int32, (8, 2 * count), 0)
    joint = dot_nt(jnp.concatenate([both[:, :count], weights], axis=0), weights)
    energy = spread(joint[:rows], 1, rows, 2 * count)
    metric = spread(joint[rows:], 1, rows, 2 * count)
    total = jnp.zeros((8, 2 * count), jnp.float32)
    for j in range(rows):
        for b in energy[j]:
            unit = jnp.where(row == j % 8, 2.0, 0.0) if b == j // 8 else 0.0
            term = energy[j][b] * (unit - metric[j][b])
            total = total + (term if b == j // 8 else term + term)
    total = jnp.sum(total, axis=0, keepdims=True)
    damping = 0.1 * total / rows + 1e-06 * scale
    columns = [{b: energy[j][b] + damping * metric[j][b] for b in energy[j]} for j in range(rows)]
    solved, _ = eliminate(columns, both)
    return solved[:, :count], solved[:, count:], enough


def combine_kernel(rows, gram_ref, leaf_ref, out_ref, change_ref):
    own = pl.ds(pl.multiple_of(lax.axis_index("grp") * rows, rows), rows)

    def finish(often):
        projected, weights, enough = solve_small(gram_ref[...], rows, often)
        change_ref[...] = lax.dot_general(
            projected, weights, (((0,), (0,)), ((), ())), precision=HI, preferred_element_type=jnp.float32
        )
        change = change_ref[own, :]
        top = change.astype(jnp.bfloat16)
        rest = (change - top.astype(jnp.float32)).astype(jnp.bfloat16)
        moved = jnp.dot(jnp.concatenate([top, rest], axis=0), leaf_ref[...], preferred_element_type=jnp.float32)
        out_ref[0] = leaf_ref[own, :].astype(jnp.float32) - (moved[:rows] + moved[rows:])
        return enough

    enough = finish(False)

    @pl.when(jnp.logical_not(enough))
    def _():
        finish(True)


def features_kernel(lengths_ref, order_ref, tokens_ref, out_ref, grads_ref, held_ref):
    examples, depth, full = tokens_ref.shape
    groups, modules, pairs, _ = out_ref.shape
    half = full // 2
    chunks = pairs // examples
    position = lax.broadcasted_iota(jnp.int32, (chunks, depth), 1)
    module = lax.rem(position, modules)
    lane = lax.broadcasted_iota(jnp.int32, (depth, full), 1)
    for e in range(examples):
        block = tokens_ref[e].astype(jnp.float32)
        left = jnp.where(lane < half, block, 0.0).astype(jnp.bfloat16)
        right = jnp.where(lane < half, 0.0, pltpu.roll(block, half, 1)).astype(jnp.bfloat16)
        grads = block.T[half:]
        for k in range(depth // full):
            grads_ref[k] = grads[:, k * full : (k + 1) * full]
        live = position < lengths_ref[e] * modules
        flat = jnp.zeros((modules * chunks, full), jnp.float32)
        for odd, side in ((0, left), (1, right)):
            every = pl.ds(odd, chunks, stride=2)
            grads = jnp.concatenate([grads_ref[k, every, :] for k in range(depth // full)], axis=1)
            grads = jnp.where(live, grads, 0.0)
            apiece = [jnp.where(module == q, grads, 0.0).astype(jnp.bfloat16) for q in range(modules)]
            flat = flat + jnp.dot(jnp.concatenate(apiece, axis=0), side, preferred_element_type=jnp.float32)
        held_ref[pl.ds(e, modules * chunks, stride=examples), :] = flat
    for slot in range(modules):
        first = pl.multiple_of(order_ref[slot] * pairs, pairs)
        message = held_ref[pl.ds(first, pairs), :].astype(jnp.bfloat16)
        for g in range(groups):
            out_ref[g, slot] = message


def gram_route(tokens, lengths, module_order):
    groups, owners = lax.axis_size("grp"), lax.axis_size("mod")
    own, slots, modules, full = tokens.shape
    width = (full // 2) ** 2
    rows = owners * own
    count = groups * rows
    chunks = width // full
    messages = pl.pallas_call(
        features_kernel,
        out_shape=jax.ShapeDtypeStruct((groups, modules, chunks * own, full), jnp.bfloat16),
        in_specs=[pl.BlockSpec(memory_space=space) for space in (pltpu.SMEM, pltpu.SMEM, pltpu.VMEM)],
        scratch_shapes=[
            pltpu.VMEM((slots * modules // full, full // 2, full), jnp.float32),
            pltpu.VMEM((modules * chunks * own, full), jnp.float32),
        ],
        compiler_params=pltpu.CompilerParams(vmem_limit_bytes=VMEM_BYTES),
    )(lengths, module_order, tokens.reshape(own, slots * modules, full))
    messages = messages.reshape(groups * modules, chunks, own, full).transpose(0, 2, 1, 3).reshape(groups * modules, own, width)
    leaf = lax.all_to_all(messages, ("grp", "mod"), split_axis=0, concat_axis=0, tiled=True)
    leaf = leaf.reshape(count, width)
    gram = lax.dot_general(leaf, leaf, (((1,), (1,)), ((), ())), preferred_element_type=jnp.float32)
    return pl.pallas_call(
        functools.partial(combine_kernel, rows),
        out_shape=jax.ShapeDtypeStruct((1, rows, width), jnp.float32),
        scratch_shapes=[pltpu.VMEM((count, count), jnp.float32)],
        compiler_params=pltpu.CompilerParams(vmem_limit_bytes=VMEM_BYTES),
    )(gram, leaf)


def local_features(token_block, live_counts):
    example_count, token_slots, module_count, full_width = token_block.shape
    half_width = full_width // 2
    live_mask = jnp.arange(token_slots, dtype=jnp.int32)[None, :] < live_counts[:, None]
    grad_side = jnp.where(
        live_mask[:, :, None, None],
        token_block[:, :, :, half_width:],
        jnp.zeros((), token_block.dtype),
    )
    input_side = token_block[:, :, :, :half_width]
    outer = jnp.einsum("etmo,etmi->meoi", grad_side, input_side, preferred_element_type=jnp.float32)
    return outer.reshape(module_count, example_count, half_width * half_width).astype(jnp.bfloat16)


def per_device(tokens, lengths, module_order):
    groups, owners = lax.axis_size("grp"), lax.axis_size("mod")
    own, slots, modules, full = tokens.shape
    if groups == 4 and owners * own == 16 and owners == modules == 8 and full == 128:
        return gram_route(tokens, lengths, module_order)
    return sketch_tree(local_features(tokens, lengths), module_order)


def solution(mesh):
    return jax.shard_map(
        per_device,
        mesh=mesh,
        in_specs=(P(("grp", "mod"), None, None, None), P(("grp", "mod")), P()),
        out_specs=P("mod", "grp", None),
        check_vma=False,
    )
```

```python
import functools
import math

import jax
import jax.numpy as jnp
import numpy as np
from jax import lax
from jax.experimental import pallas as pl
from jax.experimental.pallas import tpu as pltpu
from jax.sharding import PartitionSpec as P

ITERS = 3
HI = lax.Precision.HIGHEST
VMEM_BYTES = 48 * 1024 * 1024
FETCH_BYTES = 56 * 1024 * 1024


def partner(value, axis, bit):
    mask = 2**bit
    return xor_send(value, axis, mask)


def xor_send(value, axis, mask):
    pairs = [(source, source ^ mask) for source in range(lax.axis_size(axis))]
    return lax.ppermute(value, axis, pairs)


def start_basis(row_count, col_count):
    row_index = np.arange(row_count, dtype=np.float64)[:, None] + 0.5
    col_index = np.arange(col_count, dtype=np.float64)[None, :] + 0.5
    return np.cos(np.pi * row_index * col_index / row_count).astype(np.float32)


def orthonormal(matrix):
    for repeat in range(2):
        cross_gram = jnp.dot(matrix.T, matrix, precision=HI)
        factor = jnp.linalg.cholesky(cross_gram)
        matrix = jax.scipy.linalg.solve_triangular(factor, matrix.T, lower=True).T
    return matrix


def merge_pair(lower_sketch, upper_sketch):
    stacked = jnp.concatenate([lower_sketch, upper_sketch], axis=0)
    kernel = jnp.dot(stacked, stacked.T, precision=HI)
    current = start_basis(stacked.shape[0], lower_sketch.shape[0])
    for repeat in range(ITERS):
        current = orthonormal(jnp.dot(kernel, current, precision=HI))
    return jnp.dot(current.T, stacked, precision=HI)


def precondition(group_rows, sketch):
    sketch_rows = sketch.shape[0]
    damping = 0.1 * jnp.sum(sketch * sketch) / sketch_rows + 1e-06
    capacitance = jnp.dot(sketch, sketch.T, precision=HI) + damping * jnp.eye(sketch_rows, dtype=jnp.float32)
    projected = jnp.dot(group_rows, sketch.T, precision=HI)
    factor = jnp.linalg.cholesky(capacitance)
    middle = jax.scipy.linalg.solve_triangular(factor, projected.T, lower=True)
    weights = jax.scipy.linalg.solve_triangular(factor, middle, lower=True, trans=1).T
    return group_rows - jnp.dot(weights, sketch, precision=HI)


def sketch_tree(features, module_order):
    ordered = jnp.take(features, module_order, axis=0)
    group_rows = lax.all_to_all(ordered, "mod", split_axis=0, concat_axis=1, tiled=True)
    leaves = group_rows.astype(jnp.float32)
    merge_all = jax.vmap(merge_pair)
    levels = lax.axis_size("grp").bit_length() - 1
    position = lax.axis_index("grp")
    sketch = leaves
    for height in range(levels):
        sister = partner(sketch, "grp", height)
        upper_side = position // 2**height % 2 == 1
        lower_part = jnp.where(upper_side, sister, sketch)
        upper_part = jnp.where(upper_side, sketch, sister)
        sketch = merge_all(lower_part, upper_part)
    return jax.vmap(precondition)(leaves, sketch)


def dot_nt(a, b):
    return lax.dot_general(a, b, (((1,), (1,)), ((), ())), precision=HI, preferred_element_type=jnp.float32)


def dot_nn(a, b):
    return jnp.dot(a, b, precision=HI, preferred_element_type=jnp.float32)


def start_rows(count, width, span):
    j = lax.broadcasted_iota(jnp.int32, (count, width), 0)
    i = lax.rem(lax.broadcasted_iota(jnp.int32, (count, width), 1), span)
    turn = lax.rem((2 * i + 1) * (2 * j + 1), 8 * span)
    folded = jnp.minimum(turn, 8 * span - turn)
    angle = (2 * span - folded).astype(jnp.float32) * (math.pi / (4 * span))
    square = angle * angle
    series = jnp.full_like(angle, 1.0)
    for n in range(12, 0, -2):
        series = 1.0 - square * series * (1.0 / (n * (n + 1)))
    return angle * series


def spread(gram, problems, count, width):
    lane = lax.broadcasted_iota(jnp.int32, (8, width), 1)
    columns = []
    for j in range(count):
        blocks = {}
        for b in range(j // 8, count // 8):
            parts = [
                jnp.broadcast_to(gram[8 * b : 8 * b + 8, k * count + j : k * count + j + 1], (8, width))
                for k in range(problems)
            ]
            blocks[b] = parts[0] if problems == 1 else jnp.where(lane < width // 2, parts[0], parts[1])
        columns.append(blocks)
    return columns


def eliminate(columns, rhs):
    count = len(columns)
    width = rhs.shape[1]
    parts = [rhs[8 * b : 8 * b + 8] for b in range(count // 8)]
    row = lax.broadcasted_iota(jnp.int32, (8, width), 0)
    diag = [jnp.ones((8, width), jnp.float32) for _ in parts]
    whole = [functools.reduce(lambda x, j: jnp.where(row == j, columns[8 * k + j][k], x), range(8), d) for k, d in enumerate(diag)]
    for p in range(0, count, 2):
        home, at = divmod(p, 8)
        left, right = columns[p], columns[p + 1]
        a = left[home][at : at + 1]
        b = left[home][at + 1 : at + 2]
        c = right[home][at + 1 : at + 2]
        det = a * c - b * b
        ratio = b / a
        diag[home] = jnp.where(row == at, a, jnp.where(row == at + 1, c - b * ratio, diag[home]))
        inverse = 1.0 / det
        ia, ib, ic = c * inverse, b * inverse, a * inverse
        low, high = {}, {}
        for k in left:
            low[k] = left[k] * ia - right[k] * ib
            high[k] = right[k] * ic - left[k] * ib
        for j in range(p + 2, count):
            one = left[j // 8][j % 8 : j % 8 + 1]
            two = right[j // 8][j % 8 : j % 8 + 1]
            columns[j] = {k: block - (low[k] * one + high[k] * two) for k, block in columns[j].items()}
        low[home] = jnp.where(row > at + 1, low[home], jnp.where(row == at + 1, ratio, 0.0))
        high[home] = jnp.where(row > at + 1, high[home], 0.0)
        first, second = parts[home][at : at + 1], parts[home][at + 1 : at + 2]
        for k in low:
            parts[k] = parts[k] - (low[k] * first + high[k] * second)
    worst = functools.reduce(jnp.minimum, [d / w for d, w in zip(diag, whole)])
    return jnp.concatenate([part * lax.rsqrt(d) for part, d in zip(parts, diag)], axis=0), worst


def apart(value):
    lane = lax.broadcasted_iota(jnp.int32, value.shape, 1)
    near = lane < value.shape[1] // 2
    return jnp.concatenate([jnp.where(near, value, 0.0), jnp.where(near, 0.0, value)], axis=0)


def solve_small(gram, rows, often):
    count = gram.shape[0]
    half = count // 2
    r = lax.broadcasted_iota(jnp.int32, gram.shape, 0)
    c = lax.broadcasted_iota(jnp.int32, gram.shape, 1)
    lane = lax.broadcasted_iota(jnp.int32, (1, count), 1)
    diagonal = jnp.sum(jnp.where(r == c, gram, 0.0), axis=0, keepdims=True)
    trace_lower = jnp.sum(jnp.where(lane < half, diagonal, 0.0), axis=1, keepdims=True)
    trace_upper = jnp.sum(jnp.where(lane < half, 0.0, diagonal), axis=1, keepdims=True)
    scale = 1.0 / (trace_lower + trace_upper)
    pair_scale = 1.0 / jnp.where(lane < half, trace_lower, trace_upper)
    own_pair = jnp.where((r < half) == (c < half), gram, 0.0)

    moved = dot_nn(start_rows(rows, count, half), own_pair) * pair_scale
    own_pair = own_pair * pair_scale
    smallest = []
    if not often:
        moved = dot_nn(moved, own_pair)
    for onward_too in (True, True, False, False) if often else (True, False):
        inner = dot_nt(moved, apart(moved))
        onward = dot_nn(moved, own_pair) if onward_too else moved
        moved, worst = eliminate(spread(inner, 2, rows, count), onward)
        smallest.append(jnp.min(worst))
    basis = apart(moved)

    gram = gram * scale
    reached = dot_nn(basis, gram)
    kernel = dot_nt(reached, basis)
    moved = dot_nn(start_rows(rows, half, half), kernel)
    if often:
        for onward_too in (True, True, False):
            inner = dot_nt(moved, moved)
            onward = dot_nn(moved, kernel) if onward_too else moved
            moved, _ = eliminate(spread(inner, 1, rows, half), onward)
    else:
        moved = dot_nn(moved, dot_nn(kernel, kernel))
    inner = dot_nt(moved, moved)
    onward = dot_nn(moved, jnp.concatenate([reached, basis], axis=1))
    both, worst = eliminate(spread(inner, 1, rows, 2 * count), onward)
    smallest.append(jnp.min(worst))
    enough = jnp.logical_and(jnp.logical_and(smallest[0] > 1e-4, smallest[1] > 1e-2), smallest[-1] > 3e-4)

    weights = both[:, count:]
    row = lax.broadcasted_iota(jnp.int32, (8, 2 * count), 0)
    joint = dot_nt(jnp.concatenate([both[:, :count], weights], axis=0), weights)
    energy = spread(joint[:rows], 1, rows, 2 * count)
    metric = spread(joint[rows:], 1, rows, 2 * count)
    total = jnp.zeros((8, 2 * count), jnp.float32)
    for j in range(rows):
        for b in energy[j]:
            unit = jnp.where(row == j % 8, 2.0, 0.0) if b == j // 8 else 0.0
            term = energy[j][b] * (unit - metric[j][b])
            total = total + (term if b == j // 8 else term + term)
    total = jnp.sum(total, axis=0, keepdims=True)
    damping = 0.1 * total / rows + 1e-06 * scale
    columns = [{b: energy[j][b] + damping * metric[j][b] for b in energy[j]} for j in range(rows)]
    solved, _ = eliminate(columns, both)
    return solved[:, :count], solved[:, count:], enough


def combine_kernel(rows, leaf_ref, out_ref, gram_ref, change_ref):
    leaf = leaf_ref[...]
    gram_ref[...] = lax.dot_general(leaf, leaf, (((1,), (1,)), ((), ())), preferred_element_type=jnp.float32)
    own = pl.ds(pl.multiple_of(lax.axis_index("grp") * rows, rows), rows)

    def finish(often):
        projected, weights, enough = solve_small(gram_ref[...], rows, often)
        change_ref[...] = lax.dot_general(
            projected, weights, (((0,), (0,)), ((), ())), precision=HI, preferred_element_type=jnp.float32
        )
        change = change_ref[own, :]
        top = change.astype(jnp.bfloat16)
        rest = (change - top.astype(jnp.float32)).astype(jnp.bfloat16)
        moved = jnp.dot(jnp.concatenate([top, rest], axis=0), leaf_ref[...], preferred_element_type=jnp.float32)
        out_ref[0] = leaf_ref[own, :].astype(jnp.float32) - (moved[:rows] + moved[rows:])
        return enough

    enough = finish(False)

    @pl.when(jnp.logical_not(enough))
    def _():
        finish(True)


def features_kernel(
    lengths_hbm, order_hbm, tokens_hbm, out_hbm, lengths_ref, order_ref, tokens_ref, grads_ref, held_ref, out_ref, sems
):
    examples, depth, full = tokens_ref.shape
    groups, modules, pairs, _ = out_hbm.shape
    half = full // 2
    chunks = pairs // examples
    small = [
        pltpu.make_async_copy(lengths_hbm, lengths_ref, sems.at[0]),
        pltpu.make_async_copy(order_hbm, order_ref, sems.at[1]),
    ]
    large = [pltpu.make_async_copy(tokens_hbm.at[e], tokens_ref.at[e], sems.at[2 + e]) for e in range(examples)]
    for copy in small + large:
        copy.start()
    position = lax.broadcasted_iota(jnp.int32, (chunks, depth), 1)
    module = lax.rem(position, modules)
    lane = lax.broadcasted_iota(jnp.int32, (depth, full), 1)
    for copy in small:
        copy.wait()
    for e in range(examples):
        large[e].wait()
        block = tokens_ref[e].astype(jnp.float32)
        left = jnp.where(lane < half, block, 0.0).astype(jnp.bfloat16)
        right = jnp.where(lane < half, 0.0, pltpu.roll(block, half, 1)).astype(jnp.bfloat16)
        grads = block.T[half:]
        for k in range(depth // full):
            grads_ref[k] = grads[:, k * full : (k + 1) * full]
        live = position < lengths_ref[e] * modules
        flat = jnp.zeros((modules * chunks, full), jnp.float32)
        for odd, side in ((0, left), (1, right)):
            every = pl.ds(odd, chunks, stride=2)
            grads = jnp.concatenate([grads_ref[k, every, :] for k in range(depth // full)], axis=1)
            grads = jnp.where(live, grads, 0.0)
            apiece = [jnp.where(module == q, grads, 0.0).astype(jnp.bfloat16) for q in range(modules)]
            flat = flat + jnp.dot(jnp.concatenate(apiece, axis=0), side, preferred_element_type=jnp.float32)
        held_ref[pl.ds(e, modules * chunks, stride=examples), :] = flat
    sent = []
    for slot in range(modules):
        first = pl.multiple_of(order_ref[slot] * pairs, pairs)
        out_ref[slot] = held_ref[pl.ds(first, pairs), :].astype(jnp.bfloat16)
        for g in range(groups):
            at = 2 + examples + slot * groups + g
            sent.append(pltpu.make_async_copy(out_ref.at[slot], out_hbm.at[g, slot], sems.at[at]))
            sent[-1].start()
    for copy in sent:
        copy.wait()


def gram_route(tokens, lengths, module_order):
    groups, owners = lax.axis_size("grp"), lax.axis_size("mod")
    own, slots, modules, full = tokens.shape
    width = (full // 2) ** 2
    rows = owners * own
    count = groups * rows
    chunks = width // full
    messages = pl.pallas_call(
        features_kernel,
        out_shape=jax.ShapeDtypeStruct((groups, modules, chunks * own, full), jnp.bfloat16),
        in_specs=[pl.BlockSpec(memory_space=pl.ANY)] * 3,
        out_specs=pl.BlockSpec(memory_space=pl.ANY),
        scratch_shapes=[
            pltpu.SMEM(lengths.shape, jnp.int32),
            pltpu.SMEM(module_order.shape, jnp.int32),
            pltpu.VMEM((own, slots * modules, full), jnp.bfloat16),
            pltpu.VMEM((slots * modules // full, full // 2, full), jnp.float32),
            pltpu.VMEM((modules * chunks * own, full), jnp.float32),
            pltpu.VMEM((modules, chunks * own, full), jnp.bfloat16),
            pltpu.SemaphoreType.DMA((2 + own + modules * groups,)),
        ],
        compiler_params=pltpu.CompilerParams(vmem_limit_bytes=FETCH_BYTES),
    )(lengths, module_order, tokens.reshape(own, slots * modules, full))
    messages = messages.reshape(groups * modules, chunks, own, full).transpose(0, 2, 1, 3).reshape(groups * modules, own, width)
    leaf = lax.all_to_all(messages, ("grp", "mod"), split_axis=0, concat_axis=0, tiled=True)
    leaf = leaf.reshape(count, width)
    return pl.pallas_call(
        functools.partial(combine_kernel, rows),
        out_shape=jax.ShapeDtypeStruct((1, rows, width), jnp.float32),
        scratch_shapes=[pltpu.VMEM((count, count), jnp.float32)] * 2,
        compiler_params=pltpu.CompilerParams(vmem_limit_bytes=VMEM_BYTES),
    )(leaf)


def local_features(token_block, live_counts):
    example_count, token_slots, module_count, full_width = token_block.shape
    half_width = full_width // 2
    live_mask = jnp.arange(token_slots, dtype=jnp.int32)[None, :] < live_counts[:, None]
    grad_side = jnp.where(
        live_mask[:, :, None, None],
        token_block[:, :, :, half_width:],
        jnp.zeros((), token_block.dtype),
    )
    input_side = token_block[:, :, :, :half_width]
    outer = jnp.einsum("etmo,etmi->meoi", grad_side, input_side, preferred_element_type=jnp.float32)
    return outer.reshape(module_count, example_count, half_width * half_width).astype(jnp.bfloat16)


def per_device(tokens, lengths, module_order):
    groups, owners = lax.axis_size("grp"), lax.axis_size("mod")
    own, slots, modules, full = tokens.shape
    if groups == 4 and owners * own == 16 and owners == modules == 8 and full == 128:
        return gram_route(tokens, lengths, module_order)
    return sketch_tree(local_features(tokens, lengths), module_order)


def solution(mesh):
    return jax.shard_map(
        per_device,
        mesh=mesh,
        in_specs=(P(("grp", "mod"), None, None, None), P(("grp", "mod")), P()),
        out_specs=P("mod", "grp", None),
        check_vma=False,
    )
```

```python
import functools
import math

import jax
import jax.numpy as jnp
import numpy as np
from jax import lax
from jax.experimental import pallas as pl
from jax.experimental.pallas import tpu as pltpu
from jax.sharding import PartitionSpec as P

ITERS = 3
HI = lax.Precision.HIGHEST
VMEM_BYTES = 48 * 1024 * 1024


def partner(value, axis, bit):
    mask = 2**bit
    return xor_send(value, axis, mask)


def xor_send(value, axis, mask):
    pairs = [(source, source ^ mask) for source in range(lax.axis_size(axis))]
    return lax.ppermute(value, axis, pairs)


def start_basis(row_count, col_count):
    row_index = np.arange(row_count, dtype=np.float64)[:, None] + 0.5
    col_index = np.arange(col_count, dtype=np.float64)[None, :] + 0.5
    return np.cos(np.pi * row_index * col_index / row_count).astype(np.float32)


def orthonormal(matrix):
    for repeat in range(2):
        cross_gram = jnp.dot(matrix.T, matrix, precision=HI)
        factor = jnp.linalg.cholesky(cross_gram)
        matrix = jax.scipy.linalg.solve_triangular(factor, matrix.T, lower=True).T
    return matrix


def merge_pair(lower_sketch, upper_sketch):
    stacked = jnp.concatenate([lower_sketch, upper_sketch], axis=0)
    kernel = jnp.dot(stacked, stacked.T, precision=HI)
    current = start_basis(stacked.shape[0], lower_sketch.shape[0])
    for repeat in range(ITERS):
        current = orthonormal(jnp.dot(kernel, current, precision=HI))
    return jnp.dot(current.T, stacked, precision=HI)


def precondition(group_rows, sketch):
    sketch_rows = sketch.shape[0]
    damping = 0.1 * jnp.sum(sketch * sketch) / sketch_rows + 1e-06
    capacitance = jnp.dot(sketch, sketch.T, precision=HI) + damping * jnp.eye(sketch_rows, dtype=jnp.float32)
    projected = jnp.dot(group_rows, sketch.T, precision=HI)
    factor = jnp.linalg.cholesky(capacitance)
    middle = jax.scipy.linalg.solve_triangular(factor, projected.T, lower=True)
    weights = jax.scipy.linalg.solve_triangular(factor, middle, lower=True, trans=1).T
    return group_rows - jnp.dot(weights, sketch, precision=HI)


def sketch_tree(features, module_order):
    ordered = jnp.take(features, module_order, axis=0)
    group_rows = lax.all_to_all(ordered, "mod", split_axis=0, concat_axis=1, tiled=True)
    leaves = group_rows.astype(jnp.float32)
    merge_all = jax.vmap(merge_pair)
    levels = lax.axis_size("grp").bit_length() - 1
    position = lax.axis_index("grp")
    sketch = leaves
    for height in range(levels):
        sister = partner(sketch, "grp", height)
        upper_side = position // 2**height % 2 == 1
        lower_part = jnp.where(upper_side, sister, sketch)
        upper_part = jnp.where(upper_side, sketch, sister)
        sketch = merge_all(lower_part, upper_part)
    return jax.vmap(precondition)(leaves, sketch)


def dot_nt(a, b):
    return lax.dot_general(a, b, (((1,), (1,)), ((), ())), precision=HI, preferred_element_type=jnp.float32)


def dot_nn(a, b):
    return jnp.dot(a, b, precision=HI, preferred_element_type=jnp.float32)


def start_rows(count, width, span):
    j = lax.broadcasted_iota(jnp.int32, (count, width), 0)
    i = lax.rem(lax.broadcasted_iota(jnp.int32, (count, width), 1), span)
    turn = lax.rem((2 * i + 1) * (2 * j + 1), 8 * span)
    folded = jnp.minimum(turn, 8 * span - turn)
    angle = (2 * span - folded).astype(jnp.float32) * (math.pi / (4 * span))
    square = angle * angle
    series = jnp.full_like(angle, 1.0)
    for n in range(12, 0, -2):
        series = 1.0 - square * series * (1.0 / (n * (n + 1)))
    return angle * series


def spread(gram, problems, count, width):
    lane = lax.broadcasted_iota(jnp.int32, (8, width), 1)
    columns = []
    for j in range(count):
        blocks = {}
        for b in range(j // 8, count // 8):
            parts = [
                jnp.broadcast_to(gram[8 * b : 8 * b + 8, k * count + j : k * count + j + 1], (8, width))
                for k in range(problems)
            ]
            blocks[b] = parts[0] if problems == 1 else jnp.where(lane < width // 2, parts[0], parts[1])
        columns.append(blocks)
    return columns


def eliminate(columns, rhs):
    count = len(columns)
    width = rhs.shape[1]
    parts = [rhs[8 * b : 8 * b + 8] for b in range(count // 8)]
    row = lax.broadcasted_iota(jnp.int32, (8, width), 0)
    diag = [jnp.ones((8, width), jnp.float32) for _ in parts]
    whole = [functools.reduce(lambda x, j: jnp.where(row == j, columns[8 * k + j][k], x), range(8), d) for k, d in enumerate(diag)]
    for p in range(0, count, 2):
        home, at = divmod(p, 8)
        left, right = columns[p], columns[p + 1]
        a = left[home][at : at + 1]
        b = left[home][at + 1 : at + 2]
        c = right[home][at + 1 : at + 2]
        det = a * c - b * b
        ratio = b / a
        diag[home] = jnp.where(row == at, a, jnp.where(row == at + 1, c - b * ratio, diag[home]))
        inverse = 1.0 / det
        ia, ib, ic = c * inverse, b * inverse, a * inverse
        low, high = {}, {}
        for k in left:
            low[k] = left[k] * ia - right[k] * ib
            high[k] = right[k] * ic - left[k] * ib
        for j in range(p + 2, count):
            one = left[j // 8][j % 8 : j % 8 + 1]
            two = right[j // 8][j % 8 : j % 8 + 1]
            columns[j] = {k: block - (low[k] * one + high[k] * two) for k, block in columns[j].items()}
        low[home] = jnp.where(row > at + 1, low[home], jnp.where(row == at + 1, ratio, 0.0))
        high[home] = jnp.where(row > at + 1, high[home], 0.0)
        first, second = parts[home][at : at + 1], parts[home][at + 1 : at + 2]
        for k in low:
            parts[k] = parts[k] - (low[k] * first + high[k] * second)
    worst = functools.reduce(jnp.minimum, [d / w for d, w in zip(diag, whole)])
    return jnp.concatenate([part * lax.rsqrt(d) for part, d in zip(parts, diag)], axis=0), worst


def apart(value):
    lane = lax.broadcasted_iota(jnp.int32, value.shape, 1)
    near = lane < value.shape[1] // 2
    return jnp.concatenate([jnp.where(near, value, 0.0), jnp.where(near, 0.0, value)], axis=0)


def solve_small(gram, rows, often):
    count = gram.shape[0]
    half = count // 2
    r = lax.broadcasted_iota(jnp.int32, gram.shape, 0)
    c = lax.broadcasted_iota(jnp.int32, gram.shape, 1)
    lane = lax.broadcasted_iota(jnp.int32, (1, count), 1)
    diagonal = jnp.sum(jnp.where(r == c, gram, 0.0), axis=0, keepdims=True)
    trace_lower = jnp.sum(jnp.where(lane < half, diagonal, 0.0), axis=1, keepdims=True)
    trace_upper = jnp.sum(jnp.where(lane < half, 0.0, diagonal), axis=1, keepdims=True)
    scale = 1.0 / (trace_lower + trace_upper)
    pair_scale = 1.0 / jnp.where(lane < half, trace_lower, trace_upper)
    own_pair = jnp.where((r < half) == (c < half), gram, 0.0)

    moved = dot_nn(start_rows(rows, count, half), own_pair) * pair_scale
    own_pair = own_pair * pair_scale
    smallest = []
    if not often:
        moved = dot_nn(moved, own_pair)
    for onward_too in (True, True, False, False) if often else (True, False):
        inner = dot_nt(moved, apart(moved))
        onward = dot_nn(moved, own_pair) if onward_too else moved
        moved, worst = eliminate(spread(inner, 2, rows, count), onward)
        smallest.append(jnp.min(worst))
    basis = apart(moved)

    gram = gram * scale
    reached = dot_nn(basis, gram)
    kernel = dot_nt(reached, basis)
    moved = dot_nn(start_rows(rows, half, half), kernel)
    if often:
        for onward_too in (True, True, False):
            inner = dot_nt(moved, moved)
            onward = dot_nn(moved, kernel) if onward_too else moved
            moved, _ = eliminate(spread(inner, 1, rows, half), onward)
    else:
        moved = dot_nn(moved, dot_nn(kernel, kernel))
    inner = dot_nt(moved, moved)
    onward = dot_nn(moved, jnp.concatenate([reached, basis], axis=1))
    both, worst = eliminate(spread(inner, 1, rows, 2 * count), onward)
    smallest.append(jnp.min(worst))
    enough = jnp.logical_and(jnp.logical_and(smallest[0] > 1e-4, smallest[1] > 1e-2), smallest[-1] > 3e-4)

    weights = both[:, count:]
    row = lax.broadcasted_iota(jnp.int32, (8, 2 * count), 0)
    joint = dot_nt(jnp.concatenate([both[:, :count], weights], axis=0), weights)
    energy = spread(joint[:rows], 1, rows, 2 * count)
    metric = spread(joint[rows:], 1, rows, 2 * count)
    total = jnp.zeros((8, 2 * count), jnp.float32)
    for j in range(rows):
        for b in energy[j]:
            unit = jnp.where(row == j % 8, 2.0, 0.0) if b == j // 8 else 0.0
            term = energy[j][b] * (unit - metric[j][b])
            total = total + (term if b == j // 8 else term + term)
    total = jnp.sum(total, axis=0, keepdims=True)
    damping = 0.1 * total / rows + 1e-06 * scale
    columns = [{b: energy[j][b] + damping * metric[j][b] for b in energy[j]} for j in range(rows)]
    solved, _ = eliminate(columns, both)
    return solved[:, :count], solved[:, count:], enough


def combine_kernel(rows, leaf_ref, out_ref, gram_ref, change_ref):
    leaf = leaf_ref[...]
    gram_ref[...] = lax.dot_general(leaf, leaf, (((1,), (1,)), ((), ())), preferred_element_type=jnp.float32)
    own = pl.ds(pl.multiple_of(lax.axis_index("grp") * rows, rows), rows)

    def finish(often):
        projected, weights, enough = solve_small(gram_ref[...], rows, often)
        change_ref[...] = lax.dot_general(
            projected, weights, (((0,), (0,)), ((), ())), precision=HI, preferred_element_type=jnp.float32
        )
        change = change_ref[own, :]
        top = change.astype(jnp.bfloat16)
        rest = (change - top.astype(jnp.float32)).astype(jnp.bfloat16)
        moved = jnp.dot(jnp.concatenate([top, rest], axis=0), leaf_ref[...], preferred_element_type=jnp.float32)
        out_ref[0] = leaf_ref[own, :].astype(jnp.float32) - (moved[:rows] + moved[rows:])
        return enough

    enough = finish(False)

    @pl.when(jnp.logical_not(enough))
    def _():
        finish(True)


def features_kernel(lengths_ref, order_ref, tokens_ref, out_ref, grads_ref, held_ref):
    examples, depth, full = tokens_ref.shape
    modules, groups, pairs, _ = out_ref.shape
    half = full // 2
    chunks = pairs // examples
    position = lax.broadcasted_iota(jnp.int32, (chunks, depth), 1)
    module = lax.rem(position, modules)
    lane = lax.broadcasted_iota(jnp.int32, (depth, full), 1)
    for e in range(examples):
        block = tokens_ref[e].astype(jnp.float32)
        left = jnp.where(lane < half, block, 0.0).astype(jnp.bfloat16)
        right = jnp.where(lane < half, 0.0, pltpu.roll(block, half, 1)).astype(jnp.bfloat16)
        grads = block.T[half:]
        for k in range(depth // full):
            grads_ref[k] = grads[:, k * full : (k + 1) * full]
        live = position < lengths_ref[e] * modules
        flat = jnp.zeros((modules * chunks, full), jnp.float32)
        for odd, side in ((0, left), (1, right)):
            every = pl.ds(odd, chunks, stride=2)
            grads = jnp.concatenate([grads_ref[k, every, :] for k in range(depth // full)], axis=1)
            grads = jnp.where(live, grads, 0.0)
            apiece = [jnp.where(module == q, grads, 0.0).astype(jnp.bfloat16) for q in range(modules)]
            flat = flat + jnp.dot(jnp.concatenate(apiece, axis=0), side, preferred_element_type=jnp.float32)
        held_ref[pl.ds(e, modules * chunks, stride=examples), :] = flat
    for slot in range(modules):
        first = pl.multiple_of(order_ref[slot] * pairs, pairs)
        message = held_ref[pl.ds(first, pairs), :].astype(jnp.bfloat16)
        for g in range(groups):
            out_ref[slot, g] = message


def gram_route(tokens, lengths, module_order):
    groups, owners = lax.axis_size("grp"), lax.axis_size("mod")
    own, slots, modules, full = tokens.shape
    width = (full // 2) ** 2
    rows = owners * own
    count = groups * rows
    chunks = width // full
    messages = pl.pallas_call(
        features_kernel,
        out_shape=jax.ShapeDtypeStruct((modules, groups, chunks * own, full), jnp.bfloat16),
        in_specs=[pl.BlockSpec(memory_space=space) for space in (pltpu.SMEM, pltpu.SMEM, pltpu.VMEM)],
        scratch_shapes=[
            pltpu.VMEM((slots * modules // full, full // 2, full), jnp.float32),
            pltpu.VMEM((modules * chunks * own, full), jnp.float32),
        ],
        compiler_params=pltpu.CompilerParams(vmem_limit_bytes=VMEM_BYTES),
    )(lengths, module_order, tokens.reshape(own, slots * modules, full))
    messages = messages.reshape(groups * modules, chunks, own, full).transpose(0, 2, 1, 3).reshape(groups * modules, own, width)
    leaf = lax.all_to_all(messages, ("mod", "grp"), split_axis=0, concat_axis=0, tiled=True)
    leaf = leaf.reshape(modules, groups, own, width).transpose(1, 0, 2, 3).reshape(count, width)
    return pl.pallas_call(
        functools.partial(combine_kernel, rows),
        out_shape=jax.ShapeDtypeStruct((1, rows, width), jnp.float32),
        scratch_shapes=[pltpu.VMEM((count, count), jnp.float32)] * 2,
        compiler_params=pltpu.CompilerParams(vmem_limit_bytes=VMEM_BYTES),
    )(leaf)


def local_features(token_block, live_counts):
    example_count, token_slots, module_count, full_width = token_block.shape
    half_width = full_width // 2
    live_mask = jnp.arange(token_slots, dtype=jnp.int32)[None, :] < live_counts[:, None]
    grad_side = jnp.where(
        live_mask[:, :, None, None],
        token_block[:, :, :, half_width:],
        jnp.zeros((), token_block.dtype),
    )
    input_side = token_block[:, :, :, :half_width]
    outer = jnp.einsum("etmo,etmi->meoi", grad_side, input_side, preferred_element_type=jnp.float32)
    return outer.reshape(module_count, example_count, half_width * half_width).astype(jnp.bfloat16)


def per_device(tokens, lengths, module_order):
    groups, owners = lax.axis_size("grp"), lax.axis_size("mod")
    own, slots, modules, full = tokens.shape
    if groups == 4 and owners * own == 16 and owners == modules == 8 and full == 128:
        return gram_route(tokens, lengths, module_order)
    return sketch_tree(local_features(tokens, lengths), module_order)


def solution(mesh):
    return jax.shard_map(
        per_device,
        mesh=mesh,
        in_specs=(P(("grp", "mod"), None, None, None), P(("grp", "mod")), P()),
        out_specs=P("mod", "grp", None),
        check_vma=False,
    )
```

```python
import functools
import math

import jax
import jax.numpy as jnp
import numpy as np
from jax import lax
from jax.experimental import pallas as pl
from jax.experimental.pallas import tpu as pltpu
from jax.sharding import PartitionSpec as P

ITERS = 3
HI = lax.Precision.HIGHEST
VMEM_BYTES = 48 * 1024 * 1024


def partner(value, axis, bit):
    mask = 2**bit
    return xor_send(value, axis, mask)


def xor_send(value, axis, mask):
    pairs = [(source, source ^ mask) for source in range(lax.axis_size(axis))]
    return lax.ppermute(value, axis, pairs)


def start_basis(row_count, col_count):
    row_index = np.arange(row_count, dtype=np.float64)[:, None] + 0.5
    col_index = np.arange(col_count, dtype=np.float64)[None, :] + 0.5
    return np.cos(np.pi * row_index * col_index / row_count).astype(np.float32)


def orthonormal(matrix):
    for repeat in range(2):
        cross_gram = jnp.dot(matrix.T, matrix, precision=HI)
        factor = jnp.linalg.cholesky(cross_gram)
        matrix = jax.scipy.linalg.solve_triangular(factor, matrix.T, lower=True).T
    return matrix


def merge_pair(lower_sketch, upper_sketch):
    stacked = jnp.concatenate([lower_sketch, upper_sketch], axis=0)
    kernel = jnp.dot(stacked, stacked.T, precision=HI)
    current = start_basis(stacked.shape[0], lower_sketch.shape[0])
    for repeat in range(ITERS):
        current = orthonormal(jnp.dot(kernel, current, precision=HI))
    return jnp.dot(current.T, stacked, precision=HI)


def precondition(group_rows, sketch):
    sketch_rows = sketch.shape[0]
    damping = 0.1 * jnp.sum(sketch * sketch) / sketch_rows + 1e-06
    capacitance = jnp.dot(sketch, sketch.T, precision=HI) + damping * jnp.eye(sketch_rows, dtype=jnp.float32)
    projected = jnp.dot(group_rows, sketch.T, precision=HI)
    factor = jnp.linalg.cholesky(capacitance)
    middle = jax.scipy.linalg.solve_triangular(factor, projected.T, lower=True)
    weights = jax.scipy.linalg.solve_triangular(factor, middle, lower=True, trans=1).T
    return group_rows - jnp.dot(weights, sketch, precision=HI)


def sketch_tree(features, module_order):
    ordered = jnp.take(features, module_order, axis=0)
    group_rows = lax.all_to_all(ordered, "mod", split_axis=0, concat_axis=1, tiled=True)
    leaves = group_rows.astype(jnp.float32)
    merge_all = jax.vmap(merge_pair)
    levels = lax.axis_size("grp").bit_length() - 1
    position = lax.axis_index("grp")
    sketch = leaves
    for height in range(levels):
        sister = partner(sketch, "grp", height)
        upper_side = position // 2**height % 2 == 1
        lower_part = jnp.where(upper_side, sister, sketch)
        upper_part = jnp.where(upper_side, sketch, sister)
        sketch = merge_all(lower_part, upper_part)
    return jax.vmap(precondition)(leaves, sketch)


def dot_nt(a, b):
    return lax.dot_general(a, b, (((1,), (1,)), ((), ())), precision=HI, preferred_element_type=jnp.float32)


def dot_nn(a, b):
    return jnp.dot(a, b, precision=HI, preferred_element_type=jnp.float32)


def start_rows(count, index, span):
    j = lax.broadcasted_iota(jnp.int32, (count, index.shape[1]), 0)
    turn = lax.rem((2 * index + 1) * (2 * j + 1), 8 * span)
    folded = jnp.minimum(turn, 8 * span - turn)
    angle = (2 * span - folded).astype(jnp.float32) * (math.pi / (4 * span))
    square = angle * angle
    series = jnp.full_like(angle, 1.0)
    for n in range(12, 0, -2):
        series = 1.0 - square * series * (1.0 / (n * (n + 1)))
    return angle * series


def spread(gram, count, width, near=None):
    problems = 1 if near is None else 2
    columns = []
    for j in range(count):
        blocks = {}
        for b in range(j // 8, count // 8):
            parts = [
                jnp.broadcast_to(gram[8 * b : 8 * b + 8, k * count + j : k * count + j + 1], (8, width))
                for k in range(problems)
            ]
            blocks[b] = parts[0] if near is None else jnp.where(near, parts[0], parts[1])
        columns.append(blocks)
    return columns


def eliminate(columns, rhs):
    count = len(columns)
    width = rhs.shape[1]
    parts = [rhs[8 * b : 8 * b + 8] for b in range(count // 8)]
    row = lax.broadcasted_iota(jnp.int32, (8, width), 0)
    diag = [jnp.ones((8, width), jnp.float32) for _ in parts]
    whole = [functools.reduce(lambda x, j: jnp.where(row == j, columns[8 * k + j][k], x), range(8), d) for k, d in enumerate(diag)]
    for p in range(0, count, 2):
        home, at = divmod(p, 8)
        left, right = columns[p], columns[p + 1]
        a = left[home][at : at + 1]
        b = left[home][at + 1 : at + 2]
        c = right[home][at + 1 : at + 2]
        det = a * c - b * b
        ratio = b / a
        diag[home] = jnp.where(row == at, a, jnp.where(row == at + 1, c - b * ratio, diag[home]))
        inverse = 1.0 / det
        ia, ib, ic = c * inverse, b * inverse, a * inverse
        low, high = {}, {}
        for k in left:
            low[k] = left[k] * ia - right[k] * ib
            high[k] = right[k] * ic - left[k] * ib
        for j in range(p + 2, count):
            one = left[j // 8][j % 8 : j % 8 + 1]
            two = right[j // 8][j % 8 : j % 8 + 1]
            columns[j] = {k: block - (low[k] * one + high[k] * two) for k, block in columns[j].items()}
        low[home] = jnp.where(row > at + 1, low[home], jnp.where(row == at + 1, ratio, 0.0))
        high[home] = jnp.where(row > at + 1, high[home], 0.0)
        first, second = parts[home][at : at + 1], parts[home][at + 1 : at + 2]
        for k in low:
            parts[k] = parts[k] - (low[k] * first + high[k] * second)
    worst = functools.reduce(jnp.minimum, [d / w for d, w in zip(diag, whole)])
    return jnp.concatenate([part * lax.rsqrt(d) for part, d in zip(parts, diag)], axis=0), worst


def apart(value, near):
    return jnp.concatenate([jnp.where(near, value, 0.0), jnp.where(near, 0.0, value)], axis=0)


def place(position, groups, own, rows):
    group = lax.rem(lax.div(position, own), groups)
    example = lax.div(position, own * groups) * own + lax.rem(position, own)
    return group < groups // 2, lax.rem(group, groups // 2) * rows + example


def solve_small(gram, rows, groups, own, often):
    count = gram.shape[0]
    half = count // 2
    r = lax.broadcasted_iota(jnp.int32, gram.shape, 0)
    c = lax.broadcasted_iota(jnp.int32, gram.shape, 1)
    near_row, _ = place(r, groups, own, rows)
    near_col, index = place(c, groups, own, rows)
    near, index = near_col[:rows], index[:rows]
    diagonal = jnp.sum(jnp.where(r == c, gram, 0.0), axis=0, keepdims=True)
    trace_lower = jnp.sum(jnp.where(near[:1], diagonal, 0.0), axis=1, keepdims=True)
    trace_upper = jnp.sum(jnp.where(near[:1], 0.0, diagonal), axis=1, keepdims=True)
    scale = 1.0 / (trace_lower + trace_upper)
    pair_scale = 1.0 / jnp.where(near[:1], trace_lower, trace_upper)
    own_pair = jnp.where(jnp.logical_xor(near_row, near_col), 0.0, gram)

    moved = dot_nn(start_rows(rows, index, half), own_pair) * pair_scale
    own_pair = own_pair * pair_scale
    smallest = []
    if not often:
        moved = dot_nn(moved, own_pair)
    for onward_too in (True, True, False, False) if often else (True, False):
        inner = dot_nt(moved, apart(moved, near))
        onward = dot_nn(moved, own_pair) if onward_too else moved
        moved, worst = eliminate(spread(inner, rows, count, near[:8]), onward)
        smallest.append(jnp.min(worst))
    basis = apart(moved, near)

    gram = gram * scale
    reached = dot_nn(basis, gram)
    kernel = dot_nt(reached, basis)
    moved = dot_nn(start_rows(rows, c[:rows, :half], half), kernel)
    if often:
        for onward_too in (True, True, False):
            inner = dot_nt(moved, moved)
            onward = dot_nn(moved, kernel) if onward_too else moved
            moved, _ = eliminate(spread(inner, rows, half), onward)
    else:
        moved = dot_nn(moved, dot_nn(kernel, kernel))
    inner = dot_nt(moved, moved)
    onward = dot_nn(moved, jnp.concatenate([reached, basis], axis=1))
    both, worst = eliminate(spread(inner, rows, 2 * count), onward)
    smallest.append(jnp.min(worst))
    enough = jnp.logical_and(jnp.logical_and(smallest[0] > 1e-4, smallest[1] > 1e-2), smallest[-1] > 3e-4)

    weights = both[:, count:]
    row = lax.broadcasted_iota(jnp.int32, (8, 2 * count), 0)
    joint = dot_nt(jnp.concatenate([both[:, :count], weights], axis=0), weights)
    energy = spread(joint[:rows], rows, 2 * count)
    metric = spread(joint[rows:], rows, 2 * count)
    total = jnp.zeros((8, 2 * count), jnp.float32)
    for j in range(rows):
        for b in energy[j]:
            unit = jnp.where(row == j % 8, 2.0, 0.0) if b == j // 8 else 0.0
            term = energy[j][b] * (unit - metric[j][b])
            total = total + (term if b == j // 8 else term + term)
    total = jnp.sum(total, axis=0, keepdims=True)
    damping = 0.1 * total / rows + 1e-06 * scale
    columns = [{b: energy[j][b] + damping * metric[j][b] for b in energy[j]} for j in range(rows)]
    solved, _ = eliminate(columns, both)
    return solved[:, :count], solved[:, count:], enough


def combine_kernel(rows, groups, own, leaf_ref, out_ref, gram_ref, change_ref, mine_ref):
    leaf = leaf_ref[...]
    count = leaf.shape[0]
    gram_ref[...] = lax.dot_general(leaf, leaf, (((1,), (1,)), ((), ())), preferred_element_type=jnp.float32)
    group = lax.axis_index("grp")
    row = lax.broadcasted_iota(jnp.int32, (rows, count), 0)
    lane = lax.broadcasted_iota(jnp.int32, (rows, count), 1)
    chosen = lane == lax.div(row, own) * (own * groups) + group * own + lax.rem(row, own)

    def finish(often):
        projected, weights, enough = solve_small(gram_ref[...], rows, groups, own, often)
        change_ref[:, :count] = lax.dot_general(
            projected, weights, (((0,), (0,)), ((), ())), precision=HI, preferred_element_type=jnp.float32
        )
        owners = rows // own
        for e in range(own):
            mine_ref[pl.ds(e, owners, stride=own), :] = change_ref[pl.ds(group * own + e, owners, stride=own * groups), :]
        kept = jnp.where(chosen, 1.0, 0.0) - mine_ref[:, :count]
        top = kept.astype(jnp.bfloat16)
        rest = (kept - top.astype(jnp.float32)).astype(jnp.bfloat16)
        moved = jnp.dot(jnp.concatenate([top, rest], axis=0), leaf_ref[...], preferred_element_type=jnp.float32)
        out_ref[0] = moved[:rows] + moved[rows:]
        return enough

    enough = finish(False)

    @pl.when(jnp.logical_not(enough))
    def _():
        finish(True)


def features_kernel(lengths_ref, order_ref, tokens_ref, out_ref, grads_ref, held_ref):
    examples, depth, full = tokens_ref.shape
    modules, groups, pairs, _ = out_ref.shape
    half = full // 2
    chunks = pairs // examples
    position = lax.broadcasted_iota(jnp.int32, (chunks, depth), 1)
    module = lax.rem(position, modules)
    lane = lax.broadcasted_iota(jnp.int32, (depth, full), 1)
    for e in range(examples):
        block = tokens_ref[e].astype(jnp.float32)
        left = jnp.where(lane < half, block, 0.0).astype(jnp.bfloat16)
        right = jnp.where(lane < half, 0.0, pltpu.roll(block, half, 1)).astype(jnp.bfloat16)
        grads = block.T[half:]
        for k in range(depth // full):
            grads_ref[k] = grads[:, k * full : (k + 1) * full]
        live = position < lengths_ref[e] * modules
        flat = jnp.zeros((modules * chunks, full), jnp.float32)
        for odd, side in ((0, left), (1, right)):
            every = pl.ds(odd, chunks, stride=2)
            grads = jnp.concatenate([grads_ref[k, every, :] for k in range(depth // full)], axis=1)
            grads = jnp.where(live, grads, 0.0)
            apiece = [jnp.where(module == q, grads, 0.0).astype(jnp.bfloat16) for q in range(modules)]
            flat = flat + jnp.dot(jnp.concatenate(apiece, axis=0), side, preferred_element_type=jnp.float32)
        held_ref[pl.ds(e, modules * chunks, stride=examples), :] = flat
    for slot in range(modules):
        first = pl.multiple_of(order_ref[slot] * pairs, pairs)
        message = held_ref[pl.ds(first, pairs), :].astype(jnp.bfloat16)
        for g in range(groups):
            out_ref[slot, g] = message


def gram_route(tokens, lengths, module_order):
    groups, owners = lax.axis_size("grp"), lax.axis_size("mod")
    own, slots, modules, full = tokens.shape
    width = (full // 2) ** 2
    rows = owners * own
    count = groups * rows
    chunks = width // full
    messages = pl.pallas_call(
        features_kernel,
        out_shape=jax.ShapeDtypeStruct((modules, groups, chunks * own, full), jnp.bfloat16),
        in_specs=[pl.BlockSpec(memory_space=space) for space in (pltpu.SMEM, pltpu.SMEM, pltpu.VMEM)],
        scratch_shapes=[
            pltpu.VMEM((slots * modules // full, full // 2, full), jnp.float32),
            pltpu.VMEM((modules * chunks * own, full), jnp.float32),
        ],
        compiler_params=pltpu.CompilerParams(vmem_limit_bytes=VMEM_BYTES),
    )(lengths, module_order, tokens.reshape(own, slots * modules, full))
    messages = messages.reshape(groups * modules, chunks, own, full).transpose(0, 2, 1, 3).reshape(groups * modules, own, width)
    leaf = lax.all_to_all(messages, ("mod", "grp"), split_axis=0, concat_axis=0, tiled=True)
    leaf = leaf.reshape(count, width)
    return pl.pallas_call(
        functools.partial(combine_kernel, rows, groups, own),
        out_shape=jax.ShapeDtypeStruct((1, rows, width), jnp.float32),
        scratch_shapes=[pltpu.VMEM(shape, jnp.float32) for shape in ((count, count), (count, full), (rows, full))],
        compiler_params=pltpu.CompilerParams(vmem_limit_bytes=VMEM_BYTES),
    )(leaf)


def local_features(token_block, live_counts):
    example_count, token_slots, module_count, full_width = token_block.shape
    half_width = full_width // 2
    live_mask = jnp.arange(token_slots, dtype=jnp.int32)[None, :] < live_counts[:, None]
    grad_side = jnp.where(
        live_mask[:, :, None, None],
        token_block[:, :, :, half_width:],
        jnp.zeros((), token_block.dtype),
    )
    input_side = token_block[:, :, :, :half_width]
    outer = jnp.einsum("etmo,etmi->meoi", grad_side, input_side, preferred_element_type=jnp.float32)
    return outer.reshape(module_count, example_count, half_width * half_width).astype(jnp.bfloat16)


def per_device(tokens, lengths, module_order):
    groups, owners = lax.axis_size("grp"), lax.axis_size("mod")
    own, slots, modules, full = tokens.shape
    if groups == 4 and owners * own == 16 and owners == modules == 8 and full == 128:
        return gram_route(tokens, lengths, module_order)
    return sketch_tree(local_features(tokens, lengths), module_order)


def solution(mesh):
    return jax.shard_map(
        per_device,
        mesh=mesh,
        in_specs=(P(("grp", "mod"), None, None, None), P(("grp", "mod")), P()),
        out_specs=P("mod", "grp", None),
        check_vma=False,
    )
```

```python
import functools
import math

import jax
import jax.numpy as jnp
import numpy as np
from jax import lax
from jax.experimental import pallas as pl
from jax.experimental.pallas import tpu as pltpu
from jax.sharding import PartitionSpec as P

ITERS = 3
HI = lax.Precision.HIGHEST
VMEM_BYTES = 48 * 1024 * 1024


def partner(value, axis, bit):
    mask = 2**bit
    return xor_send(value, axis, mask)


def xor_send(value, axis, mask):
    pairs = [(source, source ^ mask) for source in range(lax.axis_size(axis))]
    return lax.ppermute(value, axis, pairs)


def start_basis(row_count, col_count):
    row_index = np.arange(row_count, dtype=np.float64)[:, None] + 0.5
    col_index = np.arange(col_count, dtype=np.float64)[None, :] + 0.5
    return np.cos(np.pi * row_index * col_index / row_count).astype(np.float32)


def orthonormal(matrix):
    for repeat in range(2):
        cross_gram = jnp.dot(matrix.T, matrix, precision=HI)
        factor = jnp.linalg.cholesky(cross_gram)
        matrix = jax.scipy.linalg.solve_triangular(factor, matrix.T, lower=True).T
    return matrix


def merge_pair(lower_sketch, upper_sketch):
    stacked = jnp.concatenate([lower_sketch, upper_sketch], axis=0)
    kernel = jnp.dot(stacked, stacked.T, precision=HI)
    current = start_basis(stacked.shape[0], lower_sketch.shape[0])
    for repeat in range(ITERS):
        current = orthonormal(jnp.dot(kernel, current, precision=HI))
    return jnp.dot(current.T, stacked, precision=HI)


def precondition(group_rows, sketch):
    sketch_rows = sketch.shape[0]
    damping = 0.1 * jnp.sum(sketch * sketch) / sketch_rows + 1e-06
    capacitance = jnp.dot(sketch, sketch.T, precision=HI) + damping * jnp.eye(sketch_rows, dtype=jnp.float32)
    projected = jnp.dot(group_rows, sketch.T, precision=HI)
    factor = jnp.linalg.cholesky(capacitance)
    middle = jax.scipy.linalg.solve_triangular(factor, projected.T, lower=True)
    weights = jax.scipy.linalg.solve_triangular(factor, middle, lower=True, trans=1).T
    return group_rows - jnp.dot(weights, sketch, precision=HI)


def sketch_tree(features, module_order):
    ordered = jnp.take(features, module_order, axis=0)
    group_rows = lax.all_to_all(ordered, "mod", split_axis=0, concat_axis=1, tiled=True)
    leaves = group_rows.astype(jnp.float32)
    merge_all = jax.vmap(merge_pair)
    levels = lax.axis_size("grp").bit_length() - 1
    position = lax.axis_index("grp")
    sketch = leaves
    for height in range(levels):
        sister = partner(sketch, "grp", height)
        upper_side = position // 2**height % 2 == 1
        lower_part = jnp.where(upper_side, sister, sketch)
        upper_part = jnp.where(upper_side, sketch, sister)
        sketch = merge_all(lower_part, upper_part)
    return jax.vmap(precondition)(leaves, sketch)


def dot_nt(a, b):
    return lax.dot_general(a, b, (((1,), (1,)), ((), ())), precision=HI, preferred_element_type=jnp.float32)


def dot_nn(a, b):
    return jnp.dot(a, b, precision=HI, preferred_element_type=jnp.float32)


def start_rows(count, index, span):
    j = lax.broadcasted_iota(jnp.int32, (count, index.shape[1]), 0)
    turn = lax.rem((2 * index + 1) * (2 * j + 1), 8 * span)
    folded = jnp.minimum(turn, 8 * span - turn)
    angle = (2 * span - folded).astype(jnp.float32) * (math.pi / (4 * span))
    square = angle * angle
    series = jnp.full_like(angle, 1.0)
    for n in range(12, 0, -2):
        series = 1.0 - square * series * (1.0 / (n * (n + 1)))
    return angle * series


def spread(gram, count, width, near=None):
    problems = 1 if near is None else 2
    columns = []
    for j in range(count):
        blocks = {}
        for b in range(j // 8, count // 8):
            parts = [
                jnp.broadcast_to(gram[8 * b : 8 * b + 8, k * count + j : k * count + j + 1], (8, width))
                for k in range(problems)
            ]
            blocks[b] = parts[0] if near is None else jnp.where(near, parts[0], parts[1])
        columns.append(blocks)
    return columns


def eliminate(columns, rhs):
    count = len(columns)
    width = rhs.shape[1]
    parts = [rhs[8 * b : 8 * b + 8] for b in range(count // 8)]
    row = lax.broadcasted_iota(jnp.int32, (8, width), 0)
    diag = [jnp.ones((8, width), jnp.float32) for _ in parts]
    whole = [functools.reduce(lambda x, j: jnp.where(row == j, columns[8 * k + j][k], x), range(8), d) for k, d in enumerate(diag)]
    for p in range(0, count, 2):
        home, at = divmod(p, 8)
        left, right = columns[p], columns[p + 1]
        a = left[home][at : at + 1]
        b = left[home][at + 1 : at + 2]
        c = right[home][at + 1 : at + 2]
        det = a * c - b * b
        ratio = b / a
        diag[home] = jnp.where(row == at, a, jnp.where(row == at + 1, c - b * ratio, diag[home]))
        inverse = 1.0 / det
        ia, ib, ic = c * inverse, b * inverse, a * inverse
        low, high = {}, {}
        for k in left:
            low[k] = left[k] * ia - right[k] * ib
            high[k] = right[k] * ic - left[k] * ib
        for j in range(p + 2, count):
            one = left[j // 8][j % 8 : j % 8 + 1]
            two = right[j // 8][j % 8 : j % 8 + 1]
            columns[j] = {k: block - (low[k] * one + high[k] * two) for k, block in columns[j].items()}
        low[home] = jnp.where(row > at + 1, low[home], jnp.where(row == at + 1, ratio, 0.0))
        high[home] = jnp.where(row > at + 1, high[home], 0.0)
        first, second = parts[home][at : at + 1], parts[home][at + 1 : at + 2]
        for k in low:
            parts[k] = parts[k] - (low[k] * first + high[k] * second)
    worst = functools.reduce(jnp.minimum, [d / w for d, w in zip(diag, whole)])
    return jnp.concatenate([part * lax.rsqrt(d) for part, d in zip(parts, diag)], axis=0), worst


def apart(value, near):
    return jnp.concatenate([jnp.where(near, value, 0.0), jnp.where(near, 0.0, value)], axis=0)


def place(position, groups, own, rows):
    group = lax.rem(lax.div(position, own), groups)
    example = lax.div(position, own * groups) * own + lax.rem(position, own)
    return group < groups // 2, lax.rem(group, groups // 2) * rows + example


def solve_small(gram, rows, groups, own, often):
    count = gram.shape[0]
    half = count // 2
    r = lax.broadcasted_iota(jnp.int32, gram.shape, 0)
    c = lax.broadcasted_iota(jnp.int32, gram.shape, 1)
    near_row, _ = place(r, groups, own, rows)
    near_col, index = place(c, groups, own, rows)
    near, index = near_col[:rows], index[:rows]
    diagonal = jnp.sum(jnp.where(r == c, gram, 0.0), axis=0, keepdims=True)
    trace_lower = jnp.sum(jnp.where(near[:1], diagonal, 0.0), axis=1, keepdims=True)
    trace_upper = jnp.sum(jnp.where(near[:1], 0.0, diagonal), axis=1, keepdims=True)
    scale = 1.0 / (trace_lower + trace_upper)
    pair_scale = 1.0 / jnp.where(near[:1], trace_lower, trace_upper)
    own_pair = jnp.where(jnp.logical_xor(near_row, near_col), 0.0, gram)

    moved = dot_nn(start_rows(rows, index, half), own_pair) * pair_scale
    own_pair = own_pair * pair_scale
    smallest = []
    if not often:
        moved = dot_nn(moved, own_pair)
    for onward_too in (True, True, False, False) if often else (True, False):
        inner = dot_nt(moved, apart(moved, near))
        onward = dot_nn(moved, own_pair) if onward_too else moved
        moved, worst = eliminate(spread(inner, rows, count, near[:8]), onward)
        smallest.append(jnp.min(worst))
    basis = apart(moved, near)

    gram = gram * scale
    reached = dot_nn(basis, gram)
    kernel = dot_nt(reached, basis)
    moved = dot_nn(start_rows(rows, c[:rows, :half], half), kernel)
    if often:
        for onward_too in (True, True, False):
            inner = dot_nt(moved, moved)
            onward = dot_nn(moved, kernel) if onward_too else moved
            moved, _ = eliminate(spread(inner, rows, half), onward)
    else:
        moved = dot_nn(moved, dot_nn(kernel, kernel))
    inner = dot_nt(moved, moved)
    onward = dot_nn(moved, jnp.concatenate([reached, basis], axis=1))
    both, worst = eliminate(spread(inner, rows, 2 * count), onward)
    smallest.append(jnp.min(worst))
    enough = jnp.logical_and(jnp.logical_and(smallest[0] > 1e-4, smallest[1] > 1e-2), smallest[-1] > 3e-4)

    weights = both[:, count:]
    joint = dot_nt(jnp.concatenate([both[:, :count], weights], axis=0), weights)
    energy, metric = joint[:rows], joint[rows:]
    twice = jnp.where(r[:rows, :rows] == c[:rows, :rows], 2.0, 0.0)
    total = jnp.sum(jnp.sum(energy * (twice - metric), axis=0, keepdims=True), axis=1, keepdims=True)
    damping = 0.1 * total / rows + 1e-06 * scale
    columns = spread(energy + damping * metric, rows, 2 * count)
    solved, _ = eliminate(columns, both)
    return solved[:, :count], solved[:, count:], enough


def combine_kernel(rows, groups, own, leaf_ref, out_ref, gram_ref, change_ref, mine_ref):
    leaf = leaf_ref[...]
    count = leaf.shape[0]
    gram_ref[...] = lax.dot_general(leaf, leaf, (((1,), (1,)), ((), ())), preferred_element_type=jnp.float32)
    group = lax.axis_index("grp")
    row = lax.broadcasted_iota(jnp.int32, (rows, count), 0)
    lane = lax.broadcasted_iota(jnp.int32, (rows, count), 1)
    chosen = lane == lax.div(row, own) * (own * groups) + group * own + lax.rem(row, own)

    def finish(often):
        projected, weights, enough = solve_small(gram_ref[...], rows, groups, own, often)
        change_ref[:, :count] = lax.dot_general(
            projected, weights, (((0,), (0,)), ((), ())), precision=HI, preferred_element_type=jnp.float32
        )
        owners = rows // own
        for e in range(own):
            mine_ref[pl.ds(e, owners, stride=own), :] = change_ref[pl.ds(group * own + e, owners, stride=own * groups), :]
        kept = jnp.where(chosen, 1.0, 0.0) - mine_ref[:, :count]
        top = kept.astype(jnp.bfloat16)
        rest = (kept - top.astype(jnp.float32)).astype(jnp.bfloat16)
        moved = jnp.dot(jnp.concatenate([top, rest], axis=0), leaf_ref[...], preferred_element_type=jnp.float32)
        out_ref[0] = moved[:rows] + moved[rows:]
        return enough

    enough = finish(False)

    @pl.when(jnp.logical_not(enough))
    def _():
        finish(True)


def features_kernel(lengths_ref, order_ref, tokens_ref, out_ref, grads_ref, held_ref):
    examples, depth, full = tokens_ref.shape
    modules, groups, pairs, _ = out_ref.shape
    half = full // 2
    chunks = pairs // examples
    position = lax.broadcasted_iota(jnp.int32, (chunks, depth), 1)
    module = lax.rem(position, modules)
    lane = lax.broadcasted_iota(jnp.int32, (depth, full), 1)
    for e in range(examples):
        block = tokens_ref[e].astype(jnp.float32)
        left = jnp.where(lane < half, block, 0.0).astype(jnp.bfloat16)
        right = jnp.where(lane < half, 0.0, pltpu.roll(block, half, 1)).astype(jnp.bfloat16)
        grads = block.T[half:]
        for k in range(depth // full):
            grads_ref[k] = grads[:, k * full : (k + 1) * full]
        live = position < lengths_ref[e] * modules
        flat = jnp.zeros((modules * chunks, full), jnp.float32)
        for odd, side in ((0, left), (1, right)):
            every = pl.ds(odd, chunks, stride=2)
            grads = jnp.concatenate([grads_ref[k, every, :] for k in range(depth // full)], axis=1)
            grads = jnp.where(live, grads, 0.0)
            apiece = [jnp.where(module == q, grads, 0.0).astype(jnp.bfloat16) for q in range(modules)]
            flat = flat + jnp.dot(jnp.concatenate(apiece, axis=0), side, preferred_element_type=jnp.float32)
        held_ref[pl.ds(e, modules * chunks, stride=examples), :] = flat
    for slot in range(modules):
        first = pl.multiple_of(order_ref[slot] * pairs, pairs)
        message = held_ref[pl.ds(first, pairs), :].astype(jnp.bfloat16)
        for g in range(groups):
            out_ref[slot, g] = message


def gram_route(tokens, lengths, module_order):
    groups, owners = lax.axis_size("grp"), lax.axis_size("mod")
    own, slots, modules, full = tokens.shape
    width = (full // 2) ** 2
    rows = owners * own
    count = groups * rows
    chunks = width // full
    messages = pl.pallas_call(
        features_kernel,
        out_shape=jax.ShapeDtypeStruct((modules, groups, chunks * own, full), jnp.bfloat16),
        in_specs=[pl.BlockSpec(memory_space=space) for space in (pltpu.SMEM, pltpu.SMEM, pltpu.VMEM)],
        scratch_shapes=[
            pltpu.VMEM((slots * modules // full, full // 2, full), jnp.float32),
            pltpu.VMEM((modules * chunks * own, full), jnp.float32),
        ],
        compiler_params=pltpu.CompilerParams(vmem_limit_bytes=VMEM_BYTES),
    )(lengths, module_order, tokens.reshape(own, slots * modules, full))
    messages = messages.reshape(groups * modules, chunks, own, full).transpose(0, 2, 1, 3).reshape(groups * modules, own, width)
    leaf = lax.all_to_all(messages, ("mod", "grp"), split_axis=0, concat_axis=0, tiled=True)
    leaf = leaf.reshape(count, width)
    return pl.pallas_call(
        functools.partial(combine_kernel, rows, groups, own),
        out_shape=jax.ShapeDtypeStruct((1, rows, width), jnp.float32),
        scratch_shapes=[pltpu.VMEM(shape, jnp.float32) for shape in ((count, count), (count, full), (rows, full))],
        compiler_params=pltpu.CompilerParams(vmem_limit_bytes=VMEM_BYTES),
    )(leaf)


def local_features(token_block, live_counts):
    example_count, token_slots, module_count, full_width = token_block.shape
    half_width = full_width // 2
    live_mask = jnp.arange(token_slots, dtype=jnp.int32)[None, :] < live_counts[:, None]
    grad_side = jnp.where(
        live_mask[:, :, None, None],
        token_block[:, :, :, half_width:],
        jnp.zeros((), token_block.dtype),
    )
    input_side = token_block[:, :, :, :half_width]
    outer = jnp.einsum("etmo,etmi->meoi", grad_side, input_side, preferred_element_type=jnp.float32)
    return outer.reshape(module_count, example_count, half_width * half_width).astype(jnp.bfloat16)


def per_device(tokens, lengths, module_order):
    groups, owners = lax.axis_size("grp"), lax.axis_size("mod")
    own, slots, modules, full = tokens.shape
    if groups == 4 and owners * own == 16 and owners == modules == 8 and full == 128:
        return gram_route(tokens, lengths, module_order)
    return sketch_tree(local_features(tokens, lengths), module_order)


def solution(mesh):
    return jax.shard_map(
        per_device,
        mesh=mesh,
        in_specs=(P(("grp", "mod"), None, None, None), P(("grp", "mod")), P()),
        out_specs=P("mod", "grp", None),
        check_vma=False,
    )
```
